512 devices in a mesh: gx: 16 (over z_hi, y), gy: 4 (over z_lo), gz: 8 (over x, core).
Axes of the slice: x: 4, y: 4, z: 16 (z_hi: 4, z_lo: 4; z = z_hi * 4 + z_lo), core: 2. Of those that a mesh axis runs over, the one named last changes fastest.
Arguments:
- initial_state: float32 [64, 32, 1024], P('gx', 'gy', 'gz'), may hold values from -6 to 6
- conductivity: float32 [64, 32, 1024], P('gx', 'gy', 'gz'), may hold values from 0.3 to 3
- reaction: float32 [64, 32, 1024], P('gx', 'gy', 'gz'), may hold values from 0.02 to 0.2
- source: float32 [64, 32, 1024], P('gx', 'gy', 'gz'), may hold values from -12 to 12, as said below
Outputs:
- solution: float32 [64, 32, 1024], P('gx', 'gy', 'gz')
- final_residual: float32 [64, 32, 1024], P('gx', 'gy', 'gz')
The draws below stay inside these ranges and needn't reach their ends.
Inputs may be any that keep to these rules, and one draw needn't show every extreme that they name: Real-valued source of order one.
All inputs are finite; a program needn't handle non-finite values.
Results may differ from the reference program's by a relative error of at most 0.0003.
Values sent between devices are 32-bit elements; how exact they have to be, the bound alone decides.
A program may use at most 64 MiB of HBM per device.

```python
import math
import jax
import jax.numpy as jnp

NEWTON = 2
KRYLOV = 3
SWEEPS_F = 2
SWEEPS_C = 2
NX = 64
NY = 32
NZ = 1024


def draw_source(key, part):
    key = jax.random.fold_in(key, 7)
    first_pos = jnp.arange(NX, dtype=jnp.float32).reshape(NX, 1, 1)
    rising = 1.0 + 2.0 * first_pos / (NX - 1)
    return jnp.clip(jax.random.normal(key, (NX, NY, NZ), jnp.float32), -4.0, 4.0) * rising


def block_scale(own_key, dims, pieces, smallest, largest):
    def one(position, shards_of):
        heights = jax.random.uniform(jax.random.fold_in(jax.random.fold_in(own_key, 6), position), (shards_of,), jnp.float32, smallest / len(pieces), largest / len(pieces))
        return jnp.repeat(jnp.exp(heights), dims[position] // shards_of).reshape((-1,) + (1,) * (len(dims) - position - 1))

    loudness = one(*pieces[0])
    for cut in pieces[1:]:
        loudness = loudness * one(*cut)
    return loudness


def bell_draw(key, extent, scale, limit, pieces=(), held_as=jnp.bfloat16):
    entries = jax.random.normal(key, extent, jnp.float32) * scale
    if len(pieces) > 0:
        entries = block_scale(key, extent, pieces, -0.22, 0.18) * entries
    return jnp.clip(entries, min=-limit, max=limit).astype(held_as)


def setup_inputs(seed: int = 0) -> dict:
    seeds = jax.random.split(jax.random.key(seed), 5)
    initial_state = bell_draw(seeds[0], (NX, NY, NZ), 1.0, 6.0, ((0, 16), (1, 4), (2, 8)), jnp.float32)
    conductivity = jnp.clip(jnp.exp(math.log(3.0) - 2.3025851 * jax.random.uniform(seeds[1], (NX, NY, NZ), jnp.float32) ** block_scale(seeds[1], (NX, NY, NZ), ((0, 16), (1, 4), (2, 8)), -0.2, 0.2)), 0.3, 3.0)
    reaction = jnp.clip(jnp.exp(math.log(0.2) - 2.3025851 * jax.random.uniform(seeds[2], (NX, NY, NZ), jnp.float32) ** block_scale(seeds[2], (NX, NY, NZ), ((0, 16), (1, 4), (2, 8)), -0.2, 0.2)), 0.02, 0.2)
    source = draw_source(jax.random.fold_in(seeds[4], 71), 0)
    return {"initial_state": initial_state, "conductivity": conductivity, "reaction": reaction, "source": source}


EPS_SQUARE = 0.25

def face_set(lower_u, lower_k, upper_u, upper_k):
    mean_k = 2.0 * lower_k * upper_k / (lower_k + upper_k)
    difference = upper_u - lower_u
    root_term = jnp.sqrt(EPS_SQUARE + difference * difference)
    return (mean_k * root_term * difference, mean_k * (EPS_SQUARE + 2.0 * difference * difference) / root_term)

def restrict(field):
    first, second, third = field.shape
    return field.reshape(first // 2, 2, second // 2, 2, third // 2, 2).sum(axis=(1, 3, 5))

def prolong(field):
    return jnp.repeat(jnp.repeat(jnp.repeat(field, 2, 0), 2, 1), 2, 2)

def parity(array_shape, axis_no, odd_flag):
    marks = (jnp.arange(array_shape[axis_no]) % 2 == odd_flag).astype(jnp.float32)
    layout = [1, 1, 1]
    layout[axis_no] = array_shape[axis_no]
    return marks.reshape(layout)

def roll_sides(field):
    return ([jnp.roll(field, -1, axis_no) for axis_no in range(3)], [jnp.roll(field, 1, axis_no) for axis_no in range(3)])

def apply_op(field, react_field, w_up, w_lo, sides):
    upper_side, lower_side = sides(field)
    result = react_field * field
    for axis_no in range(3):
        result = result + w_up[axis_no] * (field - upper_side[axis_no]) + w_lo[axis_no] * (field - lower_side[axis_no])
    return result

def smooth(rhs_field, react_field, w_up, w_lo, sides, degree, low_end):
    diagonal = react_field
    for axis_no in range(3):
        diagonal = diagonal + w_up[axis_no] + w_lo[axis_no]
    inverse = 1.0 / diagonal
    centre = (2.0 + low_end) / 2.0
    half_width = (2.0 - low_end) / 2.0
    sigma_ratio = centre / half_width
    rho_now = 1.0 / sigma_ratio
    update = inverse * rhs_field * (1.0 / centre)
    result = update
    remain = rhs_field
    for sweep_no in range(degree - 1):
        remain = remain - apply_op(update, react_field, w_up, w_lo, sides)
        rho_new = 1.0 / (2.0 * sigma_ratio - rho_now)
        update = rho_new * rho_now * update + 2.0 * rho_new / half_width * (inverse * remain)
        result = result + update
        rho_now = rho_new
    return result

def coefficients(state, conductivity, reaction, source):
    w_up, w_lo, flux_up, flux_lo = ([], [], [], [])
    for axis_no in range(3):
        flux, weight = face_set(state, conductivity, jnp.roll(state, -1, axis_no), jnp.roll(conductivity, -1, axis_no))
        w_up.append(weight)
        w_lo.append(jnp.roll(weight, 1, axis_no))
        flux_up.append(flux)
        flux_lo.append(jnp.roll(flux, 1, axis_no))
    residual = reaction * state
    for axis_no in range(3):
        residual = residual - (flux_up[axis_no] - flux_lo[axis_no])
    residual = residual - source
    return (w_up, w_lo, residual)

def reference(initial_state, conductivity, reaction, source):
    state = initial_state
    for newton_no in range(NEWTON):
        w_up, w_lo, residual = coefficients(state, conductivity, reaction, source)
        react_coarse = restrict(reaction)
        wc_up = [restrict(w_up[axis_no] * parity(state.shape, axis_no, 1)) for axis_no in range(3)]
        wc_lo = [restrict(w_lo[axis_no] * parity(state.shape, axis_no, 0)) for axis_no in range(3)]

        def precondition(remain):
            fine = smooth(remain, reaction, w_up, w_lo, roll_sides, SWEEPS_F, 0.3)
            coarse = smooth(restrict(remain), react_coarse, wc_up, wc_lo, roll_sides, SWEEPS_C, 0.05)
            return fine + prolong(coarse)
        remain = -residual
        zed = precondition(remain)
        search = zed
        rz_now = jnp.sum(remain * zed)
        delta_sol = jnp.zeros_like(state)
        for step_no in range(KRYLOV):
            image = apply_op(search, reaction, w_up, w_lo, roll_sides)
            alpha = rz_now / jnp.sum(search * image)
            delta_sol = delta_sol + alpha * search
            remain = remain - alpha * image
            if step_no + 1 < KRYLOV:
                zed = precondition(remain)
                rz_new = jnp.sum(remain * zed)
                search = zed + rz_new / rz_now * search
                rz_now = rz_new
        state = state + delta_sol
    w_up, w_lo, residual = coefficients(state, conductivity, reaction, source)
    return (state, residual)
```

```python
import functools

import jax
import jax.numpy as jnp
from jax import lax
from jax.experimental import pallas as pl
from jax.experimental.pallas import tpu as pltpu
from jax.sharding import PartitionSpec as P

NEWTON = 2
KRYLOV = 3
EPS_SQUARE = 0.25
SCALE, SHIFT = 0.7, 1.0
MESH = pl.DeviceIdType.MESH

LINE = 128
ROWS = 8


def chebyshev_pair(low):
    centre = (2.0 + low) / 2.0
    half_width = (2.0 - low) / 2.0
    sigma = centre / half_width
    rho = 1.0 / sigma
    rho_new = 1.0 / (2.0 * sigma - rho)
    last = 2.0 * rho_new / half_width
    return (1.0 + rho_new * rho) / centre + last * (1.0 - 1.0 / centre), last / centre


FINE_OWN, FINE_NEAR = chebyshev_pair(0.3)
COARSE_OWN, COARSE_NEAR = chebyshev_pair(0.05)

CROSS = [(0, 0), (1, 0), (-1, 0), (0, 1), (0, -1)]
CORNERS = [(1, 1), (1, -1), (-1, 1), (-1, -1)]


def up(field, axis):
    return pltpu.roll(field, field.shape[axis] - 1, axis)


def down(field, axis):
    return pltpu.roll(field, 1, axis)


def index_of(shape, axis):
    return lax.broadcasted_iota(jnp.int32, shape, axis)


def face_terms(mean_k, difference):
    square = difference * difference
    inverse_root = lax.rsqrt(EPS_SQUARE + square)
    root = (EPS_SQUARE + square) * inverse_root
    return mean_k * root * difference, mean_k * (EPS_SQUARE + 2.0 * square) * inverse_root


def mean_of(one, other):
    return 2.0 * one * other / (one + other)


def fold_rows(field):
    row = index_of((ROWS, field.shape[1]), 0)
    return jnp.concatenate([field[8:16], jnp.where(row < 4, field[16:24], field[0:8])], axis=0)


def pair_sum(field, axis):
    odd = lax.rem(index_of(field.shape, axis), 2) == 1
    return field + jnp.where(odd, down(field, axis), up(field, axis))


def plane_sum(field):
    return pair_sum(pair_sum(field, 0), 1)


def kernel(
    sizes, u_ref, k_ref, r_ref, s_ref, out_u, out_f,
    raw0, zed0, raw_h, zed_h, raw_e, zed_e, pack, box_u, mean_x, mean_y, mean_z, react, src,
    v0, inv, wx, wyu, wyl, wzu, wzl, cinv, cwx, cwyu, cwyl, cwzu, cwzl, zs, sums, got1, got2, got3, dummy,
    send_sem, recv_sem,
):
    nx, ny, nz = sizes
    mx, my, mz = lax.axis_index("gx"), lax.axis_index("gy"), lax.axis_index("gz")

    def block_at(dx, dy, dz):
        return (lax.rem(mx + dx + nx, nx), lax.rem(my + dy + ny, ny), lax.rem(mz + dz + nz, nz))

    core_line = [(mx, my, (mz // 2) * 2 + 1 - lax.rem(mz, 2))]
    plane = 4 * (nz // 2)
    here = lax.rem(mx, 4) * (nz // 2) + mz // 2
    plane_line = []
    for step in range(1, plane):
        there = lax.rem(here + step, plane)
        plane_line.append(
            ((mx // 4) * 4 + there // (nz // 2), my, lax.rem(there, nz // 2) * 2 + lax.rem(mz, 2))
        )
    line = (nx // 4) * ny
    at = (mx // 4) * ny + my
    long_line = []
    for step in range(1, line):
        there = lax.rem(at + step, line)
        long_line.append(((there // ny) * 4 + lax.rem(mx, 4), lax.rem(there, ny), mz))

    offsets = [(dx, dy, dz) for dx in (-1, 0, 1) for dy in (-1, 0, 1) for dz in (-1, 0, 1)]
    offsets = [d for d in offsets if d != (0, 0, 0)] + [(2, 0, 0), (-2, 0, 0)]

    zero24 = jnp.zeros((24, LINE), jnp.float32)
    for e in range(4):
        for i in range(12):
            raw_e[e, i] = zero24
    for f in range(4):
        for i in range(14):
            raw0[f, i] = zero24
    for f in range(3):
        for i in range(14):
            raw_h[f, i] = zero24
    for ref, f in ((u_ref, 0), (k_ref, 1), (r_ref, 2), (s_ref, 3)):
        raw0[f, 5:9, 8:16] = ref[...]

    barrier = pltpu.get_barrier_semaphore()
    partners = [block_at(*d) for d in offsets] + core_line + plane_line + long_line
    for partner in partners:
        pl.semaphore_signal(barrier, inc=1, device_id=partner, device_id_type=MESH)

    lane = index_of((ROWS, LINE), 1)
    copies = []

    def send(source, target, slot, device):
        copy = pltpu.make_async_remote_copy(
            source, target, send_sem.at[0], recv_sem.at[slot], device_id=device, device_id_type=MESH
        )
        copy.start()
        copies.append(copy)

    def receive(tiles, slot):
        part = dummy.at[pl.ds(0, tiles)]
        pltpu.make_async_copy(part, part, recv_sem.at[slot]).wait()

    def pack_z(tiles, place):
        low = jnp.zeros((ROWS, LINE), jnp.float32)
        high = low
        for g, tile in enumerate(tiles):
            mine = lane // 8 == g
            low = jnp.where(mine, tile if g == 0 else pltpu.roll(tile, 8 * g, 1), low)
            shift = (8 * g + 8) % LINE
            high = jnp.where(mine, pltpu.roll(tile, shift, 1) if shift else tile, high)
        pack[place, 0] = low
        pack[place, 1] = high

    def unpack_z(low_tile, high_tile, g):
        shift = (LINE - 8 * g) % LINE
        above = pltpu.roll(low_tile, shift, 1) if shift else low_tile
        shift = (LINE - 8 - 8 * g) % LINE
        below = pltpu.roll(high_tile, shift, 1) if shift else high_tile
        return jnp.where(lane < 64, above, below)

    def exchange_wide(raw, zed, place, fields, far, slot):
        everything = pl.ds(0, fields)
        own = (everything, pl.ds(5, 4), pl.ds(8, 8))
        for dx, dy in CORNERS:
            target = (everything, pl.ds(5 - 4 * dx, 4), pl.ds(8 - 8 * dy, 8))
            send(raw.at[own], raw.at[target], slot, block_at(dx, dy, 0))
        for dx, dy in CORNERS + CROSS:
            for dz in (1, -1):
                send(
                    pack.at[place, (1 + dz) // 2],
                    zed.at[1 - dx, 1 - dy, (1 - dz) // 2],
                    slot,
                    block_at(dx, dy, dz),
                )
        some = pl.ds(0, far)
        rows = pl.ds(8, 8)
        send(raw.at[some, pl.ds(8, 1), rows], raw.at[some, pl.ds(0, 1), rows], slot, block_at(2, 0, 0))
        send(raw.at[some, pl.ds(5, 1), rows], raw.at[some, pl.ds(13, 1), rows], slot, block_at(-2, 0, 0))
        for dx, dy in CROSS[1:]:
            target = (everything, pl.ds(5 - 4 * dx, 4), pl.ds(8 - 8 * dy, 8))
            send(raw.at[own], raw.at[target], slot, block_at(dx, dy, 0))
        return 16 * fields + 18 + 2 * far + 16 * fields

    def wide_slab(raw, zed, field, i):
        main = raw[field, i]
        if i in (0, 13):
            return jnp.concatenate([main, jnp.zeros_like(main)], axis=1)
        column, s = divmod(i - 1, 4)
        g = field * 4 + s
        halo = [unpack_z(zed[column, y, 1], zed[column, y, 0], g) for y in range(3)]
        return jnp.concatenate([main, jnp.concatenate(halo, axis=0)], axis=1)

    def exchange_v(tiles, e):
        place, slot = 2 + e, 2 + e
        for s in range(4):
            raw_e[e, 4 + s, 8:16] = tiles[s]
        pack_z(tiles, place)
        raw, zed = raw_e.at[e], zed_e.at[e]
        rows = pl.ds(8, 8)
        for dx, dy in CORNERS:
            source = (pl.ds(6 if dx > 0 else 4, 2), rows)
            target = (pl.ds(2 if dx > 0 else 8, 2), pl.ds(8 - 8 * dy, 8))
            send(raw.at[source], raw.at[target], slot, block_at(dx, dy, 0))
        for dx, dy in CROSS:
            for dz in (1, -1):
                send(
                    pack.at[place, (1 + dz) // 2],
                    zed.at[1 - dx, 1 - dy, (1 - dz) // 2],
                    slot,
                    block_at(dx, dy, dz),
                )
        for dx, dy in CROSS[1:]:
            target = (pl.ds(4 - 4 * dx, 4), pl.ds(8 - 8 * dy, 8))
            send(raw.at[pl.ds(4, 4), rows], raw.at[target], slot, block_at(dx, dy, 0))
        receive(8 + 10 + 16, slot)
        slabs = []
        nothing = jnp.zeros((ROWS, LINE), jnp.float32)
        row = index_of((ROWS, LINE), 0)
        for i in range(12):
            main = fold_rows(raw_e[e, i])
            column, s = divmod(i, 4)
            own_halo, side_halo = nothing, nothing
            if 2 <= i < 10:
                own_halo = unpack_z(zed_e[e, column, 1, 1], zed_e[e, column, 1, 0], s)
            if 4 <= i < 8:
                side_halo = jnp.where(
                    row < 4,
                    unpack_z(zed_e[e, 1, 2, 1], zed_e[e, 1, 2, 0], s),
                    unpack_z(zed_e[e, 1, 0, 1], zed_e[e, 1, 0, 0], s),
                )
            slabs.append(jnp.concatenate([main, jnp.concatenate([own_halo, side_halo], axis=0)], axis=1))
        return slabs

    def coefficients():
        face_x = [face_terms(mean_x[i], box_u[i + 1] - box_u[i]) for i in range(13)]
        cface = []
        for j in range(7):
            cface.append(plane_sum(face_x[2 * j][1]))
            if 1 <= j < 6:
                cwx[j - 1] = fold_rows(cface[j])
        for i in range(7):
            wx[i] = fold_rows(face_x[i + 3][1])
        for c in range(6):
            pair_y, pair_z, pair_r = None, None, None
            for half in range(2):
                i = 2 * c + half
                u = box_u[i + 1]
                re = react[i]
                flux_y, w_y = face_terms(mean_y[i], up(u, 0) - u)
                flux_z, w_z = face_terms(mean_z[i], up(u, 1) - u)
                low_y, low_z = down(w_y, 0), down(w_z, 1)
                force = (
                    src[i]
                    - re * u
                    + (face_x[i + 1][0] - face_x[i][0])
                    + (flux_y - down(flux_y, 0))
                    + (flux_z - down(flux_z, 1))
                )
                v0[i] = fold_rows(force)
                if 2 <= i < 10:
                    diagonal = re + face_x[i + 1][1] + face_x[i][1] + w_y + low_y + w_z + low_z
                    inv[i - 2] = fold_rows(1.0 / diagonal)
                if 3 <= i < 9:
                    wyu[i - 3] = fold_rows(w_y)
                    wyl[i - 3] = fold_rows(low_y)
                    wzu[i - 3] = fold_rows(w_z)
                    wzl[i - 3] = fold_rows(low_z)
                pair_y = w_y if half == 0 else pair_y + w_y
                pair_z = w_z if half == 0 else pair_z + w_z
                pair_r = re if half == 0 else pair_r + re
            odd_row = lax.rem(index_of((24, 2 * LINE), 0), 2) == 1
            odd_lane = lax.rem(index_of((24, 2 * LINE), 1), 2) == 1
            sum_y = pair_sum(jnp.where(odd_row, pair_y, up(pair_y, 0)), 1)
            sum_z = pair_sum(jnp.where(odd_lane, pair_z, up(pair_z, 1)), 0)
            low_y, low_z = pltpu.roll(sum_y, 2, 0), pltpu.roll(sum_z, 2, 1)
            diagonal = plane_sum(pair_r) + cface[c] + cface[c + 1] + sum_y + low_y + sum_z + low_z
            cinv[c] = fold_rows(1.0 / diagonal)
            if 1 <= c < 5:
                cwyu[c - 1] = fold_rows(sum_y)
                cwyl[c - 1] = fold_rows(low_y)
                cwzu[c - 1] = fold_rows(sum_z)
                cwzl[c - 1] = fold_rows(low_z)

    def precondition(v, j):
        own = [inv[i] * v[i + 2] for i in range(8)]
        coarse = [cinv[c] * plane_sum(v[2 * c] + v[2 * c + 1]) for c in range(6)]
        coarse_z = []
        for c in range(4):
            q = coarse[c + 1]
            near = (
                cwx[c] * coarse[c]
                + cwx[c + 1] * coarse[c + 2]
                + cwyu[c] * pltpu.roll(q, 14, 0)
                + cwyl[c] * pltpu.roll(q, 2, 0)
                + cwzu[c] * pltpu.roll(q, 2 * LINE - 2, 1)
                + cwzl[c] * pltpu.roll(q, 2, 1)
            )
            coarse_z.append(COARSE_OWN * q + COARSE_NEAR * (cinv[c + 1] * near))
        for i in range(6):
            q = own[i + 1]
            near = (
                wx[i] * own[i]
                + wx[i + 1] * own[i + 2]
                + wyu[i] * up(q, 0)
                + wyl[i] * down(q, 0)
                + wzu[i] * up(q, 1)
                + wzl[i] * down(q, 1)
            )
            zs[j, i] = FINE_OWN * q + FINE_NEAR * (inv[i + 1] * near) + coarse_z[(i + 1) // 2]

    def image(j, s):
        i = s + 1
        mid = zs[j, i]
        here = mid[0:8, 0:LINE]
        tall, wide = mid[:, 0:LINE], mid[0:8, :]
        own = (slice(0, 8), slice(0, LINE))
        total = react[i + 3, 8:16, 0:LINE] * here
        for weight, other in (
            (wx[(i,) + own], zs[(j, i - 1) + own]),
            (wx[(i + 1,) + own], zs[(j, i + 1) + own]),
            (wyu[(i,) + own], up(tall, 0)[0:8]),
            (wyl[(i,) + own], down(tall, 0)[0:8]),
            (wzu[(i,) + own], up(wide, 1)[:, 0:LINE]),
            (wzl[(i,) + own], down(wide, 1)[:, 0:LINE]),
        ):
            total = total + weight * (here - other)
        return total

    def global_sum(rows, which, between):
        group = index_of((1, LINE), 1) // 16
        mixed = jnp.zeros((1, LINE), jnp.float32)
        for n, row in enumerate(rows):
            row = jnp.sum(row, axis=0, keepdims=True)
            for shift in (64, 32, 16):
                row = row + pltpu.roll(row, shift, 1)
            mixed = jnp.where(group == n, row, mixed)
        phases = ((core_line, got1), (plane_line, got2), (long_line, got3))
        for phase, (partners, got) in enumerate(phases):
            sums[which, phase] = mixed
            slot = 6 + 3 * which + phase
            for n, partner in enumerate(partners):
                send(sums.at[which, phase], got.at[which, n], slot, partner)
            if phase == 0:
                between()
            part = got.at[which]
            pltpu.make_async_copy(part, part, recv_sem.at[slot]).wait()
            mixed = mixed + jnp.sum(got[which], axis=0)
        return [jnp.sum(jnp.where(group == n, mixed, 0.0), axis=1, keepdims=True) for n in range(6)]

    def solve(m):
        h = [(m[n + 1] + SHIFT * m[n]) * (1.0 / SCALE) for n in range(5)]

        def inverse(pivot, of):
            good = pivot > 1e-6 * of
            return jnp.where(good, 1.0 / jnp.where(good, pivot, 1.0), 0.0)

        i0 = inverse(h[0], jnp.zeros_like(h[0]))
        l1, l2 = h[1] * i0, h[2] * i0
        i1 = inverse(h[2] - l1 * h[1], h[2])
        h21 = h[3] - l2 * h[1]
        l21 = h21 * i1
        i2 = inverse(h[4] - l2 * h[2] - l21 * h21, h[4])
        y0 = m[0]
        y1 = m[1] - l1 * y0
        y2 = m[2] - l2 * y0 - l21 * y1
        c2 = y2 * i2
        c1 = y1 * i1 - l21 * c2
        c0 = y0 * i0 - l1 * c1 - l2 * c2
        return c0, c1, c2

    def total_of(tiles, others):
        total = tiles[0] * others[0]
        for s in range(1, 4):
            total = total + tiles[s] * others[s]
        return total

    pack_z([raw0[f, 5 + s, 8:16] for f in range(4) for s in range(4)], 0)
    pl.semaphore_wait(barrier, len(partners))
    count = exchange_wide(raw0, zed0, 0, 4, 2, 0)
    receive(count, 0)
    for i in range(14):
        box_u[i] = wide_slab(raw0, zed0, 0, i)
    k_slabs = [wide_slab(raw0, zed0, 1, i) for i in range(14)]
    for i in range(13):
        mean_x[i] = mean_of(k_slabs[i], k_slabs[i + 1])
    for i in range(12):
        k = k_slabs[i + 1]
        mean_y[i] = mean_of(k, up(k, 0))
        mean_z[i] = mean_of(k, up(k, 1))
        react[i] = wide_slab(raw0, zed0, 2, i + 1)
        src[i] = wide_slab(raw0, zed0, 3, i + 1)

    own = (slice(0, 8), slice(0, LINE))
    for newton in range(NEWTON):
        coefficients()
        rows = []
        v = [v0[i] for i in range(12)]
        tiles = [slab[0:8, 0:LINE] for slab in v[4:8]]
        for j in range(KRYLOV):
            precondition(v, j)
            z_tiles = [zs[(j, s + 1) + own] for s in range(4)]
            rows.append(total_of(tiles, z_tiles))
            if newton + 1 < NEWTON:
                for s in range(4):
                    raw_h[j, 5 + s, 8:16] = z_tiles[s]
            tiles = [SCALE * image(j, s) - SHIFT * tiles[s] for s in range(4)]
            rows.append(total_of(tiles, z_tiles))
            if j + 1 < KRYLOV:
                v = exchange_v(tiles, 2 * newton + j)

        def beside(newton=newton):
            if newton + 1 < NEWTON:
                pack_z([raw_h[f, 5 + s, 8:16] for f in range(3) for s in range(4)], 1)
                exchange_wide(raw_h, zed_h, 1, 3, 3, 1)

        c = solve(global_sum(rows, newton, beside))
        if newton + 1 < NEWTON:
            receive(32 * 3 + 18 + 6, 1)
            for i in range(14):
                total = box_u[i]
                for j in range(3):
                    total = total + c[j] * wide_slab(raw_h, zed_h, j, i)
                box_u[i] = total

    last = []
    for i in range(6):
        total = fold_rows(box_u[i + 4])
        for j in range(3):
            total = total + c[j] * zs[j, i]
        last.append(total)
    low_flux = None
    for s in range(-1, 4):
        lower, upper = last[s + 1][own], last[s + 2][own]
        flux, _ = face_terms(mean_x[s + 5, 8:16, 0:LINE], upper - lower)
        if s >= 0:
            mid = last[s + 1]
            tall = mid[:, 0:LINE]
            wide = mid[0:8, :]
            out_u[s] = lower
            flux_y, _ = face_terms(fold_rows(mean_y[s + 4, :, 0:LINE]), up(tall, 0) - tall)
            flux_z, _ = face_terms(mean_z[s + 4, 8:16, :], up(wide, 1) - wide)
            out_f[s] = (
                react[s + 4, 8:16, 0:LINE] * lower
                - (flux - low_flux)
                - (flux_y - down(flux_y, 0))[0:8]
                - (flux_z - down(flux_z, 1))[:, 0:LINE]
                - src[s + 4, 8:16, 0:LINE]
            )
        low_flux = flux
    for copy in copies:
        copy.wait_send()


def local(sizes, state, conductivity, reaction, source):
    nx, ny, nz = sizes
    plane, line = 4 * (nz // 2), (nx // 4) * ny

    def vmem(*shape):
        return pltpu.VMEM(shape, jnp.float32)

    full, half = (24, 2 * LINE), (16, 2 * LINE)
    tile = (ROWS, LINE)
    scratch = [
        vmem(4, 14, 24, LINE), vmem(3, 3, 2, *tile), vmem(3, 14, 24, LINE), vmem(3, 3, 2, *tile),
        vmem(4, 12, 24, LINE), vmem(4, 3, 3, 2, *tile), vmem(6, 2, *tile), vmem(14, *full),
        vmem(13, *full), vmem(12, *full), vmem(12, *full), vmem(12, *full), vmem(12, *full),
        vmem(12, *half), vmem(8, *half), vmem(7, *half), vmem(6, *half), vmem(6, *half), vmem(6, *half), vmem(6, *half),
        vmem(6, *half), vmem(5, *half), vmem(4, *half), vmem(4, *half), vmem(4, *half), vmem(4, *half),
        vmem(3, 6, *half), vmem(2, 3, 1, LINE), vmem(2, 1, 1, LINE), vmem(2, plane - 1, 1, LINE), vmem(2, line - 1, 1, LINE),
        vmem(160, *tile), pltpu.SemaphoreType.DMA((1,)), pltpu.SemaphoreType.DMA((12,)),
    ]
    spec = pl.BlockSpec(memory_space=pltpu.VMEM)
    return pl.pallas_call(
        functools.partial(kernel, sizes),
        out_shape=[jax.ShapeDtypeStruct(state.shape, jnp.float32)] * 2,
        in_specs=[spec] * 4,
        out_specs=[spec] * 2,
        scratch_shapes=scratch,
        compiler_params=pltpu.CompilerParams(
            collective_id=0, has_side_effects=True, vmem_limit_bytes=32 * 1024 * 1024
        ),
    )(state, conductivity, reaction, source)


def solution(mesh):
    sizes = tuple(mesh.shape[name] for name in ("gx", "gy", "gz"))
    placed = P("gx", "gy", "gz")
    return jax.shard_map(
        functools.partial(local, sizes),
        mesh=mesh,
        in_specs=(placed,) * 4,
        out_specs=(placed, placed),
        check_vma=False,
    )
```

```python
import functools

import jax
import jax.numpy as jnp
from jax import lax
from jax.experimental import pallas as pl
from jax.experimental.pallas import tpu as pltpu
from jax.sharding import PartitionSpec as P

NEWTON = 2
KRYLOV = 3
EPS_SQUARE = 0.25
SCALE, SHIFT = 0.7, 1.0
MESH = pl.DeviceIdType.MESH

LINE = 128
ROWS = 8


def chebyshev_pair(low):
    centre = (2.0 + low) / 2.0
    half_width = (2.0 - low) / 2.0
    sigma = centre / half_width
    rho = 1.0 / sigma
    rho_new = 1.0 / (2.0 * sigma - rho)
    last = 2.0 * rho_new / half_width
    return (1.0 + rho_new * rho) / centre + last * (1.0 - 1.0 / centre), last / centre


FINE_OWN, FINE_NEAR = chebyshev_pair(0.3)
COARSE_OWN, COARSE_NEAR = chebyshev_pair(0.05)

CROSS = [(0, 0), (1, 0), (-1, 0), (0, 1), (0, -1)]
CORNERS = [(1, 1), (1, -1), (-1, 1), (-1, -1)]


def up(field, axis):
    return pltpu.roll(field, field.shape[axis] - 1, axis)


def down(field, axis):
    return pltpu.roll(field, 1, axis)


def index_of(shape, axis):
    return lax.broadcasted_iota(jnp.int32, shape, axis)


def face_terms(mean_k, difference):
    square = difference * difference
    inverse_root = lax.rsqrt(EPS_SQUARE + square)
    root = (EPS_SQUARE + square) * inverse_root
    return mean_k * root * difference, mean_k * (EPS_SQUARE + 2.0 * square) * inverse_root


def mean_of(one, other):
    return 2.0 * one * other / (one + other)


def fold_rows(field):
    row = index_of((ROWS, field.shape[1]), 0)
    return jnp.concatenate([field[8:16], jnp.where(row < 4, field[16:24], field[0:8])], axis=0)


def pair_sum(field, axis):
    odd = lax.rem(index_of(field.shape, axis), 2) == 1
    return field + jnp.where(odd, down(field, axis), up(field, axis))


def plane_sum(field):
    return pair_sum(pair_sum(field, 0), 1)


def kernel(
    sizes, u_ref, k_ref, r_ref, s_ref, out_u, out_f,
    raw0, zed0, raw_h, zed_h, raw_e, zed_e, pack, box_u, mean_x, mean_y, mean_z, react, src,
    v0, inv, wx, wyu, wyl, wzu, wzl, cinv, cwx, cwyu, cwyl, cwzu, cwzl, zs, sums, got1, got2, got3, ends, dummy,
    send_sem, recv_sem,
):
    nx, ny, nz = sizes
    mx, my, mz = lax.axis_index("gx"), lax.axis_index("gy"), lax.axis_index("gz")

    group, place_y = mx // 4, lax.rem(mx, 4)
    bx, by = group * 4 + my, place_y
    partner = (group * 4 + my, place_y, mz)
    alone = my == place_y

    def block_at(dx, dy, dz):
        x, y = lax.rem(bx + dx + nx, nx), lax.rem(by + dy + ny, ny)
        return ((x // 4) * 4 + y, lax.rem(x, 4), lax.rem(mz + dz + nz, nz))

    core_line = [(mx, my, (mz // 2) * 2 + 1 - lax.rem(mz, 2))]
    plane = 4 * (nz // 2)
    here = lax.rem(mx, 4) * (nz // 2) + mz // 2
    plane_line = []
    for step in range(1, plane):
        there = lax.rem(here + step, plane)
        plane_line.append(
            ((mx // 4) * 4 + there // (nz // 2), my, lax.rem(there, nz // 2) * 2 + lax.rem(mz, 2))
        )
    line = (nx // 4) * ny
    at = (mx // 4) * ny + my
    long_line = []
    for step in range(1, line):
        there = lax.rem(at + step, line)
        long_line.append(((there // ny) * 4 + lax.rem(mx, 4), lax.rem(there, ny), mz))

    offsets = [(dx, dy, dz) for dx in (-1, 0, 1) for dy in (-1, 0, 1) for dz in (-1, 0, 1)]
    offsets = [d for d in offsets if d != (0, 0, 0)] + [(2, 0, 0), (-2, 0, 0)]

    barrier = pltpu.get_barrier_semaphore()
    partners = [block_at(*d) for d in offsets] + core_line + plane_line + long_line

    @pl.when(jnp.logical_not(alone))
    def _():
        pl.semaphore_signal(barrier, inc=1, device_id=partner, device_id_type=MESH)

    for other in partners:
        pl.semaphore_signal(barrier, inc=1, device_id=other, device_id_type=MESH)

    lane = index_of((ROWS, LINE), 1)
    copies = []

    def send(source, target, slot, device):
        copy = pltpu.make_async_remote_copy(
            source, target, send_sem.at[0], recv_sem.at[slot], device_id=device, device_id_type=MESH
        )
        copy.start()
        copies.append(copy)

    def receive(tiles, slot):
        part = dummy.at[pl.ds(0, tiles)]
        pltpu.make_async_copy(part, part, recv_sem.at[slot]).wait()

    def pack_z(tiles, place):
        low = jnp.zeros((ROWS, LINE), jnp.float32)
        high = low
        for g, tile in enumerate(tiles):
            mine = lane // 8 == g
            low = jnp.where(mine, tile if g == 0 else pltpu.roll(tile, 8 * g, 1), low)
            shift = (8 * g + 8) % LINE
            high = jnp.where(mine, pltpu.roll(tile, shift, 1) if shift else tile, high)
        pack[place, 0] = low
        pack[place, 1] = high

    def unpack_z(low_tile, high_tile, g):
        shift = (LINE - 8 * g) % LINE
        above = pltpu.roll(low_tile, shift, 1) if shift else low_tile
        shift = (LINE - 8 - 8 * g) % LINE
        below = pltpu.roll(high_tile, shift, 1) if shift else high_tile
        return jnp.where(lane < 64, above, below)

    def exchange_wide(raw, zed, place, fields, far, slot):
        everything = pl.ds(0, fields)
        own = (everything, pl.ds(5, 4), pl.ds(8, 8))
        for dx, dy in CORNERS:
            target = (everything, pl.ds(5 - 4 * dx, 4), pl.ds(8 - 8 * dy, 8))
            send(raw.at[own], raw.at[target], slot, block_at(dx, dy, 0))
        for dx, dy in CORNERS + CROSS:
            for dz in (1, -1):
                send(
                    pack.at[place, (1 + dz) // 2],
                    zed.at[1 - dx, 1 - dy, (1 - dz) // 2],
                    slot,
                    block_at(dx, dy, dz),
                )
        some = pl.ds(0, far)
        rows = pl.ds(8, 8)
        send(raw.at[some, pl.ds(8, 1), rows], raw.at[some, pl.ds(0, 1), rows], slot, block_at(2, 0, 0))
        send(raw.at[some, pl.ds(5, 1), rows], raw.at[some, pl.ds(13, 1), rows], slot, block_at(-2, 0, 0))
        for dx, dy in CROSS[1:]:
            target = (everything, pl.ds(5 - 4 * dx, 4), pl.ds(8 - 8 * dy, 8))
            send(raw.at[own], raw.at[target], slot, block_at(dx, dy, 0))
        return 16 * fields + 18 + 2 * far + 16 * fields

    def wide_slab(raw, zed, field, i):
        if i in (0, 13):
            nothing = jnp.zeros((ROWS, LINE), jnp.float32)
            main = jnp.concatenate([nothing, raw[field, i, 8:16], nothing], axis=0)
            return jnp.concatenate([main, jnp.zeros_like(main)], axis=1)
        main = raw[field, i]
        column, s = divmod(i - 1, 4)
        g = field * 4 + s
        halo = [unpack_z(zed[column, y, 1], zed[column, y, 0], g) for y in range(3)]
        return jnp.concatenate([main, jnp.concatenate(halo, axis=0)], axis=1)

    def exchange_v(tiles, e):
        place, slot = 2 + e, 2 + e
        for s in range(4):
            raw_e[e, 4 + s, 8:16] = tiles[s]
        pack_z(tiles, place)
        raw, zed = raw_e.at[e], zed_e.at[e]
        rows = pl.ds(8, 8)
        for dx, dy in CORNERS:
            source = (pl.ds(6 if dx > 0 else 4, 2), rows)
            target = (pl.ds(2 if dx > 0 else 8, 2), pl.ds(8 - 8 * dy, 8))
            send(raw.at[source], raw.at[target], slot, block_at(dx, dy, 0))
        for dx, dy in CROSS:
            for dz in (1, -1):
                send(
                    pack.at[place, (1 + dz) // 2],
                    zed.at[1 - dx, 1 - dy, (1 - dz) // 2],
                    slot,
                    block_at(dx, dy, dz),
                )
        for dx, dy in CROSS[1:]:
            target = (pl.ds(4 - 4 * dx, 4), pl.ds(8 - 8 * dy, 8))
            send(raw.at[pl.ds(4, 4), rows], raw.at[target], slot, block_at(dx, dy, 0))
        receive(8 + 10 + 16, slot)
        slabs = []
        nothing = jnp.zeros((ROWS, LINE), jnp.float32)
        row = index_of((ROWS, LINE), 0)
        for i in range(12):
            if 2 <= i < 10:
                main = fold_rows(raw_e[e, i])
            else:
                main = jnp.concatenate([raw_e[e, i, 8:16], nothing], axis=0)
            column, s = divmod(i, 4)
            own_halo, side_halo = nothing, nothing
            if 2 <= i < 10:
                own_halo = unpack_z(zed_e[e, column, 1, 1], zed_e[e, column, 1, 0], s)
            if 4 <= i < 8:
                side_halo = jnp.where(
                    row < 4,
                    unpack_z(zed_e[e, 1, 2, 1], zed_e[e, 1, 2, 0], s),
                    unpack_z(zed_e[e, 1, 0, 1], zed_e[e, 1, 0, 0], s),
                )
            slabs.append(jnp.concatenate([main, jnp.concatenate([own_halo, side_halo], axis=0)], axis=1))
        return slabs

    def coefficients():
        face_x = [face_terms(mean_x[i], box_u[i + 1] - box_u[i]) for i in range(13)]
        cface = []
        for j in range(7):
            cface.append(plane_sum(face_x[2 * j][1]))
            if 1 <= j < 6:
                cwx[j - 1] = fold_rows(cface[j])
        for i in range(7):
            wx[i] = fold_rows(face_x[i + 3][1])
        for c in range(6):
            pair_y, pair_z, pair_r = None, None, None
            for half in range(2):
                i = 2 * c + half
                u = box_u[i + 1]
                re = react[i]
                flux_y, w_y = face_terms(mean_y[i], up(u, 0) - u)
                flux_z, w_z = face_terms(mean_z[i], up(u, 1) - u)
                low_y, low_z = down(w_y, 0), down(w_z, 1)
                force = (
                    src[i]
                    - re * u
                    + (face_x[i + 1][0] - face_x[i][0])
                    + (flux_y - down(flux_y, 0))
                    + (flux_z - down(flux_z, 1))
                )
                v0[i] = fold_rows(force)
                if 2 <= i < 10:
                    diagonal = re + face_x[i + 1][1] + face_x[i][1] + w_y + low_y + w_z + low_z
                    inv[i - 2] = fold_rows(1.0 / diagonal)
                if 3 <= i < 9:
                    wyu[i - 3] = fold_rows(w_y)
                    wyl[i - 3] = fold_rows(low_y)
                    wzu[i - 3] = fold_rows(w_z)
                    wzl[i - 3] = fold_rows(low_z)
                pair_y = w_y if half == 0 else pair_y + w_y
                pair_z = w_z if half == 0 else pair_z + w_z
                pair_r = re if half == 0 else pair_r + re
            odd_row = lax.rem(index_of((24, 2 * LINE), 0), 2) == 1
            odd_lane = lax.rem(index_of((24, 2 * LINE), 1), 2) == 1
            sum_y = pair_sum(jnp.where(odd_row, pair_y, up(pair_y, 0)), 1)
            sum_z = pair_sum(jnp.where(odd_lane, pair_z, up(pair_z, 1)), 0)
            low_y, low_z = pltpu.roll(sum_y, 2, 0), pltpu.roll(sum_z, 2, 1)
            diagonal = plane_sum(pair_r) + cface[c] + cface[c + 1] + sum_y + low_y + sum_z + low_z
            cinv[c] = fold_rows(1.0 / diagonal)
            if 1 <= c < 5:
                cwyu[c - 1] = fold_rows(sum_y)
                cwyl[c - 1] = fold_rows(low_y)
                cwzu[c - 1] = fold_rows(sum_z)
                cwzl[c - 1] = fold_rows(low_z)

    def precondition(v, j):
        own = [inv[i] * v[i + 2] for i in range(8)]
        coarse = [cinv[c] * plane_sum(v[2 * c] + v[2 * c + 1]) for c in range(6)]
        coarse_z = []
        for c in range(4):
            q = coarse[c + 1]
            near = (
                cwx[c] * coarse[c]
                + cwx[c + 1] * coarse[c + 2]
                + cwyu[c] * pltpu.roll(q, 14, 0)
                + cwyl[c] * pltpu.roll(q, 2, 0)
                + cwzu[c] * pltpu.roll(q, 2 * LINE - 2, 1)
                + cwzl[c] * pltpu.roll(q, 2, 1)
            )
            coarse_z.append(COARSE_OWN * q + COARSE_NEAR * (cinv[c + 1] * near))
        for i in range(6):
            q = own[i + 1]
            near = (
                wx[i] * own[i]
                + wx[i + 1] * own[i + 2]
                + wyu[i] * up(q, 0)
                + wyl[i] * down(q, 0)
                + wzu[i] * up(q, 1)
                + wzl[i] * down(q, 1)
            )
            zs[j, i] = FINE_OWN * q + FINE_NEAR * (inv[i + 1] * near) + coarse_z[(i + 1) // 2]

    def image(j, s):
        i = s + 1
        mid = zs[j, i]
        here = mid[0:8, 0:LINE]
        tall, wide = mid[:, 0:LINE], mid[0:8, :]
        own = (slice(0, 8), slice(0, LINE))
        total = react[i + 3, 8:16, 0:LINE] * here
        for weight, other in (
            (wx[(i,) + own], zs[(j, i - 1) + own]),
            (wx[(i + 1,) + own], zs[(j, i + 1) + own]),
            (wyu[(i,) + own], up(tall, 0)[0:8]),
            (wyl[(i,) + own], down(tall, 0)[0:8]),
            (wzu[(i,) + own], up(wide, 1)[:, 0:LINE]),
            (wzl[(i,) + own], down(wide, 1)[:, 0:LINE]),
        ):
            total = total + weight * (here - other)
        return total

    def global_sum(rows, which, between):
        group = index_of((1, LINE), 1) // 16
        mixed = jnp.zeros((1, LINE), jnp.float32)
        for n, row in enumerate(rows):
            row = jnp.sum(row, axis=0, keepdims=True)
            for shift in (64, 32, 16):
                row = row + pltpu.roll(row, shift, 1)
            mixed = jnp.where(group == n, row, mixed)
        phases = ((core_line, got1), (plane_line, got2), (long_line, got3))
        for phase, (partners, got) in enumerate(phases):
            sums[which, phase] = mixed
            slot = 6 + 3 * which + phase
            for n, partner in enumerate(partners):
                send(sums.at[which, phase], got.at[which, n], slot, partner)
            if phase == 0:
                between()
            part = got.at[which]
            pltpu.make_async_copy(part, part, recv_sem.at[slot]).wait()
            mixed = mixed + jnp.sum(got[which], axis=0)
        return [jnp.sum(jnp.where(group == n, mixed, 0.0), axis=1, keepdims=True) for n in range(6)]

    def solve(m):
        h = [(m[n + 1] + SHIFT * m[n]) * (1.0 / SCALE) for n in range(5)]

        def inverse(pivot, of):
            good = pivot > 1e-6 * of
            return jnp.where(good, 1.0 / jnp.where(good, pivot, 1.0), 0.0)

        i0 = inverse(h[0], jnp.zeros_like(h[0]))
        l1, l2 = h[1] * i0, h[2] * i0
        i1 = inverse(h[2] - l1 * h[1], h[2])
        h21 = h[3] - l2 * h[1]
        l21 = h21 * i1
        i2 = inverse(h[4] - l2 * h[2] - l21 * h21, h[4])
        y0 = m[0]
        y1 = m[1] - l1 * y0
        y2 = m[2] - l2 * y0 - l21 * y1
        c2 = y2 * i2
        c1 = y1 * i1 - l21 * c2
        c0 = y0 * i0 - l1 * c1 - l2 * c2
        return c0, c1, c2

    def total_of(tiles, others):
        total = tiles[0] * others[0]
        for s in range(1, 4):
            total = total + tiles[s] * others[s]
        return total

    def swap(sources, targets, slot):
        @pl.when(alone)
        def _():
            for source, target in zip(sources, targets):
                pltpu.make_async_copy(source, target, recv_sem.at[slot]).start()

        @pl.when(jnp.logical_not(alone))
        def _():
            for source, target in zip(sources, targets):
                pltpu.make_async_remote_copy(
                    source, target, send_sem.at[0], recv_sem.at[slot], device_id=partner, device_id_type=MESH
                ).start()

        receive(4 * len(sources), slot)

        @pl.when(jnp.logical_not(alone))
        def _():
            part = dummy.at[pl.ds(0, 4 * len(sources))]
            pltpu.make_async_copy(part, part, send_sem.at[0]).wait()

    pl.semaphore_wait(barrier, len(partners) + 1 - alone.astype(jnp.int32))
    swap([u_ref, k_ref, r_ref, s_ref], [raw0.at[f, pl.ds(5, 4), pl.ds(8, 8)] for f in range(4)], 12)
    pack_z([raw0[f, 5 + s, 8:16] for f in range(4) for s in range(4)], 0)
    count = exchange_wide(raw0, zed0, 0, 4, 2, 0)
    receive(count, 0)
    for i in range(14):
        box_u[i] = wide_slab(raw0, zed0, 0, i)
    k_slabs = [wide_slab(raw0, zed0, 1, i) for i in range(14)]
    for i in range(13):
        mean_x[i] = mean_of(k_slabs[i], k_slabs[i + 1])
    for i in range(12):
        k = k_slabs[i + 1]
        mean_y[i] = mean_of(k, up(k, 0))
        mean_z[i] = mean_of(k, up(k, 1))
        react[i] = wide_slab(raw0, zed0, 2, i + 1)
        src[i] = wide_slab(raw0, zed0, 3, i + 1)

    own = (slice(0, 8), slice(0, LINE))
    for newton in range(NEWTON):
        coefficients()
        rows = []
        v = [v0[i] for i in range(12)]
        tiles = [slab[0:8, 0:LINE] for slab in v[4:8]]
        for j in range(KRYLOV):
            precondition(v, j)
            z_tiles = [zs[(j, s + 1) + own] for s in range(4)]
            rows.append(total_of(tiles, z_tiles))
            if newton + 1 < NEWTON:
                for s in range(4):
                    raw_h[j, 5 + s, 8:16] = z_tiles[s]
            tiles = [SCALE * image(j, s) - SHIFT * tiles[s] for s in range(4)]
            rows.append(total_of(tiles, z_tiles))
            if j + 1 < KRYLOV:
                v = exchange_v(tiles, 2 * newton + j)

        def beside(newton=newton):
            if newton + 1 < NEWTON:
                pack_z([raw_h[f, 5 + s, 8:16] for f in range(3) for s in range(4)], 1)
                exchange_wide(raw_h, zed_h, 1, 3, 3, 1)

        c = solve(global_sum(rows, newton, beside))
        if newton + 1 < NEWTON:
            receive(32 * 3 + 18 + 6, 1)
            for i in range(14):
                total = box_u[i]
                for j in range(3):
                    total = total + c[j] * wide_slab(raw_h, zed_h, j, i)
                box_u[i] = total

    last = []
    for i in range(6):
        total = fold_rows(box_u[i + 4])
        for j in range(3):
            total = total + c[j] * zs[j, i]
        last.append(total)
    low_flux = None
    for s in range(-1, 4):
        lower, upper = last[s + 1][own], last[s + 2][own]
        flux, _ = face_terms(mean_x[s + 5, 8:16, 0:LINE], upper - lower)
        if s >= 0:
            mid = last[s + 1]
            tall = mid[:, 0:LINE]
            wide = mid[0:8, :]
            ends[0, s] = lower
            flux_y, _ = face_terms(fold_rows(mean_y[s + 4, :, 0:LINE]), up(tall, 0) - tall)
            flux_z, _ = face_terms(mean_z[s + 4, 8:16, :], up(wide, 1) - wide)
            ends[1, s] = (
                react[s + 4, 8:16, 0:LINE] * lower
                - (flux - low_flux)
                - (flux_y - down(flux_y, 0))[0:8]
                - (flux_z - down(flux_z, 1))[:, 0:LINE]
                - src[s + 4, 8:16, 0:LINE]
            )
        low_flux = flux
    for copy in copies:
        copy.wait_send()
    swap([ends.at[0], ends.at[1]], [out_u, out_f], 13)


def local(sizes, state, conductivity, reaction, source):
    nx, ny, nz = sizes
    plane, line = 4 * (nz // 2), (nx // 4) * ny

    def vmem(*shape):
        return pltpu.VMEM(shape, jnp.float32)

    full, half = (24, 2 * LINE), (16, 2 * LINE)
    tile = (ROWS, LINE)
    scratch = [
        vmem(4, 14, 24, LINE), vmem(3, 3, 2, *tile), vmem(3, 14, 24, LINE), vmem(3, 3, 2, *tile),
        vmem(4, 12, 24, LINE), vmem(4, 3, 3, 2, *tile), vmem(6, 2, *tile), vmem(14, *full),
        vmem(13, *full), vmem(12, *full), vmem(12, *full), vmem(12, *full), vmem(12, *full),
        vmem(12, *half), vmem(8, *half), vmem(7, *half), vmem(6, *half), vmem(6, *half), vmem(6, *half), vmem(6, *half),
        vmem(6, *half), vmem(5, *half), vmem(4, *half), vmem(4, *half), vmem(4, *half), vmem(4, *half),
        vmem(3, 6, *half), vmem(2, 3, 1, LINE), vmem(2, 1, 1, LINE), vmem(2, plane - 1, 1, LINE), vmem(2, line - 1, 1, LINE),
        vmem(2, 4, *tile), vmem(160, *tile), pltpu.SemaphoreType.DMA((1,)), pltpu.SemaphoreType.DMA((14,)),
    ]
    spec = pl.BlockSpec(memory_space=pl.ANY)
    return pl.pallas_call(
        functools.partial(kernel, sizes),
        out_shape=[jax.ShapeDtypeStruct(state.shape, jnp.float32)] * 2,
        in_specs=[spec] * 4,
        out_specs=[spec] * 2,
        scratch_shapes=scratch,
        compiler_params=pltpu.CompilerParams(
            collective_id=0, has_side_effects=True, vmem_limit_bytes=32 * 1024 * 1024
        ),
    )(state, conductivity, reaction, source)


def solution(mesh):
    sizes = tuple(mesh.shape[name] for name in ("gx", "gy", "gz"))
    placed = P("gx", "gy", "gz")
    return jax.shard_map(
        functools.partial(local, sizes),
        mesh=mesh,
        in_specs=(placed,) * 4,
        out_specs=(placed, placed),
        check_vma=False,
    )
```

```python
import functools

import jax
import jax.numpy as jnp
from jax import lax
from jax.experimental import pallas as pl
from jax.experimental.pallas import tpu as pltpu
from jax.sharding import PartitionSpec as P

NEWTON = 2
KRYLOV = 3
EPS_SQUARE = 0.25
SCALE, SHIFT = 0.7, 1.0
MESH = pl.DeviceIdType.MESH

LINE = 128
ROWS = 8


def chebyshev_pair(low):
    centre = (2.0 + low) / 2.0
    half_width = (2.0 - low) / 2.0
    sigma = centre / half_width
    rho = 1.0 / sigma
    rho_new = 1.0 / (2.0 * sigma - rho)
    last = 2.0 * rho_new / half_width
    return (1.0 + rho_new * rho) / centre + last * (1.0 - 1.0 / centre), last / centre


FINE_OWN, FINE_NEAR = chebyshev_pair(0.3)
COARSE_OWN, COARSE_NEAR = chebyshev_pair(0.05)

CROSS = [(0, 0), (1, 0), (-1, 0), (0, 1), (0, -1)]
CORNERS = [(1, 1), (1, -1), (-1, 1), (-1, -1)]


def up(field, axis):
    return pltpu.roll(field, field.shape[axis] - 1, axis)


def down(field, axis):
    return pltpu.roll(field, 1, axis)


def index_of(shape, axis):
    return lax.broadcasted_iota(jnp.int32, shape, axis)


def face_terms(mean_k, difference):
    square = difference * difference
    inverse_root = lax.rsqrt(EPS_SQUARE + square)
    root = (EPS_SQUARE + square) * inverse_root
    return mean_k * root * difference, mean_k * (EPS_SQUARE + 2.0 * square) * inverse_root


def mean_of(one, other):
    return 2.0 * one * other / (one + other)


def fold_rows(field):
    row = index_of((ROWS, field.shape[1]), 0)
    return jnp.concatenate([field[8:16], jnp.where(row < 4, field[16:24], field[0:8])], axis=0)


def pair_sum(field, axis):
    odd = lax.rem(index_of(field.shape, axis), 2) == 1
    return field + jnp.where(odd, down(field, axis), up(field, axis))


def plane_sum(field):
    return pair_sum(pair_sum(field, 0), 1)


def kernel(
    sizes, u_ref, k_ref, r_ref, s_ref, out_u, out_f,
    raw0, zed0, raw_h, zed_h, raw_e, zed_e, pack, box_u, mean_x, mean_y, mean_z, react, src,
    v0, inv, wx, wyu, wyl, wzu, wzl, cinv, cwx, cwyu, cwyl, cwzu, cwzl, zs, sums, got1, got2, got3, ends, dummy,
    end_zs, end_x, end_y, end_z, end_rs, send_sem, recv_sem, far_sem,
):
    nx, ny, nz = sizes
    mx, my, mz = lax.axis_index("gx"), lax.axis_index("gy"), lax.axis_index("gz")

    group, place_y = mx // 4, lax.rem(mx, 4)
    bx, by = group * 4 + my, place_y
    partner = (group * 4 + my, place_y, mz)
    alone = my == place_y

    def block_at(dx, dy, dz):
        x, y = lax.rem(bx + dx + nx, nx), lax.rem(by + dy + ny, ny)
        return ((x // 4) * 4 + y, lax.rem(x, 4), lax.rem(mz + dz + nz, nz))

    core_line = [(mx, my, (mz // 2) * 2 + 1 - lax.rem(mz, 2))]
    plane = 4 * (nz // 2)
    here = lax.rem(mx, 4) * (nz // 2) + mz // 2
    plane_line = []
    for step in range(1, plane):
        there = lax.rem(here + step, plane)
        plane_line.append(
            ((mx // 4) * 4 + there // (nz // 2), my, lax.rem(there, nz // 2) * 2 + lax.rem(mz, 2))
        )
    line = (nx // 4) * ny
    at = (mx // 4) * ny + my
    long_line = []
    for step in range(1, line):
        there = lax.rem(at + step, line)
        long_line.append(((there // ny) * 4 + lax.rem(mx, 4), lax.rem(there, ny), mz))

    offsets = [(dx, dy, dz) for dx in (-1, 0, 1) for dy in (-1, 0, 1) for dz in (-1, 0, 1)]
    offsets = [d for d in offsets if d != (0, 0, 0)] + [(2, 0, 0), (-2, 0, 0)]

    barrier = pltpu.get_barrier_semaphore()
    partners = [block_at(*d) for d in offsets]
    far_ones = [(lax.rem(mx + 4, nx), my, mz), (lax.rem(mx + nx - 4, nx), my, mz)]

    @pl.when(jnp.logical_not(alone))
    def _():
        pl.semaphore_signal(barrier, inc=1, device_id=partner, device_id_type=MESH)

    for other in partners:
        pl.semaphore_signal(barrier, inc=1, device_id=other, device_id_type=MESH)

    lane = index_of((ROWS, LINE), 1)
    copies = []

    def send(source, target, slot, device):
        copy = pltpu.make_async_remote_copy(
            source, target, send_sem.at[0], recv_sem.at[slot], device_id=device, device_id_type=MESH
        )
        copy.start()
        copies.append(copy)

    def receive(tiles, slot):
        part = dummy.at[pl.ds(0, tiles)]
        pltpu.make_async_copy(part, part, recv_sem.at[slot]).wait()

    def pack_z(tiles, place):
        low = jnp.zeros((ROWS, LINE), jnp.float32)
        high = low
        for g, tile in enumerate(tiles):
            mine = lane // 8 == g
            low = jnp.where(mine, tile if g == 0 else pltpu.roll(tile, 8 * g, 1), low)
            shift = (8 * g + 8) % LINE
            high = jnp.where(mine, pltpu.roll(tile, shift, 1) if shift else tile, high)
        pack[place, 0] = low
        pack[place, 1] = high

    def unpack_z(low_tile, high_tile, g):
        shift = (LINE - 8 * g) % LINE
        above = pltpu.roll(low_tile, shift, 1) if shift else low_tile
        shift = (LINE - 8 - 8 * g) % LINE
        below = pltpu.roll(high_tile, shift, 1) if shift else high_tile
        return jnp.where(lane < 64, above, below)

    def exchange_wide(raw, zed, place, fields, far, slot):
        everything = pl.ds(0, fields)
        own = (everything, pl.ds(5, 4), pl.ds(8, 8))
        for dx, dy in CORNERS:
            target = (everything, pl.ds(5 - 4 * dx, 4), pl.ds(8 - 8 * dy, 8))
            send(raw.at[own], raw.at[target], slot, block_at(dx, dy, 0))
        for dx, dy in CORNERS + CROSS:
            for dz in (1, -1):
                send(
                    pack.at[place, (1 + dz) // 2],
                    zed.at[1 - dx, 1 - dy, (1 - dz) // 2],
                    slot,
                    block_at(dx, dy, dz),
                )
        some = pl.ds(0, far)
        rows = pl.ds(8, 8)
        send(raw.at[some, pl.ds(8, 1), rows], raw.at[some, pl.ds(0, 1), rows], slot, block_at(2, 0, 0))
        send(raw.at[some, pl.ds(5, 1), rows], raw.at[some, pl.ds(13, 1), rows], slot, block_at(-2, 0, 0))
        for dx, dy in CROSS[1:]:
            target = (everything, pl.ds(5 - 4 * dx, 4), pl.ds(8 - 8 * dy, 8))
            send(raw.at[own], raw.at[target], slot, block_at(dx, dy, 0))
        return 16 * fields + 18 + 2 * far + 16 * fields

    def wide_slab(raw, zed, field, i):
        if i in (0, 13):
            nothing = jnp.zeros((ROWS, LINE), jnp.float32)
            main = jnp.concatenate([nothing, raw[field, i, 8:16], nothing], axis=0)
            return jnp.concatenate([main, jnp.zeros_like(main)], axis=1)
        main = raw[field, i]
        column, s = divmod(i - 1, 4)
        g = field * 4 + s
        halo = [unpack_z(zed[column, y, 1], zed[column, y, 0], g) for y in range(3)]
        return jnp.concatenate([main, jnp.concatenate(halo, axis=0)], axis=1)

    def exchange_v(tiles, e, between):
        place, slot = 2 + e, 2 + e
        for s in range(4):
            raw_e[e, 4 + s, 8:16] = tiles[s]
        pack_z(tiles, place)
        raw, zed = raw_e.at[e], zed_e.at[e]
        rows = pl.ds(8, 8)
        for dx, dy in CORNERS:
            source = (pl.ds(6 if dx > 0 else 4, 2), rows)
            target = (pl.ds(2 if dx > 0 else 8, 2), pl.ds(8 - 8 * dy, 8))
            send(raw.at[source], raw.at[target], slot, block_at(dx, dy, 0))
        for dx, dy in CROSS:
            for dz in (1, -1):
                send(
                    pack.at[place, (1 + dz) // 2],
                    zed.at[1 - dx, 1 - dy, (1 - dz) // 2],
                    slot,
                    block_at(dx, dy, dz),
                )
        for dx, dy in CROSS[1:]:
            target = (pl.ds(4 - 4 * dx, 4), pl.ds(8 - 8 * dy, 8))
            send(raw.at[pl.ds(4, 4), rows], raw.at[target], slot, block_at(dx, dy, 0))
        between()
        receive(8 + 10 + 16, slot)
        slabs = []
        nothing = jnp.zeros((ROWS, LINE), jnp.float32)
        row = index_of((ROWS, LINE), 0)
        for i in range(12):
            if 2 <= i < 10:
                main = fold_rows(raw_e[e, i])
            else:
                main = jnp.concatenate([raw_e[e, i, 8:16], nothing], axis=0)
            column, s = divmod(i, 4)
            own_halo, side_halo = nothing, nothing
            if 2 <= i < 10:
                own_halo = unpack_z(zed_e[e, column, 1, 1], zed_e[e, column, 1, 0], s)
            if 4 <= i < 8:
                side_halo = jnp.where(
                    row < 4,
                    unpack_z(zed_e[e, 1, 2, 1], zed_e[e, 1, 2, 0], s),
                    unpack_z(zed_e[e, 1, 0, 1], zed_e[e, 1, 0, 0], s),
                )
            slabs.append(jnp.concatenate([main, jnp.concatenate([own_halo, side_halo], axis=0)], axis=1))
        return slabs

    def coefficients():
        face_x = [face_terms(mean_x[i], box_u[i + 1] - box_u[i]) for i in range(13)]
        cface = []
        for j in range(7):
            cface.append(plane_sum(face_x[2 * j][1]))
            if 1 <= j < 6:
                cwx[j - 1] = fold_rows(cface[j])
        for i in range(7):
            wx[i] = fold_rows(face_x[i + 3][1])
        for c in range(6):
            pair_y, pair_z, pair_r = None, None, None
            for half in range(2):
                i = 2 * c + half
                u = box_u[i + 1]
                re = react[i]
                flux_y, w_y = face_terms(mean_y[i], up(u, 0) - u)
                flux_z, w_z = face_terms(mean_z[i], up(u, 1) - u)
                low_y, low_z = down(w_y, 0), down(w_z, 1)
                force = (
                    src[i]
                    - re * u
                    + (face_x[i + 1][0] - face_x[i][0])
                    + (flux_y - down(flux_y, 0))
                    + (flux_z - down(flux_z, 1))
                )
                v0[i] = fold_rows(force)
                if 2 <= i < 10:
                    diagonal = re + face_x[i + 1][1] + face_x[i][1] + w_y + low_y + w_z + low_z
                    inv[i - 2] = fold_rows(1.0 / diagonal)
                if 3 <= i < 9:
                    wyu[i - 3] = fold_rows(w_y)
                    wyl[i - 3] = fold_rows(low_y)
                    wzu[i - 3] = fold_rows(w_z)
                    wzl[i - 3] = fold_rows(low_z)
                pair_y = w_y if half == 0 else pair_y + w_y
                pair_z = w_z if half == 0 else pair_z + w_z
                pair_r = re if half == 0 else pair_r + re
            odd_row = lax.rem(index_of((24, 2 * LINE), 0), 2) == 1
            odd_lane = lax.rem(index_of((24, 2 * LINE), 1), 2) == 1
            sum_y = pair_sum(jnp.where(odd_row, pair_y, up(pair_y, 0)), 1)
            sum_z = pair_sum(jnp.where(odd_lane, pair_z, up(pair_z, 1)), 0)
            low_y, low_z = pltpu.roll(sum_y, 2, 0), pltpu.roll(sum_z, 2, 1)
            diagonal = plane_sum(pair_r) + cface[c] + cface[c + 1] + sum_y + low_y + sum_z + low_z
            cinv[c] = fold_rows(1.0 / diagonal)
            if 1 <= c < 5:
                cwyu[c - 1] = fold_rows(sum_y)
                cwyl[c - 1] = fold_rows(low_y)
                cwzu[c - 1] = fold_rows(sum_z)
                cwzl[c - 1] = fold_rows(low_z)

    def precondition(v, j):
        own = [inv[i] * v[i + 2] for i in range(8)]
        coarse = [cinv[c] * plane_sum(v[2 * c] + v[2 * c + 1]) for c in range(6)]
        coarse_z = []
        for c in range(4):
            q = coarse[c + 1]
            near = (
                cwx[c] * coarse[c]
                + cwx[c + 1] * coarse[c + 2]
                + cwyu[c] * pltpu.roll(q, 14, 0)
                + cwyl[c] * pltpu.roll(q, 2, 0)
                + cwzu[c] * pltpu.roll(q, 2 * LINE - 2, 1)
                + cwzl[c] * pltpu.roll(q, 2, 1)
            )
            coarse_z.append(COARSE_OWN * q + COARSE_NEAR * (cinv[c + 1] * near))
        for i in range(6):
            q = own[i + 1]
            near = (
                wx[i] * own[i]
                + wx[i + 1] * own[i + 2]
                + wyu[i] * up(q, 0)
                + wyl[i] * down(q, 0)
                + wzu[i] * up(q, 1)
                + wzl[i] * down(q, 1)
            )
            zs[j, i] = FINE_OWN * q + FINE_NEAR * (inv[i + 1] * near) + coarse_z[(i + 1) // 2]

    def image(j, s):
        i = s + 1
        mid = zs[j, i]
        here = mid[0:8, 0:LINE]
        tall, wide = mid[:, 0:LINE], mid[0:8, :]
        own = (slice(0, 8), slice(0, LINE))
        total = react[i + 3, 8:16, 0:LINE] * here
        for weight, other in (
            (wx[(i,) + own], zs[(j, i - 1) + own]),
            (wx[(i + 1,) + own], zs[(j, i + 1) + own]),
            (wyu[(i,) + own], up(tall, 0)[0:8]),
            (wyl[(i,) + own], down(tall, 0)[0:8]),
            (wzu[(i,) + own], up(wide, 1)[:, 0:LINE]),
            (wzl[(i,) + own], down(wide, 1)[:, 0:LINE]),
        ):
            total = total + weight * (here - other)
        return total

    def global_sum(rows, which, between):
        group = index_of((1, LINE), 1) // 16
        mixed = jnp.zeros((1, LINE), jnp.float32)
        for n, row in enumerate(rows):
            row = jnp.sum(row, axis=0, keepdims=True)
            for shift in (64, 32, 16):
                row = row + pltpu.roll(row, shift, 1)
            mixed = jnp.where(group == n, row, mixed)
        phases = ((core_line, got1), (plane_line, got2), (long_line, got3))
        for phase, (partners, got) in enumerate(phases):
            sums[which, phase] = mixed
            slot = 6 + 3 * which + phase
            for n, partner in enumerate(partners):
                send(sums.at[which, phase], got.at[which, n], slot, partner)
            if phase == 0:
                between()
            if phase == 1 and which == 0:
                pl.semaphore_wait(far_sem, 2)
            part = got.at[which]
            pltpu.make_async_copy(part, part, recv_sem.at[slot]).wait()
            mixed = mixed + jnp.sum(got[which], axis=0)
        return [jnp.sum(jnp.where(group == n, mixed, 0.0), axis=1, keepdims=True) for n in range(6)]

    def solve(m):
        h = [(m[n + 1] + SHIFT * m[n]) * (1.0 / SCALE) for n in range(5)]

        def inverse(pivot, of):
            good = pivot > 1e-6 * of
            return jnp.where(good, 1.0 / jnp.where(good, pivot, 1.0), 0.0)

        i0 = inverse(h[0], jnp.zeros_like(h[0]))
        l1, l2 = h[1] * i0, h[2] * i0
        i1 = inverse(h[2] - l1 * h[1], h[2])
        h21 = h[3] - l2 * h[1]
        l21 = h21 * i1
        i2 = inverse(h[4] - l2 * h[2] - l21 * h21, h[4])
        y0 = m[0]
        y1 = m[1] - l1 * y0
        y2 = m[2] - l2 * y0 - l21 * y1
        c2 = y2 * i2
        c1 = y1 * i1 - l21 * c2
        c0 = y0 * i0 - l1 * c1 - l2 * c2
        return c0, c1, c2

    def total_of(tiles, others):
        total = tiles[0] * others[0]
        for s in range(1, 4):
            total = total + tiles[s] * others[s]
        return total

    given = []

    def give(sources, targets, slot, tiles):
        @pl.when(alone)
        def _():
            for source, target in zip(sources, targets):
                pltpu.make_async_copy(source, target, recv_sem.at[slot]).start()

        @pl.when(jnp.logical_not(alone))
        def _():
            for source, target in zip(sources, targets):
                pltpu.make_async_remote_copy(
                    source, target, send_sem.at[1], recv_sem.at[slot], device_id=partner, device_id_type=MESH
                ).start()

        given.append(tiles)

    pl.semaphore_wait(barrier, len(partners) + 1 - alone.astype(jnp.int32))
    give([u_ref, k_ref, r_ref, s_ref], [raw0.at[f, pl.ds(5, 4), pl.ds(8, 8)] for f in range(4)], 12, 16)
    last_r = pltpu.make_async_copy(r_ref, end_rs.at[0], send_sem.at[2])
    last_s = pltpu.make_async_copy(s_ref, end_rs.at[1], send_sem.at[3])
    last_r.start()
    last_s.start()
    receive(16, 12)
    pack_z([raw0[f, 5 + s, 8:16] for f in range(4) for s in range(4)], 0)
    count = exchange_wide(raw0, zed0, 0, 4, 2, 0)
    receive(count, 0)
    for other in far_ones:
        pl.semaphore_signal(far_sem, inc=1, device_id=other, device_id_type=MESH)
    for i in range(14):
        box_u[i] = wide_slab(raw0, zed0, 0, i)
    k_slabs = [wide_slab(raw0, zed0, 1, i) for i in range(14)]
    for i in range(13):
        mean_x[i] = mean_of(k_slabs[i], k_slabs[i + 1])
    for i in range(12):
        k = k_slabs[i + 1]
        mean_y[i] = mean_of(k, up(k, 0))
        mean_z[i] = mean_of(k, up(k, 1))
        react[i] = wide_slab(raw0, zed0, 2, i + 1)
        src[i] = wide_slab(raw0, zed0, 3, i + 1)

    own = (slice(0, 8), slice(0, LINE))

    def give_fields(first, count):
        which = pl.ds(first, count)
        middle, eight, lanes = pl.ds(1, 4), pl.ds(0, 8), pl.ds(0, LINE)
        regions = [
            (which, pl.ds(0, 6), eight, lanes),
            (which, middle, pl.ds(8, 8), lanes),
            (which, middle, eight, pl.ds(LINE, LINE)),
        ]
        give([zs.at[r] for r in regions], [end_zs.at[r] for r in regions], 13, 14 * count)

    def beside_v(newton, j):
        if newton == 0 and j == 0:
            four, lanes = pl.ds(4, 4), pl.ds(0, LINE)
            give(
                [
                    mean_x.at[pl.ds(4, 5), pl.ds(8, 8), lanes],
                    mean_y.at[four, pl.ds(0, 16), lanes],
                    mean_z.at[four, pl.ds(8, 8)],
                ],
                [end_x, end_y, end_z],
                13,
                5 + 8 + 8,
            )
        elif newton == 1 and j == 0:
            give_fields(3, 1)
        elif newton == 1:
            give_fields(4, 2)

    for newton in range(NEWTON):
        coefficients()
        rows = []
        v = [v0[i] for i in range(12)]
        tiles = [slab[0:8, 0:LINE] for slab in v[4:8]]
        for j in range(KRYLOV):
            at = 4 * newton + j
            precondition(v, at)
            z_tiles = [zs[(at, s + 1) + own] for s in range(4)]
            rows.append(total_of(tiles, z_tiles))
            if newton + 1 < NEWTON:
                for s in range(4):
                    raw_h[j, 5 + s, 8:16] = z_tiles[s]
            tiles = [SCALE * image(at, s) - SHIFT * tiles[s] for s in range(4)]
            rows.append(total_of(tiles, z_tiles))
            if j + 1 < KRYLOV:
                v = exchange_v(tiles, 2 * newton + j, functools.partial(beside_v, newton, j))

        def beside(newton=newton):
            if newton + 1 < NEWTON:
                pack_z([raw_h[f, 5 + s, 8:16] for f in range(3) for s in range(4)], 1)
                exchange_wide(raw_h, zed_h, 1, 3, 3, 1)
            else:
                give_fields(6, 1)

        c = solve(global_sum(rows, newton, beside))
        if newton + 1 < NEWTON:
            receive(32 * 3 + 18 + 6, 1)
            for i in range(14):
                total = box_u[i]
                for j in range(3):
                    total = total + c[j] * wide_slab(raw_h, zed_h, j, i)
                box_u[i] = total
                if 4 <= i < 10:
                    zs[3, i - 4] = fold_rows(total)

    last_r.wait()
    last_s.wait()
    receive(21 + 14 + 28 + 14, 13)
    last = []
    for i in range(6):
        total = end_zs[3, i]
        for j in range(3):
            total = total + c[j] * end_zs[4 + j, i]
        last.append(total)
    low_flux = None
    for s in range(-1, 4):
        lower, upper = last[s + 1][own], last[s + 2][own]
        flux, _ = face_terms(end_x[s + 1], upper - lower)
        if s >= 0:
            mid = last[s + 1]
            tall = mid[:, 0:LINE]
            wide = mid[0:8, :]
            ends[0, s] = lower
            near_k = jnp.concatenate([end_y[s, 8:16], end_y[s, 0:8]], axis=0)
            flux_y, _ = face_terms(near_k, up(tall, 0) - tall)
            flux_z, _ = face_terms(end_z[s], up(wide, 1) - wide)
            ends[1, s] = (
                end_rs[0, s] * lower
                - (flux - low_flux)
                - (flux_y - down(flux_y, 0))[0:8]
                - (flux_z - down(flux_z, 1))[:, 0:LINE]
                - end_rs[1, s]
            )
        low_flux = flux
    store_u = pltpu.make_async_copy(ends.at[0], out_u, send_sem.at[2])
    store_f = pltpu.make_async_copy(ends.at[1], out_f, send_sem.at[3])
    store_u.start()
    store_f.start()
    for copy in copies:
        copy.wait_send()

    @pl.when(jnp.logical_not(alone))
    def _():
        part = dummy.at[pl.ds(0, sum(given))]
        pltpu.make_async_copy(part, part, send_sem.at[1]).wait()

    store_u.wait()
    store_f.wait()


def local(sizes, state, conductivity, reaction, source):
    nx, ny, nz = sizes
    plane, line = 4 * (nz // 2), (nx // 4) * ny

    def vmem(*shape):
        return pltpu.VMEM(shape, jnp.float32)

    full, half = (24, 2 * LINE), (16, 2 * LINE)
    tile = (ROWS, LINE)
    scratch = [
        vmem(4, 14, 24, LINE), vmem(3, 3, 2, *tile), vmem(3, 14, 24, LINE), vmem(3, 3, 2, *tile),
        vmem(4, 12, 24, LINE), vmem(4, 3, 3, 2, *tile), vmem(6, 2, *tile), vmem(14, *full),
        vmem(13, *full), vmem(12, *full), vmem(12, *full), vmem(12, *full), vmem(12, *full),
        vmem(12, *half), vmem(8, *half), vmem(7, *half), vmem(6, *half), vmem(6, *half), vmem(6, *half), vmem(6, *half),
        vmem(6, *half), vmem(5, *half), vmem(4, *half), vmem(4, *half), vmem(4, *half), vmem(4, *half),
        vmem(7, 6, *half), vmem(2, 3, 1, LINE), vmem(2, 1, 1, LINE), vmem(2, plane - 1, 1, LINE), vmem(2, line - 1, 1, LINE),
        vmem(2, 4, *tile), vmem(160, *tile),
        vmem(7, 6, *half), vmem(5, *tile), vmem(4, 16, LINE), vmem(4, ROWS, 2 * LINE), vmem(2, 4, *tile),
        pltpu.SemaphoreType.DMA((4,)), pltpu.SemaphoreType.DMA((14,)), pltpu.SemaphoreType.REGULAR,
    ]
    spec = pl.BlockSpec(memory_space=pl.ANY)
    return pl.pallas_call(
        functools.partial(kernel, sizes),
        out_shape=[jax.ShapeDtypeStruct(state.shape, jnp.float32)] * 2,
        in_specs=[spec] * 4,
        out_specs=[spec] * 2,
        scratch_shapes=scratch,
        compiler_params=pltpu.CompilerParams(
            collective_id=0, has_side_effects=True, vmem_limit_bytes=32 * 1024 * 1024
        ),
    )(state, conductivity, reaction, source)


def solution(mesh):
    sizes = tuple(mesh.shape[name] for name in ("gx", "gy", "gz"))
    placed = P("gx", "gy", "gz")
    return jax.shard_map(
        functools.partial(local, sizes),
        mesh=mesh,
        in_specs=(placed,) * 4,
        out_specs=(placed, placed),
        check_vma=False,
    )
```

```python
import functools

import jax
import jax.numpy as jnp
from jax import lax
from jax.experimental import pallas as pl
from jax.experimental.pallas import tpu as pltpu
from jax.sharding import PartitionSpec as P

NEWTON = 2
KRYLOV = 3
EPS_SQUARE = 0.25
SCALE, SHIFT = 0.7, 1.0
MESH = pl.DeviceIdType.MESH

LINE = 128
ROWS = 8


def chebyshev_pair(low):
    centre = (2.0 + low) / 2.0
    half_width = (2.0 - low) / 2.0
    sigma = centre / half_width
    rho = 1.0 / sigma
    rho_new = 1.0 / (2.0 * sigma - rho)
    last = 2.0 * rho_new / half_width
    return (1.0 + rho_new * rho) / centre + last * (1.0 - 1.0 / centre), last / centre


FINE_OWN, FINE_NEAR = chebyshev_pair(0.3)
COARSE_OWN, COARSE_NEAR = chebyshev_pair(0.05)

CROSS = [(0, 0), (1, 0), (-1, 0), (0, 1), (0, -1)]
CORNERS = [(1, 1), (1, -1), (-1, 1), (-1, -1)]


def up(field, axis):
    return pltpu.roll(field, field.shape[axis] - 1, axis)


def down(field, axis):
    return pltpu.roll(field, 1, axis)


def index_of(shape, axis):
    return lax.broadcasted_iota(jnp.int32, shape, axis)


def face_terms(mean_k, difference):
    square = difference * difference
    inverse_root = lax.rsqrt(EPS_SQUARE + square)
    root = (EPS_SQUARE + square) * inverse_root
    return mean_k * root * difference, mean_k * (EPS_SQUARE + 2.0 * square) * inverse_root


def mean_of(one, other):
    return 2.0 * one * other / (one + other)


def fold_rows(field):
    row = index_of((ROWS, field.shape[1]), 0)
    return jnp.concatenate([field[8:16], jnp.where(row < 4, field[16:24], field[0:8])], axis=0)


def pair_sum(field, axis):
    odd = lax.rem(index_of(field.shape, axis), 2) == 1
    return field + jnp.where(odd, down(field, axis), up(field, axis))


def plane_sum(field):
    return pair_sum(pair_sum(field, 0), 1)


def kernel(
    sizes, u_ref, k_ref, r_ref, s_ref, out_u, out_f,
    raw0, zed0, raw_h, zed_h, raw_e, zed_e, pack, box_u, mean_x, mean_y, mean_z, react, src,
    v0, inv, wx, wyu, wyl, wzu, wzl, cinv, cwx, cwyu, cwyl, cwzu, cwzl, zs, sums, got1, got2, got3, ends, dummy,
    end_zs, end_pack, end_halo, end_x, end_y, end_z, end_rs, send_sem, recv_sem, far_sem,
):
    nx, ny, nz = sizes
    mx, my, mz = lax.axis_index("gx"), lax.axis_index("gy"), lax.axis_index("gz")

    group, place_y = mx // 4, lax.rem(mx, 4)
    bx, by = group * 4 + my, place_y
    partner = (group * 4 + my, place_y, mz)
    alone = my == place_y

    def block_at(dx, dy, dz):
        x, y = lax.rem(bx + dx + nx, nx), lax.rem(by + dy + ny, ny)
        return ((x // 4) * 4 + y, lax.rem(x, 4), lax.rem(mz + dz + nz, nz))

    core_line = [(mx, my, (mz // 2) * 2 + 1 - lax.rem(mz, 2))]
    plane = 4 * (nz // 2)
    here = lax.rem(mx, 4) * (nz // 2) + mz // 2
    plane_line = []
    for step in range(1, plane):
        there = lax.rem(here + step, plane)
        plane_line.append(
            ((mx // 4) * 4 + there // (nz // 2), my, lax.rem(there, nz // 2) * 2 + lax.rem(mz, 2))
        )
    line = (nx // 4) * ny
    at = (mx // 4) * ny + my
    long_line = []
    for step in range(1, line):
        there = lax.rem(at + step, line)
        long_line.append(((there // ny) * 4 + lax.rem(mx, 4), lax.rem(there, ny), mz))

    offsets = [(dx, dy, dz) for dx in (-1, 0, 1) for dy in (-1, 0, 1) for dz in (-1, 0, 1)]
    offsets = [d for d in offsets if d != (0, 0, 0)] + [(2, 0, 0), (-2, 0, 0)]

    barrier = pltpu.get_barrier_semaphore()
    partners = [block_at(*d) for d in offsets]
    far_ones = [(lax.rem(mx + 4, nx), my, mz), (lax.rem(mx + nx - 4, nx), my, mz)]

    @pl.when(jnp.logical_not(alone))
    def _():
        pl.semaphore_signal(barrier, inc=1, device_id=partner, device_id_type=MESH)

    for other in partners:
        pl.semaphore_signal(barrier, inc=1, device_id=other, device_id_type=MESH)

    lane = index_of((ROWS, LINE), 1)
    copies = []

    def send(source, target, slot, device):
        copy = pltpu.make_async_remote_copy(
            source, target, send_sem.at[0], recv_sem.at[slot], device_id=device, device_id_type=MESH
        )
        copy.start()
        copies.append(copy)

    def receive(tiles, slot):
        part = dummy.at[pl.ds(0, tiles)]
        pltpu.make_async_copy(part, part, recv_sem.at[slot]).wait()

    def pack_z(tiles, place):
        low = jnp.zeros((ROWS, LINE), jnp.float32)
        high = low
        for g, tile in enumerate(tiles):
            mine = lane // 8 == g
            low = jnp.where(mine, tile if g == 0 else pltpu.roll(tile, 8 * g, 1), low)
            shift = (8 * g + 8) % LINE
            high = jnp.where(mine, pltpu.roll(tile, shift, 1) if shift else tile, high)
        pack[place, 0] = low
        pack[place, 1] = high

    def unpack_z(low_tile, high_tile, g):
        shift = (LINE - 8 * g) % LINE
        above = pltpu.roll(low_tile, shift, 1) if shift else low_tile
        shift = (LINE - 8 - 8 * g) % LINE
        below = pltpu.roll(high_tile, shift, 1) if shift else high_tile
        return jnp.where(lane < 64, above, below)

    def exchange_wide(raw, zed, place, fields, far, slot):
        everything = pl.ds(0, fields)
        own = (everything, pl.ds(5, 4), pl.ds(8, 8))
        for dx, dy in CORNERS:
            target = (everything, pl.ds(5 - 4 * dx, 4), pl.ds(8 - 8 * dy, 8))
            send(raw.at[own], raw.at[target], slot, block_at(dx, dy, 0))
        for dx, dy in CORNERS + CROSS:
            for dz in (1, -1):
                send(
                    pack.at[place, (1 + dz) // 2],
                    zed.at[1 - dx, 1 - dy, (1 - dz) // 2],
                    slot,
                    block_at(dx, dy, dz),
                )
        some = pl.ds(0, far)
        rows = pl.ds(8, 8)
        send(raw.at[some, pl.ds(8, 1), rows], raw.at[some, pl.ds(0, 1), rows], slot, block_at(2, 0, 0))
        send(raw.at[some, pl.ds(5, 1), rows], raw.at[some, pl.ds(13, 1), rows], slot, block_at(-2, 0, 0))
        for dx, dy in CROSS[1:]:
            target = (everything, pl.ds(5 - 4 * dx, 4), pl.ds(8 - 8 * dy, 8))
            send(raw.at[own], raw.at[target], slot, block_at(dx, dy, 0))
        return 16 * fields + 18 + 2 * far + 16 * fields

    def wide_slab(raw, zed, field, i):
        if i in (0, 13):
            nothing = jnp.zeros((ROWS, LINE), jnp.float32)
            main = jnp.concatenate([nothing, raw[field, i, 8:16], nothing], axis=0)
            return jnp.concatenate([main, jnp.zeros_like(main)], axis=1)
        main = raw[field, i]
        column, s = divmod(i - 1, 4)
        g = field * 4 + s
        halo = [unpack_z(zed[column, y, 1], zed[column, y, 0], g) for y in range(3)]
        return jnp.concatenate([main, jnp.concatenate(halo, axis=0)], axis=1)

    def exchange_v(tiles, e, between):
        place, slot = 2 + e, 2 + e
        for s in range(4):
            raw_e[e, 4 + s, 8:16] = tiles[s]
        pack_z(tiles, place)
        raw, zed = raw_e.at[e], zed_e.at[e]
        rows = pl.ds(8, 8)
        for dx, dy in CORNERS:
            source = (pl.ds(6 if dx > 0 else 4, 2), rows)
            target = (pl.ds(2 if dx > 0 else 8, 2), pl.ds(8 - 8 * dy, 8))
            send(raw.at[source], raw.at[target], slot, block_at(dx, dy, 0))
        for dx, dy in CROSS:
            for dz in (1, -1):
                send(
                    pack.at[place, (1 + dz) // 2],
                    zed.at[1 - dx, 1 - dy, (1 - dz) // 2],
                    slot,
                    block_at(dx, dy, dz),
                )
        for dx, dy in CROSS[1:]:
            target = (pl.ds(4 - 4 * dx, 4), pl.ds(8 - 8 * dy, 8))
            send(raw.at[pl.ds(4, 4), rows], raw.at[target], slot, block_at(dx, dy, 0))
        between()
        receive(8 + 10 + 16, slot)
        slabs = []
        nothing = jnp.zeros((ROWS, LINE), jnp.float32)
        row = index_of((ROWS, LINE), 0)
        for i in range(12):
            if 2 <= i < 10:
                main = fold_rows(raw_e[e, i])
            else:
                main = jnp.concatenate([raw_e[e, i, 8:16], nothing], axis=0)
            column, s = divmod(i, 4)
            own_halo, side_halo = nothing, nothing
            if 2 <= i < 10:
                own_halo = unpack_z(zed_e[e, column, 1, 1], zed_e[e, column, 1, 0], s)
            if 4 <= i < 8:
                side_halo = jnp.where(
                    row < 4,
                    unpack_z(zed_e[e, 1, 2, 1], zed_e[e, 1, 2, 0], s),
                    unpack_z(zed_e[e, 1, 0, 1], zed_e[e, 1, 0, 0], s),
                )
            slabs.append(jnp.concatenate([main, jnp.concatenate([own_halo, side_halo], axis=0)], axis=1))
        return slabs

    def coefficients():
        face_x = [face_terms(mean_x[i], box_u[i + 1] - box_u[i]) for i in range(13)]
        cface = []
        for j in range(7):
            cface.append(plane_sum(face_x[2 * j][1]))
            if 1 <= j < 6:
                cwx[j - 1] = fold_rows(cface[j])
        for i in range(7):
            wx[i] = fold_rows(face_x[i + 3][1])
        for c in range(6):
            pair_y, pair_z, pair_r = None, None, None
            for half in range(2):
                i = 2 * c + half
                u = box_u[i + 1]
                re = react[i]
                flux_y, w_y = face_terms(mean_y[i], up(u, 0) - u)
                flux_z, w_z = face_terms(mean_z[i], up(u, 1) - u)
                low_y, low_z = down(w_y, 0), down(w_z, 1)
                force = (
                    src[i]
                    - re * u
                    + (face_x[i + 1][0] - face_x[i][0])
                    + (flux_y - down(flux_y, 0))
                    + (flux_z - down(flux_z, 1))
                )
                v0[i] = fold_rows(force)
                if 2 <= i < 10:
                    diagonal = re + face_x[i + 1][1] + face_x[i][1] + w_y + low_y + w_z + low_z
                    inv[i - 2] = fold_rows(1.0 / diagonal)
                if 3 <= i < 9:
                    wyu[i - 3] = fold_rows(w_y)
                    wyl[i - 3] = fold_rows(low_y)
                    wzu[i - 3] = fold_rows(w_z)
                    wzl[i - 3] = fold_rows(low_z)
                pair_y = w_y if half == 0 else pair_y + w_y
                pair_z = w_z if half == 0 else pair_z + w_z
                pair_r = re if half == 0 else pair_r + re
            odd_row = lax.rem(index_of((24, 2 * LINE), 0), 2) == 1
            odd_lane = lax.rem(index_of((24, 2 * LINE), 1), 2) == 1
            sum_y = pair_sum(jnp.where(odd_row, pair_y, up(pair_y, 0)), 1)
            sum_z = pair_sum(jnp.where(odd_lane, pair_z, up(pair_z, 1)), 0)
            low_y, low_z = pltpu.roll(sum_y, 2, 0), pltpu.roll(sum_z, 2, 1)
            diagonal = plane_sum(pair_r) + cface[c] + cface[c + 1] + sum_y + low_y + sum_z + low_z
            cinv[c] = fold_rows(1.0 / diagonal)
            if 1 <= c < 5:
                cwyu[c - 1] = fold_rows(sum_y)
                cwyl[c - 1] = fold_rows(low_y)
                cwzu[c - 1] = fold_rows(sum_z)
                cwzl[c - 1] = fold_rows(low_z)

    def precondition(v, j):
        own = [inv[i] * v[i + 2] for i in range(8)]
        coarse = [cinv[c] * plane_sum(v[2 * c] + v[2 * c + 1]) for c in range(6)]
        coarse_z = []
        for c in range(4):
            q = coarse[c + 1]
            near = (
                cwx[c] * coarse[c]
                + cwx[c + 1] * coarse[c + 2]
                + cwyu[c] * pltpu.roll(q, 14, 0)
                + cwyl[c] * pltpu.roll(q, 2, 0)
                + cwzu[c] * pltpu.roll(q, 2 * LINE - 2, 1)
                + cwzl[c] * pltpu.roll(q, 2, 1)
            )
            coarse_z.append(COARSE_OWN * q + COARSE_NEAR * (cinv[c + 1] * near))
        for i in range(6):
            q = own[i + 1]
            near = (
                wx[i] * own[i]
                + wx[i + 1] * own[i + 2]
                + wyu[i] * up(q, 0)
                + wyl[i] * down(q, 0)
                + wzu[i] * up(q, 1)
                + wzl[i] * down(q, 1)
            )
            zs[j, i] = FINE_OWN * q + FINE_NEAR * (inv[i + 1] * near) + coarse_z[(i + 1) // 2]

    def image(j, s):
        i = s + 1
        mid = zs[j, i]
        here = mid[0:8, 0:LINE]
        tall, wide = mid[:, 0:LINE], mid[0:8, :]
        own = (slice(0, 8), slice(0, LINE))
        total = react[i + 3, 8:16, 0:LINE] * here
        for weight, other in (
            (wx[(i,) + own], zs[(j, i - 1) + own]),
            (wx[(i + 1,) + own], zs[(j, i + 1) + own]),
            (wyu[(i,) + own], up(tall, 0)[0:8]),
            (wyl[(i,) + own], down(tall, 0)[0:8]),
            (wzu[(i,) + own], up(wide, 1)[:, 0:LINE]),
            (wzl[(i,) + own], down(wide, 1)[:, 0:LINE]),
        ):
            total = total + weight * (here - other)
        return total

    def global_sum(rows, which, between):
        group = index_of((1, LINE), 1) // 16
        mixed = jnp.zeros((1, LINE), jnp.float32)
        for n, row in enumerate(rows):
            row = jnp.sum(row, axis=0, keepdims=True)
            for shift in (64, 32, 16):
                row = row + pltpu.roll(row, shift, 1)
            mixed = jnp.where(group == n, row, mixed)
        phases = ((core_line, got1), (plane_line, got2), (long_line, got3))
        for phase, (partners, got) in enumerate(phases):
            sums[which, phase] = mixed
            slot = 6 + 3 * which + phase
            for n, partner in enumerate(partners):
                send(sums.at[which, phase], got.at[which, n], slot, partner)
            if phase == 0:
                between()
            if phase == 1 and which == 0:
                pl.semaphore_wait(far_sem, 2)
            part = got.at[which]
            pltpu.make_async_copy(part, part, recv_sem.at[slot]).wait()
            mixed = mixed + jnp.sum(got[which], axis=0)
        return [jnp.sum(jnp.where(group == n, mixed, 0.0), axis=1, keepdims=True) for n in range(6)]

    def solve(m):
        h = [(m[n + 1] + SHIFT * m[n]) * (1.0 / SCALE) for n in range(5)]

        def inverse(pivot, of):
            good = pivot > 1e-6 * of
            return jnp.where(good, 1.0 / jnp.where(good, pivot, 1.0), 0.0)

        i0 = inverse(h[0], jnp.zeros_like(h[0]))
        l1, l2 = h[1] * i0, h[2] * i0
        i1 = inverse(h[2] - l1 * h[1], h[2])
        h21 = h[3] - l2 * h[1]
        l21 = h21 * i1
        i2 = inverse(h[4] - l2 * h[2] - l21 * h21, h[4])
        y0 = m[0]
        y1 = m[1] - l1 * y0
        y2 = m[2] - l2 * y0 - l21 * y1
        c2 = y2 * i2
        c1 = y1 * i1 - l21 * c2
        c0 = y0 * i0 - l1 * c1 - l2 * c2
        return c0, c1, c2

    def total_of(tiles, others):
        total = tiles[0] * others[0]
        for s in range(1, 4):
            total = total + tiles[s] * others[s]
        return total

    given = []

    def give(sources, targets, slot, tiles):
        @pl.when(alone)
        def _():
            for source, target in zip(sources, targets):
                pltpu.make_async_copy(source, target, recv_sem.at[slot]).start()

        @pl.when(jnp.logical_not(alone))
        def _():
            for source, target in zip(sources, targets):
                pltpu.make_async_remote_copy(
                    source, target, send_sem.at[1], recv_sem.at[slot], device_id=partner, device_id_type=MESH
                ).start()

        given.append(tiles)

    pl.semaphore_wait(barrier, len(partners) + 1 - alone.astype(jnp.int32))
    give([u_ref, k_ref, r_ref, s_ref], [raw0.at[f, pl.ds(5, 4), pl.ds(8, 8)] for f in range(4)], 12, 16)
    last_r = pltpu.make_async_copy(r_ref, end_rs.at[0], send_sem.at[2])
    last_s = pltpu.make_async_copy(s_ref, end_rs.at[1], send_sem.at[3])
    last_r.start()
    last_s.start()
    receive(16, 12)
    pack_z([raw0[f, 5 + s, 8:16] for f in range(4) for s in range(4)], 0)
    count = exchange_wide(raw0, zed0, 0, 4, 2, 0)
    receive(count, 0)
    for other in far_ones:
        pl.semaphore_signal(far_sem, inc=1, device_id=other, device_id_type=MESH)
    for i in range(14):
        box_u[i] = wide_slab(raw0, zed0, 0, i)
    k_slabs = [wide_slab(raw0, zed0, 1, i) for i in range(14)]
    for i in range(13):
        mean_x[i] = mean_of(k_slabs[i], k_slabs[i + 1])
    for i in range(12):
        k = k_slabs[i + 1]
        mean_y[i] = mean_of(k, up(k, 0))
        mean_z[i] = mean_of(k, up(k, 1))
        react[i] = wide_slab(raw0, zed0, 2, i + 1)
        src[i] = wide_slab(raw0, zed0, 3, i + 1)

    own = (slice(0, 8), slice(0, LINE))

    def give_field(f, slot):
        row = index_of((ROWS, LINE), 0)
        next_rows = jnp.zeros((ROWS, LINE), jnp.float32)
        next_lanes = next_rows
        for s in range(4):
            tile = pltpu.roll(zs[f, s + 1, 8:16, 0:LINE], 2 * s + 1, 0)
            next_rows = jnp.where(row // 2 == s, tile, next_rows)
            tile = pltpu.roll(zs[f, s + 1, 0:8, LINE : 2 * LINE], 2 * s + 1, 1)
            next_lanes = jnp.where(lane // 2 == s, tile, next_lanes)
        end_pack[f - 3, 0] = next_rows
        end_pack[f - 3, 1] = next_lanes
        region = (f, pl.ds(0, 6), pl.ds(0, 8), pl.ds(0, LINE))
        give([zs.at[region], end_pack.at[f - 3]], [end_zs.at[f - 3], end_halo.at[f - 3]], slot, 8)

    def beside_v(newton, j):
        if newton == 0 and j == 0:
            for i in range(6):
                zs[7, i] = fold_rows(k_slabs[i + 4])
            give_field(7, 14)
        elif newton == 1:
            if j == 0:
                give_field(3, 13)
            give_field(4 + j, 13)

    def end_fields(slabs, halo):
        tall = [jnp.concatenate([slabs[s + 1], pltpu.roll(halo[0], 7 - 2 * s, 0)], axis=0) for s in range(4)]
        wide = [
            jnp.concatenate([slabs[s + 1], pltpu.roll(halo[1], LINE - 1 - 2 * s, 1)], axis=1) for s in range(4)
        ]
        return slabs, tall, wide

    def end_means():
        receive(8, 14)
        slabs, tall, wide = end_fields([end_zs[4, i] for i in range(6)], [end_halo[4, i] for i in range(2)])
        for i in range(5):
            end_x[i] = mean_of(slabs[i], slabs[i + 1])
        for s in range(4):
            end_y[s] = mean_of(tall[s], up(tall[s], 0))
            end_z[s] = mean_of(wide[s], up(wide[s], 1))

    for newton in range(NEWTON):
        coefficients()
        rows = []
        v = [v0[i] for i in range(12)]
        tiles = [slab[0:8, 0:LINE] for slab in v[4:8]]
        for j in range(KRYLOV):
            at = 4 * newton + j
            precondition(v, at)
            z_tiles = [zs[(at, s + 1) + own] for s in range(4)]
            rows.append(total_of(tiles, z_tiles))
            if newton + 1 < NEWTON:
                for s in range(4):
                    raw_h[j, 5 + s, 8:16] = z_tiles[s]
            tiles = [SCALE * image(at, s) - SHIFT * tiles[s] for s in range(4)]
            rows.append(total_of(tiles, z_tiles))
            if j + 1 < KRYLOV:
                v = exchange_v(tiles, 2 * newton + j, functools.partial(beside_v, newton, j))

        def beside(newton=newton):
            if newton + 1 < NEWTON:
                pack_z([raw_h[f, 5 + s, 8:16] for f in range(3) for s in range(4)], 1)
                exchange_wide(raw_h, zed_h, 1, 3, 3, 1)
            else:
                give_field(6, 13)
                end_means()

        c = solve(global_sum(rows, newton, beside))
        if newton + 1 < NEWTON:
            receive(32 * 3 + 18 + 6, 1)
            for i in range(14):
                total = box_u[i]
                for j in range(3):
                    total = total + c[j] * wide_slab(raw_h, zed_h, j, i)
                box_u[i] = total
                if 4 <= i < 10:
                    zs[3, i - 4] = fold_rows(total)

    last_r.wait()
    last_s.wait()
    receive(8 * 4, 13)
    near = []
    for tiles in ([end_zs.at[:, i] for i in range(6)], [end_halo.at[:, i] for i in range(2)]):
        for tile in tiles:
            total = tile[0]
            for j in range(3):
                total = total + c[j] * tile[1 + j]
            near.append(total)
    last, tall, wide = end_fields(near[:6], near[6:])
    low_flux = None
    for s in range(-1, 4):
        flux, _ = face_terms(end_x[s + 1], last[s + 2] - last[s + 1])
        if s >= 0:
            ends[0, s] = last[s + 1]
            flux_y, _ = face_terms(end_y[s], up(tall[s], 0) - tall[s])
            flux_z, _ = face_terms(end_z[s], up(wide[s], 1) - wide[s])
            ends[1, s] = (
                end_rs[0, s] * last[s + 1]
                - (flux - low_flux)
                - (flux_y - down(flux_y, 0))[0:8]
                - (flux_z - down(flux_z, 1))[:, 0:LINE]
                - end_rs[1, s]
            )
        low_flux = flux
    store_u = pltpu.make_async_copy(ends.at[0], out_u, send_sem.at[2])
    store_f = pltpu.make_async_copy(ends.at[1], out_f, send_sem.at[3])
    store_u.start()
    store_f.start()
    for copy in copies:
        copy.wait_send()

    @pl.when(jnp.logical_not(alone))
    def _():
        part = dummy.at[pl.ds(0, sum(given))]
        pltpu.make_async_copy(part, part, send_sem.at[1]).wait()

    store_u.wait()
    store_f.wait()


def local(sizes, state, conductivity, reaction, source):
    nx, ny, nz = sizes
    plane, line = 4 * (nz // 2), (nx // 4) * ny

    def vmem(*shape):
        return pltpu.VMEM(shape, jnp.float32)

    full, half = (24, 2 * LINE), (16, 2 * LINE)
    tile = (ROWS, LINE)
    scratch = [
        vmem(4, 14, 24, LINE), vmem(3, 3, 2, *tile), vmem(3, 14, 24, LINE), vmem(3, 3, 2, *tile),
        vmem(4, 12, 24, LINE), vmem(4, 3, 3, 2, *tile), vmem(6, 2, *tile), vmem(14, *full),
        vmem(13, *full), vmem(12, *full), vmem(12, *full), vmem(12, *full), vmem(12, *full),
        vmem(12, *half), vmem(8, *half), vmem(7, *half), vmem(6, *half), vmem(6, *half), vmem(6, *half), vmem(6, *half),
        vmem(6, *half), vmem(5, *half), vmem(4, *half), vmem(4, *half), vmem(4, *half), vmem(4, *half),
        vmem(8, 6, *half), vmem(2, 3, 1, LINE), vmem(2, 1, 1, LINE), vmem(2, plane - 1, 1, LINE), vmem(2, line - 1, 1, LINE),
        vmem(2, 4, *tile), vmem(160, *tile),
        vmem(5, 6, *tile), vmem(5, 2, *tile), vmem(5, 2, *tile), vmem(5, *tile), vmem(4, 16, LINE), vmem(4, ROWS, 2 * LINE), vmem(2, 4, *tile),
        pltpu.SemaphoreType.DMA((4,)), pltpu.SemaphoreType.DMA((15,)), pltpu.SemaphoreType.REGULAR,
    ]
    spec = pl.BlockSpec(memory_space=pltpu.MemorySpace.HBM)
    return pl.pallas_call(
        functools.partial(kernel, sizes),
        out_shape=[jax.ShapeDtypeStruct(state.shape, jnp.float32)] * 2,
        in_specs=[spec] * 4,
        out_specs=[spec] * 2,
        scratch_shapes=scratch,
        compiler_params=pltpu.CompilerParams(
            collective_id=0, has_side_effects=True, vmem_limit_bytes=61 * 1024 * 1024
        ),
    )(state, conductivity, reaction, source)


def solution(mesh):
    sizes = tuple(mesh.shape[name] for name in ("gx", "gy", "gz"))
    placed = P("gx", "gy", "gz")
    return jax.shard_map(
        functools.partial(local, sizes),
        mesh=mesh,
        in_specs=(placed,) * 4,
        out_specs=(placed, placed),
        check_vma=False,
    )
```

```python
import functools

import jax
import jax.numpy as jnp
from jax import lax
from jax.experimental import pallas as pl
from jax.experimental.pallas import tpu as pltpu
from jax.sharding import PartitionSpec as P

NEWTON = 2
KRYLOV = 3
EPS_SQUARE = 0.25
SCALE, SHIFT = 0.7, 1.0
MESH = pl.DeviceIdType.MESH

LINE = 128
ROWS = 8


def chebyshev_pair(low):
    centre = (2.0 + low) / 2.0
    half_width = (2.0 - low) / 2.0
    sigma = centre / half_width
    rho = 1.0 / sigma
    rho_new = 1.0 / (2.0 * sigma - rho)
    last = 2.0 * rho_new / half_width
    return (1.0 + rho_new * rho) / centre + last * (1.0 - 1.0 / centre), last / centre


FINE_OWN, FINE_NEAR = chebyshev_pair(0.3)
COARSE_OWN, COARSE_NEAR = chebyshev_pair(0.05)

CROSS = [(0, 0), (1, 0), (-1, 0), (0, 1), (0, -1)]
CORNERS = [(1, 1), (1, -1), (-1, 1), (-1, -1)]


def up(field, axis):
    return pltpu.roll(field, field.shape[axis] - 1, axis)


def down(field, axis):
    return pltpu.roll(field, 1, axis)


def index_of(shape, axis):
    return lax.broadcasted_iota(jnp.int32, shape, axis)


def face_terms(mean_k, difference):
    square = difference * difference
    inverse_root = lax.rsqrt(EPS_SQUARE + square)
    root = (EPS_SQUARE + square) * inverse_root
    return mean_k * root * difference, mean_k * (EPS_SQUARE + 2.0 * square) * inverse_root


def mean_of(one, other):
    return 2.0 * one * other / (one + other)


def fold_rows(field):
    row = index_of((ROWS, field.shape[1]), 0)
    return jnp.concatenate([field[8:16], jnp.where(row < 4, field[16:24], field[0:8])], axis=0)


def pair_sum(field, axis):
    odd = lax.rem(index_of(field.shape, axis), 2) == 1
    return field + jnp.where(odd, down(field, axis), up(field, axis))


def plane_sum(field):
    return pair_sum(pair_sum(field, 0), 1)


def kernel(
    sizes, u_ref, k_ref, r_ref, s_ref, out_u, out_f,
    raw0, corner0, zed0, far0, raw_h, corner_h, zed_h, far_h, v_out, v_face, v_edge, pack, corner_pack, box_u, mean_x, mean_y, mean_z, react, src,
    v0, inv, wx, wyu, wyl, wzu, wzl, cinv, cwx, cwyu, cwyl, cwzu, cwzl, zs, sums, got1, got2, got3, ends, dummy,
    end_zs, end_pack, end_halo, end_x, end_y, end_z, end_rs, send_sem, recv_sem, far_sem,
):
    nx, ny, nz = sizes
    mx, my, mz = lax.axis_index("gx"), lax.axis_index("gy"), lax.axis_index("gz")

    group, place_y = mx // 4, lax.rem(mx, 4)
    bx, by = group * 4 + my, place_y
    partner = (group * 4 + my, place_y, mz)
    alone = my == place_y

    def block_at(dx, dy, dz):
        x, y = lax.rem(bx + dx + nx, nx), lax.rem(by + dy + ny, ny)
        return ((x // 4) * 4 + y, lax.rem(x, 4), lax.rem(mz + dz + nz, nz))

    core_line = [(mx, my, (mz // 2) * 2 + 1 - lax.rem(mz, 2))]
    plane = 4 * (nz // 2)
    here = lax.rem(mx, 4) * (nz // 2) + mz // 2
    plane_line = []
    for step in range(1, plane):
        there = lax.rem(here + step, plane)
        plane_line.append(
            ((mx // 4) * 4 + there // (nz // 2), my, lax.rem(there, nz // 2) * 2 + lax.rem(mz, 2))
        )
    line = (nx // 4) * ny
    at = (mx // 4) * ny + my
    long_line = []
    for step in range(1, line):
        there = lax.rem(at + step, line)
        long_line.append(((there // ny) * 4 + lax.rem(mx, 4), lax.rem(there, ny), mz))

    offsets = [(dx, dy, dz) for dx in (-1, 0, 1) for dy in (-1, 0, 1) for dz in (-1, 0, 1)]
    offsets = [d for d in offsets if d != (0, 0, 0)]
    offsets += [(dx, 0, dz) for dx in (2, -2) for dz in (-1, 0, 1)]

    barrier = pltpu.get_barrier_semaphore()
    partners = [block_at(*d) for d in offsets]
    far_ones = [(lax.rem(mx + step, nx), my, mz) for step in (4, nx - 4)]
    far_ones += [(mx, my, lax.rem(mz + step, nz)) for step in (2, nz - 2)]

    @pl.when(jnp.logical_not(alone))
    def _():
        pl.semaphore_signal(barrier, inc=1, device_id=partner, device_id_type=MESH)

    for other in partners:
        pl.semaphore_signal(barrier, inc=1, device_id=other, device_id_type=MESH)

    lane = index_of((ROWS, LINE), 1)
    copies = []

    def send(source, target, slot, device):
        copy = pltpu.make_async_remote_copy(
            source, target, send_sem.at[0], recv_sem.at[slot], device_id=device, device_id_type=MESH
        )
        copy.start()
        copies.append(copy)

    def receive(tiles, slot):
        part = dummy.at[pl.ds(0, tiles)]
        pltpu.make_async_copy(part, part, recv_sem.at[slot]).wait()

    def pack_z(tiles, place):
        for t in range(0, len(tiles), 8):
            low = jnp.zeros((ROWS, LINE), jnp.float32)
            high = low
            for g, tile in enumerate(tiles[t : t + 8]):
                mine = lane // 16 == g
                low = jnp.where(mine, tile if g == 0 else pltpu.roll(tile, 16 * g, 1), low)
                shift = (16 * g + 16) % LINE
                high = jnp.where(mine, pltpu.roll(tile, shift, 1) if shift else tile, high)
            pack[place, 0, t // 8] = low
            pack[place, 1, t // 8] = high

    def unpack_z(low_tiles, high_tiles, g):
        t, g = divmod(g, 8)
        shift = (LINE - 16 * g) % LINE
        above = pltpu.roll(low_tiles[t], shift, 1) if shift else low_tiles[t]
        shift = (LINE - 16 - 16 * g) % LINE
        below = pltpu.roll(high_tiles[t], shift, 1) if shift else high_tiles[t]
        return jnp.where(lane < 64, above, below)

    def pack_corners(raw, place, fields):
        low_rows = index_of((ROWS, LINE), 0) < 4
        for f in range(fields):
            for pair in range(2):
                one, two = raw[f, 5 + 2 * pair, 8:16], raw[f, 6 + 2 * pair, 8:16]
                two = pltpu.roll(two, 4, 0)
                corner_pack[place, 1, f, pair] = jnp.where(low_rows, two, one)
                corner_pack[place, 0, f, pair] = jnp.where(low_rows, one, two)

    def exchange_wide(raw, corner, zed, zed2, place, fields, far, slot):
        everything = pl.ds(0, fields)
        own = (everything, pl.ds(5, 4), pl.ds(8, 8))
        rows = pl.ds(8, 8)
        far_tiles = pl.ds(0, (far + 1) // 2)
        for dx in (2, -2):
            for dz in (1, -1):
                send(
                    pack.at[place, (1 + dz) // 2, far_tiles],
                    zed2.at[(2 - dx) // 4, (1 - dz) // 2, far_tiles],
                    slot,
                    block_at(dx, 0, dz),
                )
        for dx, dy in CORNERS + CROSS:
            for dz in (1, -1):
                send(
                    pack.at[place, (1 + dz) // 2],
                    zed.at[1 - dx, 1 - dy, (1 - dz) // 2],
                    slot,
                    block_at(dx, dy, dz),
                )
        for dx, dy in CORNERS:
            send(
                corner_pack.at[place, (1 + dy) // 2, everything],
                corner.at[(1 - dx) // 2, (1 - dy) // 2, everything],
                slot,
                block_at(dx, dy, 0),
            )
        some = pl.ds(0, far)
        send(raw.at[some, pl.ds(8, 1), rows], raw.at[some, pl.ds(0, 1), rows], slot, block_at(2, 0, 0))
        send(raw.at[some, pl.ds(5, 1), rows], raw.at[some, pl.ds(13, 1), rows], slot, block_at(-2, 0, 0))
        for dx, dy in CROSS[1:]:
            target = (everything, pl.ds(5 - 4 * dx, 4), pl.ds(8 - 8 * dy, 8))
            send(raw.at[own], raw.at[target], slot, block_at(dx, dy, 0))
        return wide_tiles(fields, far)

    def wide_tiles(fields, far):
        return 4 * ((far + 1) // 2) + 36 + 8 * fields + 2 * far + 16 * fields

    nothing = jnp.zeros((ROWS, LINE), jnp.float32)

    def wide_slab(raw, corner, zed, zed2, field, i):
        if i in (0, 13):
            side, s = (0, 3) if i == 0 else (1, 0)
            halo = unpack_z(zed2[side, 1], zed2[side, 0], field * 4 + s)
            mid = jnp.concatenate([raw[field, i, 8:16], halo], axis=1)
            empty = jnp.zeros_like(mid)
            return jnp.concatenate([empty, mid, empty], axis=0)
        column, s = divmod(i - 1, 4)
        if column == 1:
            main = raw[field, i]
        else:
            ends_y = []
            for y in range(2):
                packed = corner[column // 2, y, field, s // 2]
                ends_y.append(pltpu.roll(packed, 4, 0) if s % 2 else packed)
            main = jnp.concatenate([ends_y[0], raw[field, i, 8:16], ends_y[1]], axis=0)
        g = field * 4 + s
        halo = [unpack_z(zed[column, y, 1], zed[column, y, 0], g) for y in range(3)]
        return jnp.concatenate([main, jnp.concatenate(halo, axis=0)], axis=1)

    def exchange_v(tiles, e, between):
        slot = 2 + e
        packed = nothing
        for s in range(4):
            v_out[e, 1 + s] = tiles[s][:, 0:LINE]
            part = pltpu.roll(tiles[s][:, LINE : 2 * LINE], 16 * s + 8, 1)
            packed = jnp.where(lane // 16 == s, part, packed)
        v_out[e, 0] = packed
        v_out[e, 5] = packed
        for dx, dy in CORNERS:
            send(
                v_out.at[e, pl.ds(3 if dx > 0 else 0, 3)],
                v_edge.at[e, (1 - dx) // 2, (1 - dy) // 2],
                slot,
                block_at(dx, dy, 0),
            )
        for n, (dx, dy) in enumerate(CROSS[1:]):
            send(v_out.at[e, pl.ds(1, 5)], v_face.at[e, n], slot, block_at(dx, dy, 0))
        between()
        receive(12 + 20, slot)
        row = index_of((ROWS, LINE), 0)

        def spread(zeds, s):
            return pltpu.roll(zeds, LINE - 8 - 16 * s, 1)

        slabs = []
        for i in range(12):
            column, s = divmod(i, 4)
            if column == 1:
                mid = tiles[s]
                side = [
                    jnp.where(row < 4, v_face[e, 3, s], v_face[e, 2, s]),
                    jnp.where(row < 4, spread(v_face[e, 3, 4], s), spread(v_face[e, 2, 4], s)),
                ]
            else:
                face = 0 if column == 0 else 1
                mid = jnp.concatenate([v_face[e, face, s], spread(v_face[e, face, 4], s)], axis=1)
                side = [nothing, nothing]
                if 2 <= i < 10:
                    at = s - 2 if column == 0 else s + 1
                    z_at = 2 if column == 0 else 0
                    low, high = v_edge.at[e, face, 0], v_edge.at[e, face, 1]
                    side = [
                        jnp.where(row < 4, high[at], low[at]),
                        jnp.where(row < 4, spread(high[z_at], s), spread(low[z_at], s)),
                    ]
            slabs.append(jnp.concatenate([mid, jnp.concatenate(side, axis=1)], axis=0))
        return slabs

    def coefficients():
        face_x = [face_terms(mean_x[i], box_u[i + 1] - box_u[i]) for i in range(13)]
        cface = []
        for j in range(7):
            cface.append(plane_sum(face_x[2 * j][1]))
            if 1 <= j < 6:
                cwx[j - 1] = fold_rows(cface[j])
        for i in range(7):
            wx[i] = fold_rows(face_x[i + 3][1])
        for c in range(6):
            pair_y, pair_z, pair_r = None, None, None
            for half in range(2):
                i = 2 * c + half
                u = box_u[i + 1]
                re = react[i]
                flux_y, w_y = face_terms(mean_y[i], up(u, 0) - u)
                flux_z, w_z = face_terms(mean_z[i], up(u, 1) - u)
                low_y, low_z = down(w_y, 0), down(w_z, 1)
                force = (
                    src[i]
                    - re * u
                    + (face_x[i + 1][0] - face_x[i][0])
                    + (flux_y - down(flux_y, 0))
                    + (flux_z - down(flux_z, 1))
                )
                v0[i] = fold_rows(force)
                if 2 <= i < 10:
                    diagonal = re + face_x[i + 1][1] + face_x[i][1] + w_y + low_y + w_z + low_z
                    inv[i - 2] = fold_rows(1.0 / diagonal)
                if 3 <= i < 9:
                    wyu[i - 3] = fold_rows(w_y)
                    wyl[i - 3] = fold_rows(low_y)
                    wzu[i - 3] = fold_rows(w_z)
                    wzl[i - 3] = fold_rows(low_z)
                pair_y = w_y if half == 0 else pair_y + w_y
                pair_z = w_z if half == 0 else pair_z + w_z
                pair_r = re if half == 0 else pair_r + re
            odd_row = lax.rem(index_of((24, 2 * LINE), 0), 2) == 1
            odd_lane = lax.rem(index_of((24, 2 * LINE), 1), 2) == 1
            sum_y = pair_sum(jnp.where(odd_row, pair_y, up(pair_y, 0)), 1)
            sum_z = pair_sum(jnp.where(odd_lane, pair_z, up(pair_z, 1)), 0)
            low_y, low_z = pltpu.roll(sum_y, 2, 0), pltpu.roll(sum_z, 2, 1)
            diagonal = plane_sum(pair_r) + cface[c] + cface[c + 1] + sum_y + low_y + sum_z + low_z
            cinv[c] = fold_rows(1.0 / diagonal)
            if 1 <= c < 5:
                cwyu[c - 1] = fold_rows(sum_y)
                cwyl[c - 1] = fold_rows(low_y)
                cwzu[c - 1] = fold_rows(sum_z)
                cwzl[c - 1] = fold_rows(low_z)

    def precondition(v, j):
        own = [inv[i] * v[i + 2] for i in range(8)]
        coarse = [cinv[c] * plane_sum(v[2 * c] + v[2 * c + 1]) for c in range(6)]
        coarse_z = []
        for c in range(4):
            q = coarse[c + 1]
            near = (
                cwx[c] * coarse[c]
                + cwx[c + 1] * coarse[c + 2]
                + cwyu[c] * pltpu.roll(q, 14, 0)
                + cwyl[c] * pltpu.roll(q, 2, 0)
                + cwzu[c] * pltpu.roll(q, 2 * LINE - 2, 1)
                + cwzl[c] * pltpu.roll(q, 2, 1)
            )
            coarse_z.append(COARSE_OWN * q + COARSE_NEAR * (cinv[c + 1] * near))
        for i in range(6):
            q = own[i + 1]
            near = (
                wx[i] * own[i]
                + wx[i + 1] * own[i + 2]
                + wyu[i] * up(q, 0)
                + wyl[i] * down(q, 0)
                + wzu[i] * up(q, 1)
                + wzl[i] * down(q, 1)
            )
            zs[j, i] = FINE_OWN * q + FINE_NEAR * (inv[i + 1] * near) + coarse_z[(i + 1) // 2]

    def image(j, s):
        i = s + 1
        tall = zs[j, i]
        here = tall[0:8]
        total = react[i + 3, 8:16] * here
        for weight, other in (
            (wx[i, 0:8], zs[j, i - 1, 0:8]),
            (wx[i + 1, 0:8], zs[j, i + 1, 0:8]),
            (wyu[i, 0:8], up(tall, 0)[0:8]),
            (wyl[i, 0:8], down(tall, 0)[0:8]),
            (wzu[i, 0:8], up(here, 1)),
            (wzl[i, 0:8], down(here, 1)),
        ):
            total = total + weight * (here - other)
        return total

    def global_sum(rows, which, between):
        group = index_of((1, LINE), 1) // 16
        mixed = jnp.zeros((1, LINE), jnp.float32)
        for n, row in enumerate(rows):
            row = jnp.sum(row, axis=0, keepdims=True)
            for shift in (64, 32, 16):
                row = row + pltpu.roll(row, shift, 1)
            mixed = jnp.where(group == n, row, mixed)
        phases = ((core_line, got1), (plane_line, got2), (long_line, got3))
        for phase, (partners, got) in enumerate(phases):
            if phase == 1 and which == 0:
                pl.semaphore_wait(far_sem, 4)
            sums[which, phase] = mixed
            slot = 6 + 3 * which + phase
            for n, partner in enumerate(partners):
                send(sums.at[which, phase], got.at[which, n], slot, partner)
            if phase == 0:
                between()
            part = got.at[which]
            pltpu.make_async_copy(part, part, recv_sem.at[slot]).wait()
            mixed = mixed + jnp.sum(got[which], axis=0)
        return [jnp.sum(jnp.where(group == n, mixed, 0.0), axis=1, keepdims=True) for n in range(6)]

    def solve(m):
        h = [(m[n + 1] + SHIFT * m[n]) * (1.0 / SCALE) for n in range(5)]

        def inverse(pivot, of):
            good = pivot > 1e-6 * of
            return jnp.where(good, 1.0 / jnp.where(good, pivot, 1.0), 0.0)

        i0 = inverse(h[0], jnp.zeros_like(h[0]))
        l1, l2 = h[1] * i0, h[2] * i0
        i1 = inverse(h[2] - l1 * h[1], h[2])
        h21 = h[3] - l2 * h[1]
        l21 = h21 * i1
        i2 = inverse(h[4] - l2 * h[2] - l21 * h21, h[4])
        y0 = m[0]
        y1 = m[1] - l1 * y0
        y2 = m[2] - l2 * y0 - l21 * y1
        c2 = y2 * i2
        c1 = y1 * i1 - l21 * c2
        c0 = y0 * i0 - l1 * c1 - l2 * c2
        return c0, c1, c2

    def total_of(tiles, others):
        total = tiles[0][:, 0:LINE] * others[0]
        for s in range(1, 4):
            total = total + tiles[s][:, 0:LINE] * others[s]
        return total

    given = []

    def give(sources, targets, slot, tiles):
        @pl.when(alone)
        def _():
            for source, target in zip(sources, targets):
                pltpu.make_async_copy(source, target, recv_sem.at[slot]).start()

        @pl.when(jnp.logical_not(alone))
        def _():
            for source, target in zip(sources, targets):
                pltpu.make_async_remote_copy(
                    source, target, send_sem.at[1], recv_sem.at[slot], device_id=partner, device_id_type=MESH
                ).start()

        given.append(tiles)

    pl.semaphore_wait(barrier, len(partners) + 1 - alone.astype(jnp.int32))
    give([u_ref, k_ref, r_ref, s_ref], [raw0.at[f, pl.ds(5, 4), pl.ds(8, 8)] for f in range(4)], 12, 16)
    last_r = pltpu.make_async_copy(r_ref, end_rs.at[0], send_sem.at[2])
    last_s = pltpu.make_async_copy(s_ref, end_rs.at[1], send_sem.at[3])
    last_r.start()
    last_s.start()
    receive(16, 12)
    pack_z([raw0[f, 5 + s, 8:16] for f in range(4) for s in range(4)], 0)
    pack_corners(raw0, 0, 4)
    count = exchange_wide(raw0, corner0, zed0, far0, 0, 4, 2, 0)
    receive(count, 0)
    for other in far_ones:
        pl.semaphore_signal(far_sem, inc=1, device_id=other, device_id_type=MESH)
    for i in range(14):
        box_u[i] = wide_slab(raw0, corner0, zed0, far0, 0, i)
    k_slabs = [wide_slab(raw0, corner0, zed0, far0, 1, i) for i in range(14)]
    for i in range(13):
        mean_x[i] = mean_of(k_slabs[i], k_slabs[i + 1])
    for i in range(12):
        k = k_slabs[i + 1]
        mean_y[i] = mean_of(k, up(k, 0))
        mean_z[i] = mean_of(k, up(k, 1))
        react[i] = wide_slab(raw0, corner0, zed0, far0, 2, i + 1)
        src[i] = wide_slab(raw0, corner0, zed0, far0, 3, i + 1)

    own = (slice(0, 8), slice(0, LINE))

    def give_field(f, slot):
        row = index_of((ROWS, LINE), 0)
        next_rows = jnp.zeros((ROWS, LINE), jnp.float32)
        next_lanes = next_rows
        for s in range(4):
            tile = pltpu.roll(zs[f, s + 1, 8:16, 0:LINE], 2 * s + 1, 0)
            next_rows = jnp.where(row // 2 == s, tile, next_rows)
            tile = pltpu.roll(zs[f, s + 1, 0:8, LINE : 2 * LINE], 2 * s + 1, 1)
            next_lanes = jnp.where(lane // 2 == s, tile, next_lanes)
        end_pack[f - 3, 0] = next_rows
        end_pack[f - 3, 1] = next_lanes
        region = (f, pl.ds(0, 6), pl.ds(0, 8), pl.ds(0, LINE))
        give([zs.at[region], end_pack.at[f - 3]], [end_zs.at[f - 3], end_halo.at[f - 3]], slot, 8)

    def beside_v(newton, j):
        if newton == 0 and j == 0:
            for i in range(6):
                zs[7, i] = fold_rows(k_slabs[i + 4])
            give_field(7, 14)
        elif newton == 1:
            if j == 0:
                give_field(3, 13)
            give_field(4 + j, 13)

    def end_fields(slabs, halo):
        tall = [jnp.concatenate([slabs[s + 1], pltpu.roll(halo[0], 7 - 2 * s, 0)], axis=0) for s in range(4)]
        wide = [
            jnp.concatenate([slabs[s + 1], pltpu.roll(halo[1], LINE - 1 - 2 * s, 1)], axis=1) for s in range(4)
        ]
        return slabs, tall, wide

    def end_means():
        receive(8, 14)
        slabs, tall, wide = end_fields([end_zs[4, i] for i in range(6)], [end_halo[4, i] for i in range(2)])
        for i in range(5):
            end_x[i] = mean_of(slabs[i], slabs[i + 1])
        for s in range(4):
            end_y[s] = mean_of(tall[s], up(tall[s], 0))
            end_z[s] = mean_of(wide[s], up(wide[s], 1))

    for newton in range(NEWTON):
        coefficients()
        rows = []
        v = [v0[i] for i in range(12)]
        tiles = [slab[0:8] for slab in v[4:8]]
        for j in range(KRYLOV):
            at = 4 * newton + j
            precondition(v, at)
            z_tiles = [zs[(at, s + 1) + own] for s in range(4)]
            rows.append(total_of(tiles, z_tiles))
            if newton + 1 < NEWTON:
                for s in range(4):
                    raw_h[j, 5 + s, 8:16] = z_tiles[s]
            tiles = [SCALE * image(at, s) - SHIFT * tiles[s] for s in range(4)]
            rows.append(total_of(tiles, z_tiles))
            if j + 1 < KRYLOV:
                v = exchange_v(tiles, 2 * newton + j, functools.partial(beside_v, newton, j))

        def beside(newton=newton):
            if newton + 1 < NEWTON:
                pack_z([raw_h[f, 5 + s, 8:16] for f in range(3) for s in range(4)], 1)
                pack_corners(raw_h, 1, 3)
                exchange_wide(raw_h, corner_h, zed_h, far_h, 1, 3, 3, 1)
            else:
                give_field(6, 13)
                end_means()

        c = solve(global_sum(rows, newton, beside))
        if newton + 1 < NEWTON:
            receive(wide_tiles(3, 3), 1)
            for i in range(14):
                total = box_u[i]
                for j in range(3):
                    total = total + c[j] * wide_slab(raw_h, corner_h, zed_h, far_h, j, i)
                box_u[i] = total
                if 4 <= i < 10:
                    zs[3, i - 4] = fold_rows(total)

    last_r.wait()
    last_s.wait()
    receive(8 * 4, 13)
    near = []
    for tiles in ([end_zs.at[:, i] for i in range(6)], [end_halo.at[:, i] for i in range(2)]):
        for tile in tiles:
            total = tile[0]
            for j in range(3):
                total = total + c[j] * tile[1 + j]
            near.append(total)
    last, tall, wide = end_fields(near[:6], near[6:])
    low_flux = None
    for s in range(-1, 4):
        flux, _ = face_terms(end_x[s + 1], last[s + 2] - last[s + 1])
        if s >= 0:
            ends[0, s] = last[s + 1]
            flux_y, _ = face_terms(end_y[s], up(tall[s], 0) - tall[s])
            flux_z, _ = face_terms(end_z[s], up(wide[s], 1) - wide[s])
            ends[1, s] = (
                end_rs[0, s] * last[s + 1]
                - (flux - low_flux)
                - (flux_y - down(flux_y, 0))[0:8]
                - (flux_z - down(flux_z, 1))[:, 0:LINE]
                - end_rs[1, s]
            )
        low_flux = flux
    store_u = pltpu.make_async_copy(ends.at[0], out_u, send_sem.at[2])
    store_f = pltpu.make_async_copy(ends.at[1], out_f, send_sem.at[3])
    store_u.start()
    store_f.start()
    for copy in copies:
        copy.wait_send()

    @pl.when(jnp.logical_not(alone))
    def _():
        part = dummy.at[pl.ds(0, sum(given))]
        pltpu.make_async_copy(part, part, send_sem.at[1]).wait()

    store_u.wait()
    store_f.wait()


def local(sizes, state, conductivity, reaction, source):
    nx, ny, nz = sizes
    plane, line = 4 * (nz // 2), (nx // 4) * ny

    def vmem(*shape):
        return pltpu.VMEM(shape, jnp.float32)

    full, half = (24, 2 * LINE), (16, 2 * LINE)
    tile = (ROWS, LINE)
    scratch = [
        vmem(4, 14, 24, LINE), vmem(2, 2, 4, 2, *tile), vmem(3, 3, 2, 2, *tile), vmem(2, 2, 2, *tile),
        vmem(3, 14, 24, LINE), vmem(2, 2, 3, 2, *tile), vmem(3, 3, 2, 2, *tile), vmem(2, 2, 2, *tile),
        vmem(4, 6, *tile), vmem(4, 4, 5, *tile), vmem(4, 2, 2, 3, *tile), vmem(2, 2, 2, *tile), vmem(2, 2, 4, 2, *tile), vmem(14, *full),
        vmem(13, *full), vmem(12, *full), vmem(12, *full), vmem(12, *full), vmem(12, *full),
        vmem(12, *half), vmem(8, *half), vmem(7, *half), vmem(6, *half), vmem(6, *half), vmem(6, *half), vmem(6, *half),
        vmem(6, *half), vmem(5, *half), vmem(4, *half), vmem(4, *half), vmem(4, *half), vmem(4, *half),
        vmem(8, 6, *half), vmem(2, 3, 1, LINE), vmem(2, 1, 1, LINE), vmem(2, plane - 1, 1, LINE), vmem(2, line - 1, 1, LINE),
        vmem(2, 4, *tile), vmem(160, *tile),
        vmem(5, 6, *tile), vmem(5, 2, *tile), vmem(5, 2, *tile), vmem(5, *tile), vmem(4, 16, LINE), vmem(4, ROWS, 2 * LINE), vmem(2, 4, *tile),
        pltpu.SemaphoreType.DMA((4,)), pltpu.SemaphoreType.DMA((15,)), pltpu.SemaphoreType.REGULAR,
    ]
    spec = pl.BlockSpec(memory_space=pltpu.MemorySpace.HBM)
    return pl.pallas_call(
        functools.partial(kernel, sizes),
        out_shape=[jax.ShapeDtypeStruct(state.shape, jnp.float32)] * 2,
        in_specs=[spec] * 4,
        out_specs=[spec] * 2,
        scratch_shapes=scratch,
        compiler_params=pltpu.CompilerParams(
            collective_id=0, has_side_effects=True, vmem_limit_bytes=61 * 1024 * 1024
        ),
    )(state, conductivity, reaction, source)


def solution(mesh):
    sizes = tuple(mesh.shape[name] for name in ("gx", "gy", "gz"))
    placed = P("gx", "gy", "gz")
    return jax.shard_map(
        functools.partial(local, sizes),
        mesh=mesh,
        in_specs=(placed,) * 4,
        out_specs=(placed, placed),
        check_vma=False,
    )
```

```python
import functools

import jax
import jax.numpy as jnp
from jax import lax
from jax.experimental import pallas as pl
from jax.experimental.pallas import tpu as pltpu
from jax.sharding import PartitionSpec as P

NEWTON = 2
KRYLOV = 3
EPS_SQUARE = 0.25
SCALE, SHIFT = 0.7, 1.0
MESH = pl.DeviceIdType.MESH

LINE = 128
ROWS = 8


def chebyshev_pair(low):
    centre = (2.0 + low) / 2.0
    half_width = (2.0 - low) / 2.0
    sigma = centre / half_width
    rho = 1.0 / sigma
    rho_new = 1.0 / (2.0 * sigma - rho)
    last = 2.0 * rho_new / half_width
    return (1.0 + rho_new * rho) / centre + last * (1.0 - 1.0 / centre), last / centre


FINE_OWN, FINE_NEAR = chebyshev_pair(0.3)
COARSE_OWN, COARSE_NEAR = chebyshev_pair(0.05)

CROSS = [(0, 0), (1, 0), (-1, 0), (0, 1), (0, -1)]
CORNERS = [(1, 1), (1, -1), (-1, 1), (-1, -1)]


def up(field, axis):
    return pltpu.roll(field, field.shape[axis] - 1, axis)


def down(field, axis):
    return pltpu.roll(field, 1, axis)


def index_of(shape, axis):
    return lax.broadcasted_iota(jnp.int32, shape, axis)


def face_terms(mean_k, difference):
    square = difference * difference
    inverse_root = lax.rsqrt(EPS_SQUARE + square)
    root = (EPS_SQUARE + square) * inverse_root
    return mean_k * root * difference, mean_k * (EPS_SQUARE + 2.0 * square) * inverse_root


def mean_of(one, other):
    return 2.0 * one * other / (one + other)


def fold_rows(field):
    row = index_of((ROWS, field.shape[1]), 0)
    return jnp.concatenate([field[8:16], jnp.where(row < 4, field[16:24], field[0:8])], axis=0)


def pair_sum(field, axis):
    odd = lax.rem(index_of(field.shape, axis), 2) == 1
    return field + jnp.where(odd, down(field, axis), up(field, axis))


def plane_sum(field):
    return pair_sum(pair_sum(field, 0), 1)


def kernel(
    sizes, u_ref, k_ref, r_ref, s_ref, out,
    raw0, corner0, zed0, far0, raw_h, corner_h, zed_h, far_h, v_out, v_face, v_edge, pack, corner_pack, box_u, mean_x, mean_y, mean_z, react, src,
    v0, inv, wx, wyu, wyl, wzu, wzl, cinv, cwx, cwyu, cwyl, cwzu, cwzl, zs, sums, got1, got2, got3, dummy,
    end_zs, end_pack, end_halo, end_x, end_y, end_z, end_rs, send_sem, recv_sem, far_sem,
):
    nx, ny, nz = sizes
    mx, my, mz = lax.axis_index("gx"), lax.axis_index("gy"), lax.axis_index("gz")

    group, place_y = mx // 4, lax.rem(mx, 4)
    bx, by = group * 4 + my, place_y
    partner = (group * 4 + my, place_y, mz)
    alone = my == place_y

    def block_at(dx, dy, dz):
        x, y = lax.rem(bx + dx + nx, nx), lax.rem(by + dy + ny, ny)
        return ((x // 4) * 4 + y, lax.rem(x, 4), lax.rem(mz + dz + nz, nz))

    core_line = [(mx, my, (mz // 2) * 2 + 1 - lax.rem(mz, 2))]
    plane = 4 * (nz // 2)
    here = lax.rem(mx, 4) * (nz // 2) + mz // 2
    plane_line = []
    for step in range(1, plane):
        there = lax.rem(here + step, plane)
        plane_line.append(
            ((mx // 4) * 4 + there // (nz // 2), my, lax.rem(there, nz // 2) * 2 + lax.rem(mz, 2))
        )
    line = (nx // 4) * ny
    at = (mx // 4) * ny + my
    long_line = []
    for step in range(1, line):
        there = lax.rem(at + step, line)
        long_line.append(((there // ny) * 4 + lax.rem(mx, 4), lax.rem(there, ny), mz))

    offsets = [(dx, dy, dz) for dx in (-1, 0, 1) for dy in (-1, 0, 1) for dz in (-1, 0, 1)]
    offsets = [d for d in offsets if d != (0, 0, 0)]
    offsets += [(dx, 0, dz) for dx in (2, -2) for dz in (-1, 0, 1)]

    barrier = pltpu.get_barrier_semaphore()
    partners = [block_at(*d) for d in offsets]
    far_ones = [(lax.rem(mx + step, nx), my, mz) for step in (4, nx - 4)]
    far_ones += [(mx, my, lax.rem(mz + step, nz)) for step in (2, nz - 2)]

    @pl.when(jnp.logical_not(alone))
    def _():
        pl.semaphore_signal(barrier, inc=1, device_id=partner, device_id_type=MESH)

    for other in partners:
        pl.semaphore_signal(barrier, inc=1, device_id=other, device_id_type=MESH)

    lane = index_of((ROWS, LINE), 1)
    copies = []

    def send(source, target, slot, device):
        copy = pltpu.make_async_remote_copy(
            source, target, send_sem.at[0], recv_sem.at[slot], device_id=device, device_id_type=MESH
        )
        copy.start()
        copies.append(copy)

    def receive(tiles, slot):
        part = dummy.at[pl.ds(0, tiles)]
        pltpu.make_async_copy(part, part, recv_sem.at[slot]).wait()

    def pack_z(tiles, place, at):
        low = jnp.zeros((ROWS, LINE), jnp.float32)
        high = low
        for g, tile in enumerate(tiles):
            mine = lane // 16 == g
            low = jnp.where(mine, tile if g == 0 else pltpu.roll(tile, 16 * g, 1), low)
            shift = (16 * g + 16) % LINE
            high = jnp.where(mine, pltpu.roll(tile, shift, 1) if shift else tile, high)
        pack[place, 0, at] = low
        pack[place, 1, at] = high

    def unpack_z(low_tiles, high_tiles, g):
        t, g = divmod(g, 8)
        shift = (LINE - 16 * g) % LINE
        above = pltpu.roll(low_tiles[t], shift, 1) if shift else low_tiles[t]
        shift = (LINE - 16 - 16 * g) % LINE
        below = pltpu.roll(high_tiles[t], shift, 1) if shift else high_tiles[t]
        return jnp.where(lane < 64, above, below)

    def pack_corners(raw, place, first, fields):
        low_rows = index_of((ROWS, LINE), 0) < 4
        for f in range(first, first + fields):
            for pair in range(2):
                one, two = raw[f, 5 + 2 * pair, 8:16], raw[f, 6 + 2 * pair, 8:16]
                two = pltpu.roll(two, 4, 0)
                corner_pack[place, 1, f, pair] = jnp.where(low_rows, two, one)
                corner_pack[place, 0, f, pair] = jnp.where(low_rows, one, two)

    def exchange_wide(raw, corner, place, first, fields, all_pairs, slot):
        which = pl.ds(first, fields)
        own = (which, pl.ds(5, 4), pl.ds(8, 8))
        for dx, dy in CROSS[1:3]:
            target = (which, pl.ds(5 - 4 * dx, 4), pl.ds(8 - 8 * dy, 8))
            send(raw.at[own], raw.at[target], slot, block_at(dx, dy, 0))
        for dx, dy in CORNERS:
            pairs = pl.ds(0, 2) if all_pairs else pl.ds((1 + dx) // 2, 1)
            send(
                corner_pack.at[place, (1 + dy) // 2, which, pairs],
                corner.at[(1 - dx) // 2, (1 - dy) // 2, which, pairs],
                slot,
                block_at(dx, dy, 0),
            )
        for dx, dy in CROSS[3:]:
            target = (which, pl.ds(5 - 4 * dx, 4), pl.ds(8 - 8 * dy, 8))
            send(raw.at[own], raw.at[target], slot, block_at(dx, dy, 0))
        return 16 * fields + (8 if all_pairs else 4) * fields

    def exchange_far(raw, zed2, place, fields, slot):
        some, rows, tiles = pl.ds(0, fields), pl.ds(8, 8), (fields + 1) // 2
        send(raw.at[some, pl.ds(8, 1), rows], raw.at[some, pl.ds(0, 1), rows], slot, block_at(2, 0, 0))
        send(raw.at[some, pl.ds(5, 1), rows], raw.at[some, pl.ds(13, 1), rows], slot, block_at(-2, 0, 0))
        for dx in (2, -2):
            for dz in (1, -1):
                send(
                    pack.at[place, (1 + dz) // 2, pl.ds(0, tiles)],
                    zed2.at[(2 - dx) // 4, (1 - dz) // 2, pl.ds(0, tiles)],
                    slot,
                    block_at(dx, 0, dz),
                )
        return 2 * fields + 4 * tiles

    def exchange_z(zed, place, slot):
        for dx, dy in CORNERS + CROSS:
            for dz in (1, -1):
                send(
                    pack.at[place, (1 + dz) // 2],
                    zed.at[1 - dx, 1 - dy, (1 - dz) // 2],
                    slot,
                    block_at(dx, dy, dz),
                )
        return 36

    nothing = jnp.zeros((ROWS, LINE), jnp.float32)

    def wide_slab(raw, corner, zed, zed2, field, i, slim=False):
        outer = i in (0, 13)
        if outer or (slim and i in (1, 2, 11, 12)):
            column, s = ((i - 1) // 4, (i - 1) % 4) if not outer else (0, 3) if i == 0 else (1, 0)
            low, high = (zed2[column, 1], zed2[column, 0]) if outer else (zed[column, 1, 1], zed[column, 1, 0])
            halo = unpack_z(low, high, field * 4 + s)
            mid = jnp.concatenate([raw[field, i, 8:16], halo], axis=1)
            empty = jnp.zeros_like(mid)
            return jnp.concatenate([empty, mid, empty], axis=0)
        column, s = divmod(i - 1, 4)
        if column == 1:
            main = raw[field, i]
        else:
            ends_y = []
            for y in range(2):
                packed = corner[column // 2, y, field, s // 2]
                ends_y.append(pltpu.roll(packed, 4, 0) if s % 2 else packed)
            main = jnp.concatenate([ends_y[0], raw[field, i, 8:16], ends_y[1]], axis=0)
        g = field * 4 + s
        halo = [unpack_z(zed[column, y, 1], zed[column, y, 0], g) for y in range(3)]
        return jnp.concatenate([main, jnp.concatenate(halo, axis=0)], axis=1)

    def exchange_v(tiles, e, between):
        slot = 2 + e
        packed = nothing
        for s in range(4):
            v_out[e, 1 + s] = tiles[s][:, 0:LINE]
            part = pltpu.roll(tiles[s][:, LINE : 2 * LINE], 16 * s + 8, 1)
            packed = jnp.where(lane // 16 == s, part, packed)
        v_out[e, 0] = packed
        v_out[e, 5] = packed
        for dx, dy in CORNERS:
            send(
                v_out.at[e, pl.ds(3 if dx > 0 else 0, 3)],
                v_edge.at[e, (1 - dx) // 2, (1 - dy) // 2],
                slot,
                block_at(dx, dy, 0),
            )
        for n, (dx, dy) in enumerate(CROSS[1:]):
            send(v_out.at[e, pl.ds(1, 5)], v_face.at[e, n], slot, block_at(dx, dy, 0))
        between()
        receive(12 + 20, slot)
        row = index_of((ROWS, LINE), 0)

        def spread(zeds, s):
            return pltpu.roll(zeds, LINE - 8 - 16 * s, 1)

        slabs = []
        for i in range(12):
            column, s = divmod(i, 4)
            if column == 1:
                mid = tiles[s]
                side = [
                    jnp.where(row < 4, v_face[e, 3, s], v_face[e, 2, s]),
                    jnp.where(row < 4, spread(v_face[e, 3, 4], s), spread(v_face[e, 2, 4], s)),
                ]
            else:
                face = 0 if column == 0 else 1
                mid = jnp.concatenate([v_face[e, face, s], spread(v_face[e, face, 4], s)], axis=1)
                side = [nothing, nothing]
                if 2 <= i < 10:
                    at = s - 2 if column == 0 else s + 1
                    z_at = 2 if column == 0 else 0
                    low, high = v_edge.at[e, face, 0], v_edge.at[e, face, 1]
                    side = [
                        jnp.where(row < 4, high[at], low[at]),
                        jnp.where(row < 4, spread(high[z_at], s), spread(low[z_at], s)),
                    ]
            slabs.append(jnp.concatenate([mid, jnp.concatenate(side, axis=1)], axis=0))
        return slabs

    def coefficients():
        face_x = [face_terms(mean_x[i], box_u[i + 1] - box_u[i]) for i in range(13)]
        cface = []
        for j in range(7):
            cface.append(plane_sum(face_x[2 * j][1]))
            if 1 <= j < 6:
                cwx[j - 1] = fold_rows(cface[j])
        for i in range(7):
            wx[i] = fold_rows(face_x[i + 3][1])
        for c in range(6):
            pair_y, pair_z, pair_r = None, None, None
            for half in range(2):
                i = 2 * c + half
                u = box_u[i + 1]
                re = react[i]
                flux_y, w_y = face_terms(mean_y[i], up(u, 0) - u)
                flux_z, w_z = face_terms(mean_z[i], up(u, 1) - u)
                low_y, low_z = down(w_y, 0), down(w_z, 1)
                force = (
                    src[i]
                    - re * u
                    + (face_x[i + 1][0] - face_x[i][0])
                    + (flux_y - down(flux_y, 0))
                    + (flux_z - down(flux_z, 1))
                )
                v0[i] = fold_rows(force)
                if 2 <= i < 10:
                    diagonal = re + face_x[i + 1][1] + face_x[i][1] + w_y + low_y + w_z + low_z
                    inv[i - 2] = fold_rows(1.0 / diagonal)
                if 3 <= i < 9:
                    wyu[i - 3] = fold_rows(w_y)
                    wyl[i - 3] = fold_rows(low_y)
                    wzu[i - 3] = fold_rows(w_z)
                    wzl[i - 3] = fold_rows(low_z)
                pair_y = w_y if half == 0 else pair_y + w_y
                pair_z = w_z if half == 0 else pair_z + w_z
                pair_r = re if half == 0 else pair_r + re
            odd_row = lax.rem(index_of((24, 2 * LINE), 0), 2) == 1
            odd_lane = lax.rem(index_of((24, 2 * LINE), 1), 2) == 1
            sum_y = pair_sum(jnp.where(odd_row, pair_y, up(pair_y, 0)), 1)
            sum_z = pair_sum(jnp.where(odd_lane, pair_z, up(pair_z, 1)), 0)
            low_y, low_z = pltpu.roll(sum_y, 2, 0), pltpu.roll(sum_z, 2, 1)
            diagonal = plane_sum(pair_r) + cface[c] + cface[c + 1] + sum_y + low_y + sum_z + low_z
            cinv[c] = fold_rows(1.0 / diagonal)
            if 1 <= c < 5:
                cwyu[c - 1] = fold_rows(sum_y)
                cwyl[c - 1] = fold_rows(low_y)
                cwzu[c - 1] = fold_rows(sum_z)
                cwzl[c - 1] = fold_rows(low_z)

    def precondition(v, j):
        own = [inv[i] * v[i + 2] for i in range(8)]
        coarse = [cinv[c] * plane_sum(v[2 * c] + v[2 * c + 1]) for c in range(6)]
        coarse_z = []
        for c in range(4):
            q = coarse[c + 1]
            near = (
                cwx[c] * coarse[c]
                + cwx[c + 1] * coarse[c + 2]
                + cwyu[c] * pltpu.roll(q, 14, 0)
                + cwyl[c] * pltpu.roll(q, 2, 0)
                + cwzu[c] * pltpu.roll(q, 2 * LINE - 2, 1)
                + cwzl[c] * pltpu.roll(q, 2, 1)
            )
            coarse_z.append(COARSE_OWN * q + COARSE_NEAR * (cinv[c + 1] * near))
        for i in range(6):
            q = own[i + 1]
            near = (
                wx[i] * own[i]
                + wx[i + 1] * own[i + 2]
                + wyu[i] * up(q, 0)
                + wyl[i] * down(q, 0)
                + wzu[i] * up(q, 1)
                + wzl[i] * down(q, 1)
            )
            zs[j, i] = FINE_OWN * q + FINE_NEAR * (inv[i + 1] * near) + coarse_z[(i + 1) // 2]

    def image(j, s):
        i = s + 1
        tall = zs[j, i]
        here = tall[0:8]
        total = react[i + 3, 8:16] * here
        for weight, other in (
            (wx[i, 0:8], zs[j, i - 1, 0:8]),
            (wx[i + 1, 0:8], zs[j, i + 1, 0:8]),
            (wyu[i, 0:8], up(tall, 0)[0:8]),
            (wyl[i, 0:8], down(tall, 0)[0:8]),
            (wzu[i, 0:8], up(here, 1)),
            (wzl[i, 0:8], down(here, 1)),
        ):
            total = total + weight * (here - other)
        return total

    def global_sum(rows, which, between):
        group = index_of((1, LINE), 1) // 16
        mixed = jnp.zeros((1, LINE), jnp.float32)
        for n, row in enumerate(rows):
            row = jnp.sum(row, axis=0, keepdims=True)
            for shift in (64, 32, 16):
                row = row + pltpu.roll(row, shift, 1)
            mixed = jnp.where(group == n, row, mixed)
        phases = ((core_line, got1), (plane_line, got2), (long_line, got3))
        for phase, (partners, got) in enumerate(phases):
            if phase == 1 and which == 0:
                pl.semaphore_wait(far_sem, 4)
            sums[which, phase] = mixed
            slot = 6 + 3 * which + phase
            for n, partner in enumerate(partners):
                send(sums.at[which, phase], got.at[which, n], slot, partner)
            if phase == 1:
                between()
            part = got.at[which]
            pltpu.make_async_copy(part, part, recv_sem.at[slot]).wait()
            mixed = mixed + jnp.sum(got[which], axis=0)
        return [jnp.sum(jnp.where(group == n, mixed, 0.0), axis=1, keepdims=True) for n in range(6)]

    def solve(m):
        h = [(m[n + 1] + SHIFT * m[n]) * (1.0 / SCALE) for n in range(5)]

        def inverse(pivot, of):
            good = pivot > 1e-6 * of
            return jnp.where(good, 1.0 / jnp.where(good, pivot, 1.0), 0.0)

        i0 = inverse(h[0], jnp.zeros_like(h[0]))
        l1, l2 = h[1] * i0, h[2] * i0
        i1 = inverse(h[2] - l1 * h[1], h[2])
        h21 = h[3] - l2 * h[1]
        l21 = h21 * i1
        i2 = inverse(h[4] - l2 * h[2] - l21 * h21, h[4])
        y0 = m[0]
        y1 = m[1] - l1 * y0
        y2 = m[2] - l2 * y0 - l21 * y1
        c2 = y2 * i2
        c1 = y1 * i1 - l21 * c2
        c0 = y0 * i0 - l1 * c1 - l2 * c2
        return c0, c1, c2

    def total_of(tiles, others):
        total = tiles[0][:, 0:LINE] * others[0]
        for s in range(1, 4):
            total = total + tiles[s][:, 0:LINE] * others[s]
        return total

    given = []

    def give(sources, targets, slot, tiles):
        @pl.when(alone)
        def _():
            for source, target in zip(sources, targets):
                pltpu.make_async_copy(source, target, recv_sem.at[slot]).start()

        @pl.when(jnp.logical_not(alone))
        def _():
            for source, target in zip(sources, targets):
                pltpu.make_async_remote_copy(
                    source, target, send_sem.at[1], recv_sem.at[slot], device_id=partner, device_id_type=MESH
                ).start()

        given.append(tiles)

    pl.semaphore_wait(barrier, len(partners) + 1 - alone.astype(jnp.int32))
    homes = [raw0.at[f, pl.ds(5, 4), pl.ds(8, 8)] for f in range(4)]
    give([u_ref, k_ref], homes[:2], 12, 8)
    give([r_ref, s_ref], homes[2:], 15, 8)
    last_r = pltpu.make_async_copy(r_ref, end_rs.at[0], send_sem.at[2])
    last_s = pltpu.make_async_copy(s_ref, end_rs.at[1], send_sem.at[3])
    last_r.start()
    last_s.start()
    receive(8, 12)
    pack_corners(raw0, 0, 0, 2)
    count = exchange_wide(raw0, corner0, 0, 0, 2, True, 0)
    pack_z([raw0[f, 5 + s, 8:16] for f in range(2) for s in range(4)], 0, 0)
    count += exchange_far(raw0, far0, 0, 2, 0)
    receive(8, 15)
    pack_corners(raw0, 0, 2, 2)
    count += exchange_wide(raw0, corner0, 0, 2, 2, False, 0)
    pack_z([raw0[f, 5 + s, 8:16] for f in range(2, 4) for s in range(4)], 0, 1)
    count += exchange_z(zed0, 0, 0)
    receive(count, 0)
    for other in far_ones:
        pl.semaphore_signal(far_sem, inc=1, device_id=other, device_id_type=MESH)
    for i in range(14):
        box_u[i] = wide_slab(raw0, corner0, zed0, far0, 0, i)
    k_slabs = [wide_slab(raw0, corner0, zed0, far0, 1, i) for i in range(14)]
    for i in range(13):
        mean_x[i] = mean_of(k_slabs[i], k_slabs[i + 1])
    for i in range(12):
        k = k_slabs[i + 1]
        mean_y[i] = mean_of(k, up(k, 0))
        mean_z[i] = mean_of(k, up(k, 1))
        react[i] = wide_slab(raw0, corner0, zed0, far0, 2, i + 1, True)
        src[i] = wide_slab(raw0, corner0, zed0, far0, 3, i + 1, True)

    own = (slice(0, 8), slice(0, LINE))

    def give_field(f, slot):
        row = index_of((ROWS, LINE), 0)
        next_rows = jnp.zeros((ROWS, LINE), jnp.float32)
        next_lanes = next_rows
        for s in range(4):
            tile = pltpu.roll(zs[f, s + 1, 8:16, 0:LINE], 2 * s + 1, 0)
            next_rows = jnp.where(row // 2 == s, tile, next_rows)
            tile = pltpu.roll(zs[f, s + 1, 0:8, LINE : 2 * LINE], 2 * s + 1, 1)
            next_lanes = jnp.where(lane // 2 == s, tile, next_lanes)
        end_pack[f - 3, 0] = next_rows
        end_pack[f - 3, 1] = next_lanes
        region = (f, pl.ds(0, 6), pl.ds(0, 8), pl.ds(0, LINE))
        give([zs.at[region], end_pack.at[f - 3]], [end_zs.at[f - 3], end_halo.at[f - 3]], slot, 8)

    def beside_v(newton, j):
        if newton == 0 and j == 0:
            for i in range(6):
                zs[7, i] = fold_rows(k_slabs[i + 4])
            give_field(7, 14)
        elif newton == 1:
            if j == 0:
                give_field(3, 13)
            give_field(4 + j, 13)

    def end_fields(slabs, halo):
        tall = [jnp.concatenate([slabs[s + 1], pltpu.roll(halo[0], 7 - 2 * s, 0)], axis=0) for s in range(4)]
        wide = [
            jnp.concatenate([slabs[s + 1], pltpu.roll(halo[1], LINE - 1 - 2 * s, 1)], axis=1) for s in range(4)
        ]
        return slabs, tall, wide

    def end_means():
        receive(8, 14)
        slabs, tall, wide = end_fields([end_zs[4, i] for i in range(6)], [end_halo[4, i] for i in range(2)])
        for i in range(5):
            end_x[i] = mean_of(slabs[i], slabs[i + 1])
        for s in range(4):
            end_y[s] = mean_of(tall[s], up(tall[s], 0))
            end_z[s] = mean_of(wide[s], up(wide[s], 1))

    for newton in range(NEWTON):
        coefficients()
        rows = []
        v = [v0[i] for i in range(12)]
        tiles = [slab[0:8] for slab in v[4:8]]
        for j in range(KRYLOV):
            at = 4 * newton + j
            precondition(v, at)
            z_tiles = [zs[(at, s + 1) + own] for s in range(4)]
            rows.append(total_of(tiles, z_tiles))
            if newton + 1 < NEWTON:
                for s in range(4):
                    raw_h[j, 5 + s, 8:16] = z_tiles[s]
            tiles = [SCALE * image(at, s) - SHIFT * tiles[s] for s in range(4)]
            rows.append(total_of(tiles, z_tiles))
            if j + 1 < KRYLOV:
                v = exchange_v(tiles, 2 * newton + j, functools.partial(beside_v, newton, j))

        counts = []

        def beside(newton=newton, counts=counts):
            if newton + 1 < NEWTON:
                pack_corners(raw_h, 1, 0, 3)
                counts.append(exchange_wide(raw_h, corner_h, 1, 0, 3, True, 1))
                pack_z([raw_h[f, 5 + s, 8:16] for f in range(2) for s in range(4)], 1, 0)
                pack_z([raw_h[2, 5 + s, 8:16] for s in range(4)], 1, 1)
                counts.append(exchange_far(raw_h, far_h, 1, 3, 1))
                counts.append(exchange_z(zed_h, 1, 1))
            else:
                give_field(6, 13)
                end_means()

        c = solve(global_sum(rows, newton, beside))
        if newton + 1 < NEWTON:
            receive(sum(counts), 1)
            for i in range(14):
                total = box_u[i]
                for j in range(3):
                    total = total + c[j] * wide_slab(raw_h, corner_h, zed_h, far_h, j, i)
                box_u[i] = total
                if 4 <= i < 10:
                    zs[3, i - 4] = fold_rows(total)

    last_r.wait()
    last_s.wait()
    receive(8 * 4, 13)
    near = []
    for tiles in ([end_zs.at[:, i] for i in range(6)], [end_halo.at[:, i] for i in range(2)]):
        for tile in tiles:
            total = tile[0]
            for j in range(3):
                total = total + c[j] * tile[1 + j]
            near.append(total)
    last, tall, wide = end_fields(near[:6], near[6:])
    low_flux = None
    for s in range(-1, 4):
        flux, _ = face_terms(end_x[s + 1], last[s + 2] - last[s + 1])
        if s >= 0:
            out[0, s] = last[s + 1]
            flux_y, _ = face_terms(end_y[s], up(tall[s], 0) - tall[s])
            flux_z, _ = face_terms(end_z[s], up(wide[s], 1) - wide[s])
            out[1, s] = (
                end_rs[0, s] * last[s + 1]
                - (flux - low_flux)
                - (flux_y - down(flux_y, 0))[0:8]
                - (flux_z - down(flux_z, 1))[:, 0:LINE]
                - end_rs[1, s]
            )
        low_flux = flux
    for copy in copies:
        copy.wait_send()

    @pl.when(jnp.logical_not(alone))
    def _():
        part = dummy.at[pl.ds(0, sum(given))]
        pltpu.make_async_copy(part, part, send_sem.at[1]).wait()


def local(sizes, state, conductivity, reaction, source):
    nx, ny, nz = sizes
    plane, line = 4 * (nz // 2), (nx // 4) * ny

    def vmem(*shape):
        return pltpu.VMEM(shape, jnp.float32)

    full, half = (24, 2 * LINE), (16, 2 * LINE)
    tile = (ROWS, LINE)
    scratch = [
        vmem(4, 14, 24, LINE), vmem(2, 2, 4, 2, *tile), vmem(3, 3, 2, 2, *tile), vmem(2, 2, 2, *tile),
        vmem(3, 14, 24, LINE), vmem(2, 2, 3, 2, *tile), vmem(3, 3, 2, 2, *tile), vmem(2, 2, 2, *tile),
        vmem(4, 6, *tile), vmem(4, 4, 5, *tile), vmem(4, 2, 2, 3, *tile), vmem(2, 2, 2, *tile), vmem(2, 2, 4, 2, *tile), vmem(14, *full),
        vmem(13, *full), vmem(12, *full), vmem(12, *full), vmem(12, *full), vmem(12, *full),
        vmem(12, *half), vmem(8, *half), vmem(7, *half), vmem(6, *half), vmem(6, *half), vmem(6, *half), vmem(6, *half),
        vmem(6, *half), vmem(5, *half), vmem(4, *half), vmem(4, *half), vmem(4, *half), vmem(4, *half),
        vmem(8, 6, *half), vmem(2, 3, 1, LINE), vmem(2, 1, 1, LINE), vmem(2, plane - 1, 1, LINE), vmem(2, line - 1, 1, LINE),
        vmem(160, *tile),
        vmem(5, 6, *tile), vmem(5, 2, *tile), vmem(5, 2, *tile), vmem(5, *tile), vmem(4, 16, LINE), vmem(4, ROWS, 2 * LINE), vmem(2, 4, *tile),
        pltpu.SemaphoreType.DMA((4,)), pltpu.SemaphoreType.DMA((16,)), pltpu.SemaphoreType.REGULAR,
    ]
    spec = pl.BlockSpec(memory_space=pltpu.MemorySpace.HBM)
    both = pl.pallas_call(
        functools.partial(kernel, sizes),
        out_shape=jax.ShapeDtypeStruct((2, *state.shape), jnp.float32),
        in_specs=[spec] * 4,
        out_specs=pl.BlockSpec(memory_space=pltpu.VMEM),
        scratch_shapes=scratch,
        compiler_params=pltpu.CompilerParams(
            collective_id=0, has_side_effects=True, vmem_limit_bytes=61 * 1024 * 1024
        ),
    )(state, conductivity, reaction, source)
    return both[0], both[1]


def solution(mesh):
    sizes = tuple(mesh.shape[name] for name in ("gx", "gy", "gz"))
    placed = P("gx", "gy", "gz")
    return jax.shard_map(
        functools.partial(local, sizes),
        mesh=mesh,
        in_specs=(placed,) * 4,
        out_specs=(placed, placed),
        check_vma=False,
    )
```

```python
import functools

import jax
import jax.numpy as jnp
from jax import lax
from jax.experimental import pallas as pl
from jax.experimental.pallas import tpu as pltpu
from jax.sharding import PartitionSpec as P

NEWTON = 2
KRYLOV = 3
EPS_SQUARE = 0.25
SCALE, SHIFT = 0.7, 1.0
MESH = pl.DeviceIdType.MESH

LINE = 128
ROWS = 8


def chebyshev_pair(low):
    centre = (2.0 + low) / 2.0
    half_width = (2.0 - low) / 2.0
    sigma = centre / half_width
    rho = 1.0 / sigma
    rho_new = 1.0 / (2.0 * sigma - rho)
    last = 2.0 * rho_new / half_width
    return (1.0 + rho_new * rho) / centre + last * (1.0 - 1.0 / centre), last / centre


FINE_OWN, FINE_NEAR = chebyshev_pair(0.3)
COARSE_OWN, COARSE_NEAR = chebyshev_pair(0.05)

CROSS = [(0, 0), (1, 0), (-1, 0), (0, 1), (0, -1)]
CORNERS = [(1, 1), (1, -1), (-1, 1), (-1, -1)]


def up(field, axis):
    return pltpu.roll(field, field.shape[axis] - 1, axis)


def down(field, axis):
    return pltpu.roll(field, 1, axis)


def index_of(shape, axis):
    return lax.broadcasted_iota(jnp.int32, shape, axis)


def face_terms(mean_k, difference):
    square = difference * difference
    inverse_root = lax.rsqrt(EPS_SQUARE + square)
    root = (EPS_SQUARE + square) * inverse_root
    return mean_k * root * difference, mean_k * (EPS_SQUARE + 2.0 * square) * inverse_root


def mean_of(one, other):
    return 2.0 * one * other / (one + other)


def fold_rows(field):
    row = index_of((ROWS, field.shape[1]), 0)
    return jnp.concatenate([field[8:16], jnp.where(row < 4, field[16:24], field[0:8])], axis=0)


def pair_sum(field, axis):
    odd = lax.rem(index_of(field.shape, axis), 2) == 1
    return field + jnp.where(odd, down(field, axis), up(field, axis))


def plane_sum(field):
    return pair_sum(pair_sum(field, 0), 1)


def kernel(
    sizes, u_ref, k_ref, r_ref, s_ref, out,
    raw0, corner0, zed0, far0, raw_h, corner_h, zed_h, far_h, v_out, v_face, v_edge, pack, corner_pack, box_u, mean_x, mean_y, mean_z, react, src,
    creact, v0, inv, wx, wyu, wyl, wzu, wzl, cinv, cwx, cwyu, cwyl, cwzu, cwzl, zs, sums, got1, got2, got3, dummy,
    end_zs, end_pack, end_halo, end_x, end_y, end_z, end_rs, send_sem, recv_sem, far_sem,
):
    nx, ny, nz = sizes
    mx, my, mz = lax.axis_index("gx"), lax.axis_index("gy"), lax.axis_index("gz")

    group, place_y = mx // 4, lax.rem(mx, 4)
    bx, by = group * 4 + my, place_y
    partner = (group * 4 + my, place_y, mz)
    alone = my == place_y

    def block_at(dx, dy, dz):
        x, y = lax.rem(bx + dx + nx, nx), lax.rem(by + dy + ny, ny)
        return ((x // 4) * 4 + y, lax.rem(x, 4), lax.rem(mz + dz + nz, nz))

    core_line = [(mx, my, (mz // 2) * 2 + 1 - lax.rem(mz, 2))]
    plane = 4 * (nz // 2)
    here = lax.rem(mx, 4) * (nz // 2) + mz // 2
    plane_line = []
    for step in range(1, plane):
        there = lax.rem(here + step, plane)
        plane_line.append(
            ((mx // 4) * 4 + there // (nz // 2), my, lax.rem(there, nz // 2) * 2 + lax.rem(mz, 2))
        )
    line = (nx // 4) * ny
    at = (mx // 4) * ny + my
    long_line = []
    for step in range(1, line):
        there = lax.rem(at + step, line)
        long_line.append(((there // ny) * 4 + lax.rem(mx, 4), lax.rem(there, ny), mz))

    offsets = [(dx, dy, dz) for dx in (-1, 0, 1) for dy in (-1, 0, 1) for dz in (-1, 0, 1)]
    offsets = [d for d in offsets if d != (0, 0, 0)]
    offsets += [(dx, 0, dz) for dx in (2, -2) for dz in (-1, 0, 1)]

    barrier = pltpu.get_barrier_semaphore()
    partners = [block_at(*d) for d in offsets]
    far_ones = [(lax.rem(mx + step, nx), my, mz) for step in (4, nx - 4)]
    far_ones += [(mx, my, lax.rem(mz + step, nz)) for step in (2, nz - 2)]

    @pl.when(jnp.logical_not(alone))
    def _():
        pl.semaphore_signal(barrier, inc=1, device_id=partner, device_id_type=MESH)

    for other in partners:
        pl.semaphore_signal(barrier, inc=1, device_id=other, device_id_type=MESH)

    lane = index_of((ROWS, LINE), 1)
    copies = []

    def send(source, target, slot, device):
        copy = pltpu.make_async_remote_copy(
            source, target, send_sem.at[0], recv_sem.at[slot], device_id=device, device_id_type=MESH
        )
        copy.start()
        copies.append(copy)

    def receive(tiles, slot):
        part = dummy.at[pl.ds(0, tiles)]
        pltpu.make_async_copy(part, part, recv_sem.at[slot]).wait()

    def pack_z(tiles, place, at):
        low = jnp.zeros((ROWS, LINE), jnp.float32)
        high = low
        for g, tile in enumerate(tiles):
            mine = lane // 16 == g
            low = jnp.where(mine, tile if g == 0 else pltpu.roll(tile, 16 * g, 1), low)
            shift = (16 * g + 16) % LINE
            high = jnp.where(mine, pltpu.roll(tile, shift, 1) if shift else tile, high)
        pack[place, 0, at] = low
        pack[place, 1, at] = high

    def unpack_z(low_tiles, high_tiles, g):
        t, g = divmod(g, 8)
        shift = (LINE - 16 * g) % LINE
        above = pltpu.roll(low_tiles[t], shift, 1) if shift else low_tiles[t]
        shift = (LINE - 16 - 16 * g) % LINE
        below = pltpu.roll(high_tiles[t], shift, 1) if shift else high_tiles[t]
        return jnp.where(lane < 64, above, below)

    def pack_corners(raw, place, first, fields):
        low_rows = index_of((ROWS, LINE), 0) < 4
        for f in range(first, first + fields):
            for pair in range(2):
                one, two = raw[f, 5 + 2 * pair, 8:16], raw[f, 6 + 2 * pair, 8:16]
                two = pltpu.roll(two, 4, 0)
                corner_pack[place, 1, f, pair] = jnp.where(low_rows, two, one)
                corner_pack[place, 0, f, pair] = jnp.where(low_rows, one, two)

    def exchange_wide(raw, corner, place, first, fields, all_pairs, slot):
        which = pl.ds(first, fields)
        own = (which, pl.ds(5, 4), pl.ds(8, 8))
        for dx, dy in CROSS[1:3]:
            target = (which, pl.ds(5 - 4 * dx, 4), pl.ds(8 - 8 * dy, 8))
            send(raw.at[own], raw.at[target], slot, block_at(dx, dy, 0))
        for dx, dy in CORNERS:
            pairs = pl.ds(0, 2) if all_pairs else pl.ds((1 + dx) // 2, 1)
            send(
                corner_pack.at[place, (1 + dy) // 2, which, pairs],
                corner.at[(1 - dx) // 2, (1 - dy) // 2, which, pairs],
                slot,
                block_at(dx, dy, 0),
            )
        for dx, dy in CROSS[3:]:
            target = (which, pl.ds(5 - 4 * dx, 4), pl.ds(8 - 8 * dy, 8))
            send(raw.at[own], raw.at[target], slot, block_at(dx, dy, 0))
        return 16 * fields + (8 if all_pairs else 4) * fields

    def exchange_far(raw, zed2, place, fields, slot):
        some, rows, tiles = pl.ds(0, fields), pl.ds(8, 8), (fields + 1) // 2
        send(raw.at[some, pl.ds(8, 1), rows], raw.at[some, pl.ds(0, 1), rows], slot, block_at(2, 0, 0))
        send(raw.at[some, pl.ds(5, 1), rows], raw.at[some, pl.ds(13, 1), rows], slot, block_at(-2, 0, 0))
        for dx in (2, -2):
            for dz in (1, -1):
                send(
                    pack.at[place, (1 + dz) // 2, pl.ds(0, tiles)],
                    zed2.at[(2 - dx) // 4, (1 - dz) // 2, pl.ds(0, tiles)],
                    slot,
                    block_at(dx, 0, dz),
                )
        return 2 * fields + 4 * tiles

    def exchange_z(zed, place, slot):
        for dx, dy in CORNERS + CROSS:
            for dz in (1, -1):
                send(
                    pack.at[place, (1 + dz) // 2],
                    zed.at[1 - dx, 1 - dy, (1 - dz) // 2],
                    slot,
                    block_at(dx, dy, dz),
                )
        return 36

    nothing = jnp.zeros((ROWS, LINE), jnp.float32)

    def wide_slab(raw, corner, zed, zed2, field, i, slim=False):
        outer = i in (0, 13)
        if outer or (slim and i in (1, 2, 11, 12)):
            column, s = ((i - 1) // 4, (i - 1) % 4) if not outer else (0, 3) if i == 0 else (1, 0)
            low, high = (zed2[column, 1], zed2[column, 0]) if outer else (zed[column, 1, 1], zed[column, 1, 0])
            halo = unpack_z(low, high, field * 4 + s)
            mid = jnp.concatenate([raw[field, i, 8:16], halo], axis=1)
            empty = jnp.zeros_like(mid)
            return jnp.concatenate([empty, mid, empty], axis=0)
        column, s = divmod(i - 1, 4)
        if column == 1:
            main = raw[field, i]
        else:
            ends_y = []
            for y in range(2):
                packed = corner[column // 2, y, field, s // 2]
                ends_y.append(pltpu.roll(packed, 4, 0) if s % 2 else packed)
            main = jnp.concatenate([ends_y[0], raw[field, i, 8:16], ends_y[1]], axis=0)
        g = field * 4 + s
        halo = [unpack_z(zed[column, y, 1], zed[column, y, 0], g) for y in range(3)]
        return jnp.concatenate([main, jnp.concatenate(halo, axis=0)], axis=1)

    def exchange_v(tiles, e, between):
        slot = 2 + e
        packed = nothing
        for s in range(4):
            v_out[e, 1 + s] = tiles[s][:, 0:LINE]
            part = pltpu.roll(tiles[s][:, LINE : 2 * LINE], 16 * s + 8, 1)
            packed = jnp.where(lane // 16 == s, part, packed)
        v_out[e, 0] = packed
        v_out[e, 5] = packed
        for dx, dy in CORNERS:
            send(
                v_out.at[e, pl.ds(3 if dx > 0 else 0, 3)],
                v_edge.at[e, (1 - dx) // 2, (1 - dy) // 2],
                slot,
                block_at(dx, dy, 0),
            )
        for n, (dx, dy) in enumerate(CROSS[1:]):
            send(v_out.at[e, pl.ds(1, 5)], v_face.at[e, n], slot, block_at(dx, dy, 0))
        between()
        receive(12 + 20, slot)
        row = index_of((ROWS, LINE), 0)

        def spread(zeds, s):
            return pltpu.roll(zeds, LINE - 8 - 16 * s, 1)

        slabs = []
        for i in range(12):
            column, s = divmod(i, 4)
            if column == 1:
                mid = tiles[s]
                side = [
                    jnp.where(row < 4, v_face[e, 3, s], v_face[e, 2, s]),
                    jnp.where(row < 4, spread(v_face[e, 3, 4], s), spread(v_face[e, 2, 4], s)),
                ]
            else:
                face = 0 if column == 0 else 1
                mid = jnp.concatenate([v_face[e, face, s], spread(v_face[e, face, 4], s)], axis=1)
                side = [nothing, nothing]
                if 2 <= i < 10:
                    at = s - 2 if column == 0 else s + 1
                    z_at = 2 if column == 0 else 0
                    low, high = v_edge.at[e, face, 0], v_edge.at[e, face, 1]
                    side = [
                        jnp.where(row < 4, high[at], low[at]),
                        jnp.where(row < 4, spread(high[z_at], s), spread(low[z_at], s)),
                    ]
            slabs.append(jnp.concatenate([mid, jnp.concatenate(side, axis=1)], axis=0))
        return slabs

    def is_own(i):
        return 5 <= i < 9

    def narrow(slab, i):
        return slab if is_own(i) else fold_rows(slab)

    def put(ref, i, value, whole):
        if whole:
            ref[i] = value
        else:
            ref[i, 0:8] = value[0:8]

    def coefficients():
        u16 = [fold_rows(box_u[i]) if is_own(i) else box_u[i, 0:16] for i in range(14)]
        face_x = [face_terms(mean_x[i], u16[i + 1] - u16[i]) for i in range(13)]
        cface = []
        for j in range(7):
            cface.append(plane_sum(face_x[2 * j][1]))
            if 1 <= j < 6:
                put(cwx, j - 1, cface[j], 1 < j < 5)
        for i in range(7):
            put(wx, i, face_x[i + 3][1], 0 < i < 6)
        odd_row = lax.rem(index_of((16, 2 * LINE), 0), 2) == 1
        odd_lane = lax.rem(index_of((16, 2 * LINE), 1), 2) == 1
        for c in range(6):
            pairs = None
            for half in range(2):
                i = 2 * c + half
                u, re = u16[i + 1], react[i]
                if is_own(i + 1):
                    tall = box_u[i + 1]
                    flux, w = face_terms(mean_y[i], up(tall, 0) - tall)
                    flux_y, w_y = fold_rows(flux), fold_rows(w)
                    low_flux_y, low_y = fold_rows(down(flux, 0)), fold_rows(down(w, 0))
                else:
                    flux_y, w_y = face_terms(mean_y[i, 0:16], up(u, 0) - u)
                    low_flux_y, low_y = down(flux_y, 0), down(w_y, 0)
                flux_z, w_z = face_terms(mean_z[i], up(u, 1) - u)
                low_z = down(w_z, 1)
                force = (
                    src[i]
                    - re * u
                    + (face_x[i + 1][0] - face_x[i][0])
                    + (flux_y - low_flux_y)
                    + (flux_z - down(flux_z, 1))
                )
                put(v0, i, force, 2 <= i < 10)
                if 2 <= i < 10:
                    diagonal = re + face_x[i + 1][1] + face_x[i][1] + w_y + low_y + w_z + low_z
                    put(inv, i - 2, 1.0 / diagonal, 3 <= i < 9)
                if 3 <= i < 9:
                    for ref, weight in ((wyu, w_y), (wyl, low_y), (wzu, w_z), (wzl, low_z)):
                        put(ref, i - 3, weight, 4 <= i < 8)
                now = (w_y, low_y, w_z)
                pairs = now if half == 0 else tuple(one + two for one, two in zip(pairs, now))
            pair_y, pair_low, pair_z = pairs
            sum_y = pair_sum(jnp.where(odd_row, pair_y, up(pair_y, 0)), 1)
            sum_z = pair_sum(jnp.where(odd_lane, pair_z, up(pair_z, 1)), 0)
            if c in (2, 3):
                low_y = pair_sum(jnp.where(odd_row, down(pair_low, 0), pair_low), 1)
            else:
                low_y = pltpu.roll(sum_y, 2, 0)
            low_z = pltpu.roll(sum_z, 2, 1)
            diagonal = creact[c] + cface[c] + cface[c + 1] + sum_y + low_y + sum_z + low_z
            put(cinv, c, 1.0 / diagonal, 1 <= c < 5)
            if 1 <= c < 5:
                for ref, weight in ((cwyu, sum_y), (cwyl, low_y), (cwzu, sum_z), (cwzl, low_z)):
                    put(ref, c - 1, weight, 2 <= c < 4)

    def precondition(v, j):
        def part(whole):
            return slice(0, 16) if whole else slice(0, 8)

        own = [inv[i, part(0 < i < 7)] * v[i + 2][part(0 < i < 7)] for i in range(8)]
        coarse = []
        for c in range(6):
            rows = part(1 <= c < 5)
            coarse.append(cinv[c, rows] * plane_sum(v[2 * c][rows] + v[2 * c + 1][rows]))
        coarse_z = []
        for c in range(4):
            q, rows = coarse[c + 1], part(1 <= c < 3)
            near = (
                cwx[c, rows] * coarse[c][rows]
                + cwx[c + 1, rows] * coarse[c + 2][rows]
                + cwyu[c, rows] * pltpu.roll(q, 14, 0)[rows]
                + cwyl[c, rows] * pltpu.roll(q, 2, 0)[rows]
                + cwzu[c, rows] * pltpu.roll(q[rows], 2 * LINE - 2, 1)
                + cwzl[c, rows] * pltpu.roll(q[rows], 2, 1)
            )
            coarse_z.append(COARSE_OWN * q[rows] + COARSE_NEAR * (cinv[c + 1, rows] * near))
        for i in range(6):
            q, rows = own[i + 1], part(0 < i < 5)
            near = (
                wx[i, rows] * own[i][rows]
                + wx[i + 1, rows] * own[i + 2][rows]
                + wyu[i, rows] * up(q, 0)[rows]
                + wyl[i, rows] * down(q, 0)[rows]
                + wzu[i, rows] * up(q[rows], 1)
                + wzl[i, rows] * down(q[rows], 1)
            )
            zs[j, i, rows] = (
                FINE_OWN * q[rows] + FINE_NEAR * (inv[i + 1, rows] * near) + coarse_z[(i + 1) // 2][rows]
            )

    def image(j, s):
        i = s + 1
        tall = zs[j, i]
        here = tall[0:8]
        total = react[i + 3, 0:8] * here
        for weight, other in (
            (wx[i, 0:8], zs[j, i - 1, 0:8]),
            (wx[i + 1, 0:8], zs[j, i + 1, 0:8]),
            (wyu[i, 0:8], up(tall, 0)[0:8]),
            (wyl[i, 0:8], down(tall, 0)[0:8]),
            (wzu[i, 0:8], up(here, 1)),
            (wzl[i, 0:8], down(here, 1)),
        ):
            total = total + weight * (here - other)
        return total

    def global_sum(rows, which, between):
        group = index_of((1, LINE), 1) // 16
        mixed = jnp.zeros((1, LINE), jnp.float32)
        for n, row in enumerate(rows):
            row = jnp.sum(row, axis=0, keepdims=True)
            for shift in (64, 32, 16):
                row = row + pltpu.roll(row, shift, 1)
            mixed = jnp.where(group == n, row, mixed)
        phases = ((core_line, got1), (plane_line, got2), (long_line, got3))
        for phase, (partners, got) in enumerate(phases):
            if phase == 1 and which == 0:
                pl.semaphore_wait(far_sem, 4)
            sums[which, phase] = mixed
            slot = 6 + 3 * which + phase
            for n, partner in enumerate(partners):
                send(sums.at[which, phase], got.at[which, n], slot, partner)
            if phase == 1:
                between()
            part = got.at[which]
            pltpu.make_async_copy(part, part, recv_sem.at[slot]).wait()
            mixed = mixed + jnp.sum(got[which], axis=0)
        return [jnp.sum(jnp.where(group == n, mixed, 0.0), axis=1, keepdims=True) for n in range(6)]

    def solve(m):
        h = [(m[n + 1] + SHIFT * m[n]) * (1.0 / SCALE) for n in range(5)]

        def inverse(pivot, of):
            good = pivot > 1e-6 * of
            return jnp.where(good, 1.0 / jnp.where(good, pivot, 1.0), 0.0)

        i0 = inverse(h[0], jnp.zeros_like(h[0]))
        l1, l2 = h[1] * i0, h[2] * i0
        i1 = inverse(h[2] - l1 * h[1], h[2])
        h21 = h[3] - l2 * h[1]
        l21 = h21 * i1
        i2 = inverse(h[4] - l2 * h[2] - l21 * h21, h[4])
        y0 = m[0]
        y1 = m[1] - l1 * y0
        y2 = m[2] - l2 * y0 - l21 * y1
        c2 = y2 * i2
        c1 = y1 * i1 - l21 * c2
        c0 = y0 * i0 - l1 * c1 - l2 * c2
        return c0, c1, c2

    def total_of(tiles, others):
        total = tiles[0][:, 0:LINE] * others[0]
        for s in range(1, 4):
            total = total + tiles[s][:, 0:LINE] * others[s]
        return total

    given = []

    def give(sources, targets, slot, tiles):
        @pl.when(alone)
        def _():
            for source, target in zip(sources, targets):
                pltpu.make_async_copy(source, target, recv_sem.at[slot]).start()

        @pl.when(jnp.logical_not(alone))
        def _():
            for source, target in zip(sources, targets):
                pltpu.make_async_remote_copy(
                    source, target, send_sem.at[1], recv_sem.at[slot], device_id=partner, device_id_type=MESH
                ).start()

        given.append(tiles)

    pl.semaphore_wait(barrier, len(partners) + 1 - alone.astype(jnp.int32))
    homes = [raw0.at[f, pl.ds(5, 4), pl.ds(8, 8)] for f in range(4)]
    give([u_ref, k_ref], homes[:2], 12, 8)
    give([r_ref, s_ref], homes[2:], 15, 8)
    last_r = pltpu.make_async_copy(r_ref, end_rs.at[0], send_sem.at[2])
    last_s = pltpu.make_async_copy(s_ref, end_rs.at[1], send_sem.at[3])
    last_r.start()
    last_s.start()
    receive(8, 12)
    pack_corners(raw0, 0, 0, 2)
    count = exchange_wide(raw0, corner0, 0, 0, 2, True, 0)
    pack_z([raw0[f, 5 + s, 8:16] for f in range(2) for s in range(4)], 0, 0)
    count += exchange_far(raw0, far0, 0, 2, 0)
    receive(8, 15)
    pack_corners(raw0, 0, 2, 2)
    count += exchange_wide(raw0, corner0, 0, 2, 2, False, 0)
    pack_z([raw0[f, 5 + s, 8:16] for f in range(2, 4) for s in range(4)], 0, 1)
    count += exchange_z(zed0, 0, 0)
    receive(count, 0)
    for other in far_ones:
        pl.semaphore_signal(far_sem, inc=1, device_id=other, device_id_type=MESH)
    def put_box(i, value):
        if is_own(i):
            box_u[i] = value
        else:
            box_u[i, 0:16] = value

    def get_box(i):
        return box_u[i] if is_own(i) else box_u[i, 0:16]

    k_slabs = []
    for i in range(14):
        put_box(i, narrow(wide_slab(raw0, corner0, zed0, far0, 0, i), i))
        k_slabs.append(narrow(wide_slab(raw0, corner0, zed0, far0, 1, i), i))
    k16 = [fold_rows(k_slabs[i]) if is_own(i) else k_slabs[i] for i in range(14)]
    for i in range(13):
        mean_x[i] = mean_of(k16[i], k16[i + 1])
    for i in range(12):
        k = k_slabs[i + 1]
        if is_own(i + 1):
            mean_y[i] = mean_of(k, up(k, 0))
        else:
            mean_y[i, 0:16] = mean_of(k, up(k, 0))
        mean_z[i] = mean_of(k16[i + 1], up(k16[i + 1], 1))
        react[i] = fold_rows(wide_slab(raw0, corner0, zed0, far0, 2, i + 1, True))
        src[i] = fold_rows(wide_slab(raw0, corner0, zed0, far0, 3, i + 1, True))
    for c in range(6):
        creact[c] = plane_sum(react[2 * c] + react[2 * c + 1])

    own = (slice(0, 8), slice(0, LINE))

    def give_field(f, slot):
        row = index_of((ROWS, LINE), 0)
        next_rows = jnp.zeros((ROWS, LINE), jnp.float32)
        next_lanes = next_rows
        for s in range(4):
            tile = pltpu.roll(zs[f, s + 1, 8:16, 0:LINE], 2 * s + 1, 0)
            next_rows = jnp.where(row // 2 == s, tile, next_rows)
            tile = pltpu.roll(zs[f, s + 1, 0:8, LINE : 2 * LINE], 2 * s + 1, 1)
            next_lanes = jnp.where(lane // 2 == s, tile, next_lanes)
        end_pack[f - 3, 0] = next_rows
        end_pack[f - 3, 1] = next_lanes
        region = (f, pl.ds(0, 6), pl.ds(0, 8), pl.ds(0, LINE))
        give([zs.at[region], end_pack.at[f - 3]], [end_zs.at[f - 3], end_halo.at[f - 3]], slot, 8)

    def beside_v(newton, j):
        if newton == 0 and j == 0:
            for i in range(6):
                zs[7, i] = k16[i + 4]
            give_field(7, 14)
        elif newton == 1:
            if j == 0:
                give_field(3, 13)
            give_field(4 + j, 13)

    def end_fields(slabs, halo):
        tall = [jnp.concatenate([slabs[s + 1], pltpu.roll(halo[0], 7 - 2 * s, 0)], axis=0) for s in range(4)]
        wide = [
            jnp.concatenate([slabs[s + 1], pltpu.roll(halo[1], LINE - 1 - 2 * s, 1)], axis=1) for s in range(4)
        ]
        return slabs, tall, wide

    def end_means():
        receive(8, 14)
        slabs, tall, wide = end_fields([end_zs[4, i] for i in range(6)], [end_halo[4, i] for i in range(2)])
        for i in range(5):
            end_x[i] = mean_of(slabs[i], slabs[i + 1])
        for s in range(4):
            end_y[s] = mean_of(tall[s], up(tall[s], 0))
            end_z[s] = mean_of(wide[s], up(wide[s], 1))

    for newton in range(NEWTON):
        coefficients()
        rows = []
        v = [v0[i] if 2 <= i < 10 else v0[i, 0:8] for i in range(12)]
        tiles = [slab[0:8] for slab in v[4:8]]
        for j in range(KRYLOV):
            at = 4 * newton + j
            precondition(v, at)
            z_tiles = [zs[(at, s + 1) + own] for s in range(4)]
            rows.append(total_of(tiles, z_tiles))
            if newton + 1 < NEWTON:
                for s in range(4):
                    raw_h[j, 5 + s, 8:16] = z_tiles[s]
            tiles = [SCALE * image(at, s) - SHIFT * tiles[s] for s in range(4)]
            rows.append(total_of(tiles, z_tiles))
            if j + 1 < KRYLOV:
                v = exchange_v(tiles, 2 * newton + j, functools.partial(beside_v, newton, j))

        counts = []

        def beside(newton=newton, counts=counts):
            if newton + 1 < NEWTON:
                pack_corners(raw_h, 1, 0, 3)
                counts.append(exchange_wide(raw_h, corner_h, 1, 0, 3, True, 1))
                pack_z([raw_h[f, 5 + s, 8:16] for f in range(2) for s in range(4)], 1, 0)
                pack_z([raw_h[2, 5 + s, 8:16] for s in range(4)], 1, 1)
                counts.append(exchange_far(raw_h, far_h, 1, 3, 1))
                counts.append(exchange_z(zed_h, 1, 1))
            else:
                give_field(6, 13)
                end_means()

        c = solve(global_sum(rows, newton, beside))
        if newton + 1 < NEWTON:
            receive(sum(counts), 1)
            for i in range(14):
                total = get_box(i)
                for j in range(3):
                    total = total + c[j] * narrow(wide_slab(raw_h, corner_h, zed_h, far_h, j, i), i)
                put_box(i, total)
                if 4 <= i < 10:
                    zs[3, i - 4] = fold_rows(total) if is_own(i) else total

    last_r.wait()
    last_s.wait()
    receive(8 * 4, 13)
    near = []
    for tiles in ([end_zs.at[:, i] for i in range(6)], [end_halo.at[:, i] for i in range(2)]):
        for tile in tiles:
            total = tile[0]
            for j in range(3):
                total = total + c[j] * tile[1 + j]
            near.append(total)
    last, tall, wide = end_fields(near[:6], near[6:])
    low_flux = None
    for s in range(-1, 4):
        flux, _ = face_terms(end_x[s + 1], last[s + 2] - last[s + 1])
        if s >= 0:
            out[0, s] = last[s + 1]
            flux_y, _ = face_terms(end_y[s], up(tall[s], 0) - tall[s])
            flux_z, _ = face_terms(end_z[s], up(wide[s], 1) - wide[s])
            out[1, s] = (
                end_rs[0, s] * last[s + 1]
                - (flux - low_flux)
                - (flux_y - down(flux_y, 0))[0:8]
                - (flux_z - down(flux_z, 1))[:, 0:LINE]
                - end_rs[1, s]
            )
        low_flux = flux
    for copy in copies:
        copy.wait_send()

    @pl.when(jnp.logical_not(alone))
    def _():
        part = dummy.at[pl.ds(0, sum(given))]
        pltpu.make_async_copy(part, part, send_sem.at[1]).wait()


def local(sizes, state, conductivity, reaction, source):
    nx, ny, nz = sizes
    plane, line = 4 * (nz // 2), (nx // 4) * ny

    def vmem(*shape):
        return pltpu.VMEM(shape, jnp.float32)

    full, half = (24, 2 * LINE), (16, 2 * LINE)
    tile = (ROWS, LINE)
    scratch = [
        vmem(4, 14, 24, LINE), vmem(2, 2, 4, 2, *tile), vmem(3, 3, 2, 2, *tile), vmem(2, 2, 2, *tile),
        vmem(3, 14, 24, LINE), vmem(2, 2, 3, 2, *tile), vmem(3, 3, 2, 2, *tile), vmem(2, 2, 2, *tile),
        vmem(4, 6, *tile), vmem(4, 4, 5, *tile), vmem(4, 2, 2, 3, *tile), vmem(2, 2, 2, *tile), vmem(2, 2, 4, 2, *tile), vmem(14, *full),
        vmem(13, *half), vmem(12, *full), vmem(12, *half), vmem(12, *half), vmem(12, *half), vmem(6, *half),
        vmem(12, *half), vmem(8, *half), vmem(7, *half), vmem(6, *half), vmem(6, *half), vmem(6, *half), vmem(6, *half),
        vmem(6, *half), vmem(5, *half), vmem(4, *half), vmem(4, *half), vmem(4, *half), vmem(4, *half),
        vmem(8, 6, *half), vmem(2, 3, 1, LINE), vmem(2, 1, 1, LINE), vmem(2, plane - 1, 1, LINE), vmem(2, line - 1, 1, LINE),
        vmem(160, *tile),
        vmem(5, 6, *tile), vmem(5, 2, *tile), vmem(5, 2, *tile), vmem(5, *tile), vmem(4, 16, LINE), vmem(4, ROWS, 2 * LINE), vmem(2, 4, *tile),
        pltpu.SemaphoreType.DMA((4,)), pltpu.SemaphoreType.DMA((16,)), pltpu.SemaphoreType.REGULAR,
    ]
    spec = pl.BlockSpec(memory_space=pltpu.MemorySpace.HBM)
    both = pl.pallas_call(
        functools.partial(kernel, sizes),
        out_shape=jax.ShapeDtypeStruct((2, *state.shape), jnp.float32),
        in_specs=[spec] * 4,
        out_specs=pl.BlockSpec(memory_space=pltpu.VMEM),
        scratch_shapes=scratch,
        compiler_params=pltpu.CompilerParams(
            collective_id=0, has_side_effects=True, vmem_limit_bytes=61 * 1024 * 1024
        ),
    )(state, conductivity, reaction, source)
    return both[0], both[1]


def solution(mesh):
    sizes = tuple(mesh.shape[name] for name in ("gx", "gy", "gz"))
    placed = P("gx", "gy", "gz")
    return jax.shard_map(
        functools.partial(local, sizes),
        mesh=mesh,
        in_specs=(placed,) * 4,
        out_specs=(placed, placed),
        check_vma=False,
    )
```

```python
import functools

import jax
import jax.numpy as jnp
from jax import lax
from jax.experimental import pallas as pl
from jax.experimental.pallas import tpu as pltpu
from jax.sharding import PartitionSpec as P

NEWTON = 2
KRYLOV = 3
EPS_SQUARE = 0.25
SCALE, SHIFT = 0.7, 1.0
MESH = pl.DeviceIdType.MESH

LINE = 128
ROWS = 8


def chebyshev_pair(low):
    centre = (2.0 + low) / 2.0
    half_width = (2.0 - low) / 2.0
    sigma = centre / half_width
    rho = 1.0 / sigma
    rho_new = 1.0 / (2.0 * sigma - rho)
    last = 2.0 * rho_new / half_width
    return (1.0 + rho_new * rho) / centre + last * (1.0 - 1.0 / centre), last / centre


FINE_OWN, FINE_NEAR = chebyshev_pair(0.3)
COARSE_OWN, COARSE_NEAR = chebyshev_pair(0.05)

CROSS = [(0, 0), (1, 0), (-1, 0), (0, 1), (0, -1)]
CORNERS = [(1, 1), (1, -1), (-1, 1), (-1, -1)]


def up(field, axis):
    return pltpu.roll(field, field.shape[axis] - 1, axis)


def down(field, axis):
    return pltpu.roll(field, 1, axis)


def index_of(shape, axis):
    return lax.broadcasted_iota(jnp.int32, shape, axis)


def face_terms(mean_k, difference):
    square = difference * difference
    inverse_root = lax.rsqrt(EPS_SQUARE + square)
    root = (EPS_SQUARE + square) * inverse_root
    return mean_k * root * difference, mean_k * (EPS_SQUARE + 2.0 * square) * inverse_root


def mean_of(one, other):
    return 2.0 * one * other / (one + other)


def fold_rows(field):
    row = index_of((ROWS, field.shape[1]), 0)
    return jnp.concatenate([field[8:16], jnp.where(row < 4, field[16:24], field[0:8])], axis=0)


def pair_sum(field, axis):
    odd = lax.rem(index_of(field.shape, axis), 2) == 1
    return field + jnp.where(odd, down(field, axis), up(field, axis))


def plane_sum(field):
    return pair_sum(pair_sum(field, 0), 1)


def kernel(
    sizes, u_ref, k_ref, r_ref, s_ref, out,
    raw0, corner0, zed0, far0, raw_h, corner_h, zed_h, far_h, v_out, v_face, v_edge, pack, corner_pack, box_u, box_z, mean_x, mean_y, mean_z, react, src,
    creact, v0, inv, wx, wyu, wyl, wzu, wzl, cinv, cwx, cwyu, cwyl, cwzu, cwzl, zs, sums, got1, got2, got3, dummy,
    end_zs, end_pack, end_halo, end_x, end_y, end_z, end_rs, send_sem, recv_sem, far_sem,
):
    nx, ny, nz = sizes
    mx, my, mz = lax.axis_index("gx"), lax.axis_index("gy"), lax.axis_index("gz")

    group, place_y = mx // 4, lax.rem(mx, 4)
    bx, by = group * 4 + my, place_y
    partner = (group * 4 + my, place_y, mz)
    alone = my == place_y

    def block_at(dx, dy, dz):
        x, y = lax.rem(bx + dx + nx, nx), lax.rem(by + dy + ny, ny)
        return ((x // 4) * 4 + y, lax.rem(x, 4), lax.rem(mz + dz + nz, nz))

    core_line = [(mx, my, (mz // 2) * 2 + 1 - lax.rem(mz, 2))]
    def around(step, size):
        return min(step, size - step)

    chips = nz // 2
    plane_line = []
    steps = [(dy, dx) for dy in range(4) for dx in range(chips)][1:]
    for dy, dx in sorted(steps, key=lambda d: -around(d[0], 4) - around(d[1], chips)):
        x = lax.rem(mz // 2 + dx, chips)
        plane_line.append(((mx // 4) * 4 + lax.rem(mx + dy, 4), my, x * 2 + lax.rem(mz, 2)))
    line = (nx // 4) * ny
    at = (mx // 4) * ny + my
    long_line = []
    for step in sorted(range(1, line), key=lambda d: -around(d, line)):
        there = lax.rem(at + step, line)
        long_line.append(((there // ny) * 4 + lax.rem(mx, 4), lax.rem(there, ny), mz))

    offsets = [(dx, dy, dz) for dx in (-1, 0, 1) for dy in (-1, 0, 1) for dz in (-1, 0, 1)]
    offsets = [d for d in offsets if d != (0, 0, 0)]
    offsets += [(dx, 0, dz) for dx in (2, -2) for dz in (-1, 0, 1)]

    barrier = pltpu.get_barrier_semaphore()
    partners = [block_at(*d) for d in offsets]
    far_ones = [(lax.rem(mx + step, nx), my, mz) for step in (4, nx - 4)]
    far_ones += [(mx, my, lax.rem(mz + step, nz)) for step in (2, nz - 2)]

    @pl.when(jnp.logical_not(alone))
    def _():
        pl.semaphore_signal(barrier, inc=1, device_id=partner, device_id_type=MESH)

    for other in partners:
        pl.semaphore_signal(barrier, inc=1, device_id=other, device_id_type=MESH)

    lane = index_of((ROWS, LINE), 1)
    copies = []

    def send(source, target, slot, device):
        copy = pltpu.make_async_remote_copy(
            source, target, send_sem.at[0], recv_sem.at[slot], device_id=device, device_id_type=MESH
        )
        copy.start()
        copies.append(copy)

    def receive(tiles, slot):
        part = dummy.at[pl.ds(0, tiles)]
        pltpu.make_async_copy(part, part, recv_sem.at[slot]).wait()

    def pack_z(tiles, place, at):
        low = jnp.zeros((ROWS, LINE), jnp.float32)
        high = low
        for g, tile in enumerate(tiles):
            mine = lane // 16 == g
            low = jnp.where(mine, tile if g == 0 else pltpu.roll(tile, 16 * g, 1), low)
            shift = (16 * g + 16) % LINE
            high = jnp.where(mine, pltpu.roll(tile, shift, 1) if shift else tile, high)
        pack[place, 0, at] = low
        pack[place, 1, at] = high

    def unpack_z(low_tiles, high_tiles, g):
        t, g = divmod(g, 8)
        shift = (LINE - 16 * g) % LINE
        above = pltpu.roll(low_tiles[t], shift, 1) if shift else low_tiles[t]
        shift = (LINE - 16 - 16 * g) % LINE
        below = pltpu.roll(high_tiles[t], shift, 1) if shift else high_tiles[t]
        return jnp.where(lane < 64, above, below)

    def pack_corners(raw, place, first, fields):
        low_rows = index_of((ROWS, LINE), 0) < 4
        for f in range(first, first + fields):
            for pair in range(2):
                one, two = raw[f, 5 + 2 * pair, 8:16], raw[f, 6 + 2 * pair, 8:16]
                two = pltpu.roll(two, 4, 0)
                corner_pack[place, 1, f, pair] = jnp.where(low_rows, two, one)
                corner_pack[place, 0, f, pair] = jnp.where(low_rows, one, two)

    def exchange_wide(raw, corner, place, first, fields, all_pairs, slot):
        which = pl.ds(first, fields)
        own = (which, pl.ds(5, 4), pl.ds(8, 8))
        for dx, dy in CROSS[1:3]:
            target = (which, pl.ds(5 - 4 * dx, 4), pl.ds(8 - 8 * dy, 8))
            send(raw.at[own], raw.at[target], slot, block_at(dx, dy, 0))
        for dx, dy in CORNERS:
            pairs = pl.ds(0, 2) if all_pairs else pl.ds((1 + dx) // 2, 1)
            send(
                corner_pack.at[place, (1 + dy) // 2, which, pairs],
                corner.at[(1 - dx) // 2, (1 - dy) // 2, which, pairs],
                slot,
                block_at(dx, dy, 0),
            )
        for dx, dy in CROSS[3:]:
            target = (which, pl.ds(5 - 4 * dx, 4), pl.ds(8 - 8 * dy, 8))
            send(raw.at[own], raw.at[target], slot, block_at(dx, dy, 0))
        return 16 * fields + (8 if all_pairs else 4) * fields

    def exchange_far(raw, zed2, place, fields, slot):
        some, rows, tiles = pl.ds(0, fields), pl.ds(8, 8), (fields + 1) // 2
        send(raw.at[some, pl.ds(8, 1), rows], raw.at[some, pl.ds(0, 1), rows], slot, block_at(2, 0, 0))
        send(raw.at[some, pl.ds(5, 1), rows], raw.at[some, pl.ds(13, 1), rows], slot, block_at(-2, 0, 0))
        for dx in (2, -2):
            for dz in (1, -1):
                send(
                    pack.at[place, (1 + dz) // 2, pl.ds(0, tiles)],
                    zed2.at[(2 - dx) // 4, (1 - dz) // 2, pl.ds(0, tiles)],
                    slot,
                    block_at(dx, 0, dz),
                )
        return 2 * fields + 4 * tiles

    def exchange_z(zed, place, slot):
        for dx, dy in CORNERS + CROSS:
            for dz in (1, -1):
                send(
                    pack.at[place, (1 + dz) // 2],
                    zed.at[1 - dx, 1 - dy, (1 - dz) // 2],
                    slot,
                    block_at(dx, dy, dz),
                )
        return 36

    nothing = jnp.zeros((ROWS, LINE), jnp.float32)

    def wide_slab(raw, corner, zed, zed2, field, i, slim=False):
        outer = i in (0, 13)
        if outer or (slim and i in (1, 2, 11, 12)):
            column, s = ((i - 1) // 4, (i - 1) % 4) if not outer else (0, 3) if i == 0 else (1, 0)
            low, high = (zed2[column, 1], zed2[column, 0]) if outer else (zed[column, 1, 1], zed[column, 1, 0])
            halo = unpack_z(low, high, field * 4 + s)
            mid = jnp.concatenate([raw[field, i, 8:16], halo], axis=1)
            empty = jnp.zeros_like(mid)
            return jnp.concatenate([empty, mid, empty], axis=0)
        column, s = divmod(i - 1, 4)
        if column == 1:
            main = raw[field, i]
        else:
            ends_y = []
            for y in range(2):
                packed = corner[column // 2, y, field, s // 2]
                ends_y.append(pltpu.roll(packed, 4, 0) if s % 2 else packed)
            main = jnp.concatenate([ends_y[0], raw[field, i, 8:16], ends_y[1]], axis=0)
        g = field * 4 + s
        halo = [unpack_z(zed[column, y, 1], zed[column, y, 0], g) for y in range(3)]
        return jnp.concatenate([main, jnp.concatenate(halo, axis=0)], axis=1)

    def exchange_v(tiles, e, between):
        slot = 2 + e
        packed = nothing
        for s in range(4):
            v_out[e, 1 + s] = tiles[s][:, 0:LINE]
            part = pltpu.roll(tiles[s][:, LINE : 2 * LINE], 16 * s + 8, 1)
            packed = jnp.where(lane // 16 == s, part, packed)
        v_out[e, 0] = packed
        v_out[e, 5] = packed
        for dx, dy in CORNERS:
            send(
                v_out.at[e, pl.ds(3 if dx > 0 else 0, 3)],
                v_edge.at[e, (1 - dx) // 2, (1 - dy) // 2],
                slot,
                block_at(dx, dy, 0),
            )
        for n, (dx, dy) in enumerate(CROSS[1:]):
            send(v_out.at[e, pl.ds(1, 5)], v_face.at[e, n], slot, block_at(dx, dy, 0))
        between()
        receive(12 + 20, slot)
        row = index_of((ROWS, LINE), 0)

        def spread(zeds, s):
            return pltpu.roll(zeds, LINE - 8 - 16 * s, 1)

        slabs = []
        for i in range(12):
            column, s = divmod(i, 4)
            if column == 1:
                mid = tiles[s]
                side = [
                    jnp.where(row < 4, v_face[e, 3, s], v_face[e, 2, s]),
                    jnp.where(row < 4, spread(v_face[e, 3, 4], s), spread(v_face[e, 2, 4], s)),
                ]
            else:
                face = 0 if column == 0 else 1
                mid = jnp.concatenate([v_face[e, face, s], spread(v_face[e, face, 4], s)], axis=1)
                side = [nothing, nothing]
                if 2 <= i < 10:
                    at = s - 2 if column == 0 else s + 1
                    z_at = 2 if column == 0 else 0
                    low, high = v_edge.at[e, face, 0], v_edge.at[e, face, 1]
                    side = [
                        jnp.where(row < 4, high[at], low[at]),
                        jnp.where(row < 4, spread(high[z_at], s), spread(low[z_at], s)),
                    ]
            slabs.append(jnp.concatenate([mid, jnp.concatenate(side, axis=1)], axis=0))
        return slabs

    def is_own(i):
        return 5 <= i < 9

    def narrow(slab, i):
        return slab if is_own(i) else fold_rows(slab)

    def put(ref, i, value, whole):
        if whole:
            ref[i] = value
        else:
            ref[i, 0:8] = value[0:8]

    def coefficients():
        u16 = [fold_rows(box_u[i]) if is_own(i) else box_u[i, 0:16] for i in range(14)]
        face_x = [face_terms(mean_x[i], u16[i + 1] - u16[i]) for i in range(13)]
        cface = []
        for j in range(7):
            cface.append(plane_sum(face_x[2 * j][1]))
            if 1 <= j < 6:
                put(cwx, j - 1, cface[j], 1 < j < 5)
        for i in range(7):
            put(wx, i, face_x[i + 3][1], 0 < i < 6)
        odd_row = lax.rem(index_of((16, 2 * LINE), 0), 2) == 1
        odd_lane = lax.rem(index_of((16, 2 * LINE), 1), 2) == 1
        for c in range(6):
            pairs = None
            for half in range(2):
                i = 2 * c + half
                u, re = u16[i + 1], react[i]
                if is_own(i + 1):
                    tall = box_u[i + 1]
                    flux, w = face_terms(mean_y[i], up(tall, 0) - tall)
                    flux_y, w_y = fold_rows(flux), fold_rows(w)
                    low_flux_y, low_y = fold_rows(down(flux, 0)), fold_rows(down(w, 0))
                else:
                    flux_y, w_y = face_terms(mean_y[i, 0:16], up(u, 0) - u)
                    low_flux_y, low_y = down(flux_y, 0), down(w_y, 0)
                flux_z, w_z = face_terms(mean_z[i], up(u, 1) - u)
                low_z = down(w_z, 1)
                force = (
                    src[i]
                    - re * u
                    + (face_x[i + 1][0] - face_x[i][0])
                    + (flux_y - low_flux_y)
                    + (flux_z - down(flux_z, 1))
                )
                put(v0, i, force, 2 <= i < 10)
                if 2 <= i < 10:
                    diagonal = re + face_x[i + 1][1] + face_x[i][1] + w_y + low_y + w_z + low_z
                    put(inv, i - 2, 1.0 / diagonal, 3 <= i < 9)
                if 3 <= i < 9:
                    for ref, weight in ((wyu, w_y), (wyl, low_y), (wzu, w_z), (wzl, low_z)):
                        put(ref, i - 3, weight, 4 <= i < 8)
                now = (w_y, low_y, w_z)
                pairs = now if half == 0 else tuple(one + two for one, two in zip(pairs, now))
            pair_y, pair_low, pair_z = pairs
            sum_y = pair_sum(jnp.where(odd_row, pair_y, up(pair_y, 0)), 1)
            sum_z = pair_sum(jnp.where(odd_lane, pair_z, up(pair_z, 1)), 0)
            if c in (2, 3):
                low_y = pair_sum(jnp.where(odd_row, down(pair_low, 0), pair_low), 1)
            else:
                low_y = pltpu.roll(sum_y, 2, 0)
            low_z = pltpu.roll(sum_z, 2, 1)
            diagonal = creact[c] + cface[c] + cface[c + 1] + sum_y + low_y + sum_z + low_z
            put(cinv, c, 1.0 / diagonal, 1 <= c < 5)
            if 1 <= c < 5:
                for ref, weight in ((cwyu, sum_y), (cwyl, low_y), (cwzu, sum_z), (cwzl, low_z)):
                    put(ref, c - 1, weight, 2 <= c < 4)

    def precondition(v, j):
        def part(whole):
            return slice(0, 16) if whole else slice(0, 8)

        own = [inv[i, part(0 < i < 7)] * v[i + 2][part(0 < i < 7)] for i in range(8)]
        coarse = []
        for c in range(6):
            rows = part(1 <= c < 5)
            coarse.append(cinv[c, rows] * plane_sum(v[2 * c][rows] + v[2 * c + 1][rows]))
        coarse_z = []
        for c in range(4):
            q, rows = coarse[c + 1], part(1 <= c < 3)
            near = (
                cwx[c, rows] * coarse[c][rows]
                + cwx[c + 1, rows] * coarse[c + 2][rows]
                + cwyu[c, rows] * pltpu.roll(q, 14, 0)[rows]
                + cwyl[c, rows] * pltpu.roll(q, 2, 0)[rows]
                + cwzu[c, rows] * pltpu.roll(q[rows], 2 * LINE - 2, 1)
                + cwzl[c, rows] * pltpu.roll(q[rows], 2, 1)
            )
            coarse_z.append(COARSE_OWN * q[rows] + COARSE_NEAR * (cinv[c + 1, rows] * near))
        for i in range(6):
            q, rows = own[i + 1], part(0 < i < 5)
            near = (
                wx[i, rows] * own[i][rows]
                + wx[i + 1, rows] * own[i + 2][rows]
                + wyu[i, rows] * up(q, 0)[rows]
                + wyl[i, rows] * down(q, 0)[rows]
                + wzu[i, rows] * up(q[rows], 1)
                + wzl[i, rows] * down(q[rows], 1)
            )
            zs[j, i, rows] = (
                FINE_OWN * q[rows] + FINE_NEAR * (inv[i + 1, rows] * near) + coarse_z[(i + 1) // 2][rows]
            )

    def image(j, s):
        i = s + 1
        tall = zs[j, i]
        here = tall[0:8]
        total = react[i + 3, 0:8] * here
        for weight, other in (
            (wx[i, 0:8], zs[j, i - 1, 0:8]),
            (wx[i + 1, 0:8], zs[j, i + 1, 0:8]),
            (wyu[i, 0:8], up(tall, 0)[0:8]),
            (wyl[i, 0:8], down(tall, 0)[0:8]),
            (wzu[i, 0:8], up(here, 1)),
            (wzl[i, 0:8], down(here, 1)),
        ):
            total = total + weight * (here - other)
        return total

    group_of = lane // 16

    def gather(total, moments):
        for n, tile in moments:
            for shift in (64, 32, 16):
                tile = tile + pltpu.roll(tile, shift, 1)
            total = total + jnp.where(group_of == n, tile, 0.0)
        return total

    def global_sum(tile, which, beside):
        group = index_of((1, LINE), 1) // 16
        mixed = jnp.sum(tile, axis=0, keepdims=True)
        phases = ((core_line, got1), (plane_line, got2), (long_line, got3))
        for phase, (partners, got) in enumerate(phases):
            if phase == 1 and which == 0:
                pl.semaphore_wait(far_sem, 4)
            sums[which, phase] = mixed
            slot = 6 + 3 * which + phase
            for n, partner in enumerate(partners):
                send(sums.at[which, phase], got.at[which, n], slot, partner)
            beside(phase)
            part = got.at[which]
            pltpu.make_async_copy(part, part, recv_sem.at[slot]).wait()
            mixed = mixed + jnp.sum(got[which], axis=0)
        return [jnp.sum(jnp.where(group == n, mixed, 0.0), axis=1, keepdims=True) for n in range(6)]

    def solve(m):
        h = [(m[n + 1] + SHIFT * m[n]) * (1.0 / SCALE) for n in range(5)]

        def inverse(pivot, of):
            good = pivot > 1e-6 * of
            return jnp.where(good, 1.0 / jnp.where(good, pivot, 1.0), 0.0)

        i0 = inverse(h[0], jnp.zeros_like(h[0]))
        l1, l2 = h[1] * i0, h[2] * i0
        i1 = inverse(h[2] - l1 * h[1], h[2])
        h21 = h[3] - l2 * h[1]
        l21 = h21 * i1
        i2 = inverse(h[4] - l2 * h[2] - l21 * h21, h[4])
        y0 = m[0]
        y1 = m[1] - l1 * y0
        y2 = m[2] - l2 * y0 - l21 * y1
        c2 = y2 * i2
        c1 = y1 * i1 - l21 * c2
        c0 = y0 * i0 - l1 * c1 - l2 * c2
        return c0, c1, c2

    def total_of(tiles, others):
        total = tiles[0][:, 0:LINE] * others[0]
        for s in range(1, 4):
            total = total + tiles[s][:, 0:LINE] * others[s]
        return total

    given = []

    def give(sources, targets, slot, tiles):
        @pl.when(alone)
        def _():
            for source, target in zip(sources, targets):
                pltpu.make_async_copy(source, target, recv_sem.at[slot]).start()

        @pl.when(jnp.logical_not(alone))
        def _():
            for source, target in zip(sources, targets):
                pltpu.make_async_remote_copy(
                    source, target, send_sem.at[1], recv_sem.at[slot], device_id=partner, device_id_type=MESH
                ).start()

        given.append(tiles)

    pl.semaphore_wait(barrier, len(partners) + 1 - alone.astype(jnp.int32))
    homes = [raw0.at[f, pl.ds(5, 4), pl.ds(8, 8)] for f in range(4)]
    give([u_ref, k_ref], homes[:2], 12, 8)
    give([r_ref, s_ref], homes[2:], 15, 8)
    last_r = pltpu.make_async_copy(r_ref, end_rs.at[0], send_sem.at[2])
    last_s = pltpu.make_async_copy(s_ref, end_rs.at[1], send_sem.at[3])
    last_r.start()
    last_s.start()
    receive(8, 12)
    pack_corners(raw0, 0, 0, 2)
    count = exchange_wide(raw0, corner0, 0, 0, 2, True, 0)
    pack_z([raw0[f, 5 + s, 8:16] for f in range(2) for s in range(4)], 0, 0)
    count += exchange_far(raw0, far0, 0, 2, 0)
    receive(8, 15)
    pack_corners(raw0, 0, 2, 2)
    count += exchange_wide(raw0, corner0, 0, 2, 2, False, 0)
    pack_z([raw0[f, 5 + s, 8:16] for f in range(2, 4) for s in range(4)], 0, 1)
    count += exchange_z(zed0, 0, 0)
    receive(count, 0)
    for other in far_ones:
        pl.semaphore_signal(far_sem, inc=1, device_id=other, device_id_type=MESH)
    def put_box(i, value):
        if is_own(i):
            box_u[i] = value
        else:
            box_u[i, 0:16] = value

    def get_box(i):
        return box_u[i] if is_own(i) else box_u[i, 0:16]

    k_slabs = []
    for i in range(14):
        put_box(i, narrow(wide_slab(raw0, corner0, zed0, far0, 0, i), i))
        k_slabs.append(narrow(wide_slab(raw0, corner0, zed0, far0, 1, i), i))
    k16 = [fold_rows(k_slabs[i]) if is_own(i) else k_slabs[i] for i in range(14)]
    for i in range(13):
        mean_x[i] = mean_of(k16[i], k16[i + 1])
    for i in range(12):
        k = k_slabs[i + 1]
        if is_own(i + 1):
            mean_y[i] = mean_of(k, up(k, 0))
        else:
            mean_y[i, 0:16] = mean_of(k, up(k, 0))
        mean_z[i] = mean_of(k16[i + 1], up(k16[i + 1], 1))
        react[i] = fold_rows(wide_slab(raw0, corner0, zed0, far0, 2, i + 1, True))
        src[i] = fold_rows(wide_slab(raw0, corner0, zed0, far0, 3, i + 1, True))
    for c in range(6):
        creact[c] = plane_sum(react[2 * c] + react[2 * c + 1])

    own = (slice(0, 8), slice(0, LINE))

    def give_field(f, slot):
        row = index_of((ROWS, LINE), 0)
        next_rows = jnp.zeros((ROWS, LINE), jnp.float32)
        next_lanes = next_rows
        for s in range(4):
            tile = pltpu.roll(zs[f, s + 1, 8:16, 0:LINE], 2 * s + 1, 0)
            next_rows = jnp.where(row // 2 == s, tile, next_rows)
            tile = pltpu.roll(zs[f, s + 1, 0:8, LINE : 2 * LINE], 2 * s + 1, 1)
            next_lanes = jnp.where(lane // 2 == s, tile, next_lanes)
        end_pack[f - 3, 0] = next_rows
        end_pack[f - 3, 1] = next_lanes
        region = (f, pl.ds(0, 6), pl.ds(0, 8), pl.ds(0, LINE))
        give([zs.at[region], end_pack.at[f - 3]], [end_zs.at[f - 3], end_halo.at[f - 3]], slot, 8)

    def beside_v(newton, j):
        if newton == 0 and j == 0:
            for i in range(6):
                zs[7, i] = k16[i + 4]
            give_field(7, 14)
        elif newton == 1:
            if j == 0:
                give_field(3, 13)
            give_field(4 + j, 13)

    def end_fields(slabs, halo):
        tall = [jnp.concatenate([slabs[s + 1], pltpu.roll(halo[0], 7 - 2 * s, 0)], axis=0) for s in range(4)]
        wide = [
            jnp.concatenate([slabs[s + 1], pltpu.roll(halo[1], LINE - 1 - 2 * s, 1)], axis=1) for s in range(4)
        ]
        return slabs, tall, wide

    def end_means():
        receive(8, 14)
        slabs, tall, wide = end_fields([end_zs[4, i] for i in range(6)], [end_halo[4, i] for i in range(2)])
        for i in range(5):
            end_x[i] = mean_of(slabs[i], slabs[i + 1])
        for s in range(4):
            end_y[s] = mean_of(tall[s], up(tall[s], 0))
            end_z[s] = mean_of(wide[s], up(wide[s], 1))

    for newton in range(NEWTON):
        coefficients()
        sofar = []
        moments = []
        v = [v0[i] if 2 <= i < 10 else v0[i, 0:8] for i in range(12)]
        tiles = [slab[0:8] for slab in v[4:8]]
        for j in range(KRYLOV):
            at = 4 * newton + j
            precondition(v, at)
            z_tiles = [zs[(at, s + 1) + own] for s in range(4)]
            moments.append((2 * j, total_of(tiles, z_tiles)))
            if newton + 1 < NEWTON:
                for s in range(4):
                    raw_h[j, 5 + s, 8:16] = z_tiles[s]
            tiles = [SCALE * image(at, s) - SHIFT * tiles[s] for s in range(4)]
            moments.append((2 * j + 1, total_of(tiles, z_tiles)))
            if j + 1 < KRYLOV:

                def meanwhile(newton=newton, j=j, moments=moments):
                    sofar.append(gather(sofar[-1] if j else nothing, moments))
                    beside_v(newton, j)

                v = exchange_v(tiles, 2 * newton + j, meanwhile)
                moments = []

        counts = []

        def beside(phase, newton=newton, counts=counts):
            if phase == 1 and newton + 1 < NEWTON:
                pack_corners(raw_h, 1, 0, 3)
                counts.append(exchange_wide(raw_h, corner_h, 1, 0, 3, True, 1))
                pack_z([raw_h[f, 5 + s, 8:16] for f in range(2) for s in range(4)], 1, 0)
                pack_z([raw_h[2, 5 + s, 8:16] for s in range(4)], 1, 1)
                counts.append(exchange_far(raw_h, far_h, 1, 3, 1))
                counts.append(exchange_z(zed_h, 1, 1))
            elif phase == 1:
                give_field(6, 13)
                end_means()
            elif phase == 2 and newton + 1 < NEWTON:
                receive(sum(counts), 1)
                for j in range(3):
                    for i in range(14):
                        slab = narrow(wide_slab(raw_h, corner_h, zed_h, far_h, j, i), i)
                        if is_own(i):
                            box_z[j, i] = slab
                        else:
                            box_z[j, i, 0:16] = slab

        c = solve(global_sum(gather(sofar[-1], moments), newton, beside))
        if newton + 1 < NEWTON:
            for i in range(14):
                rows = slice(0, 24 if is_own(i) else 16)
                total = get_box(i)
                for j in range(3):
                    total = total + c[j] * box_z[j, i, rows]
                put_box(i, total)
                if 4 <= i < 10:
                    zs[3, i - 4] = fold_rows(total) if is_own(i) else total

    last_r.wait()
    last_s.wait()
    receive(8 * 4, 13)
    near = []
    for tiles in ([end_zs.at[:, i] for i in range(6)], [end_halo.at[:, i] for i in range(2)]):
        for tile in tiles:
            total = tile[0]
            for j in range(3):
                total = total + c[j] * tile[1 + j]
            near.append(total)
    last, tall, wide = end_fields(near[:6], near[6:])
    low_flux = None
    for s in range(-1, 4):
        flux, _ = face_terms(end_x[s + 1], last[s + 2] - last[s + 1])
        if s >= 0:
            out[0, s] = last[s + 1]
            flux_y, _ = face_terms(end_y[s], up(tall[s], 0) - tall[s])
            flux_z, _ = face_terms(end_z[s], up(wide[s], 1) - wide[s])
            out[1, s] = (
                end_rs[0, s] * last[s + 1]
                - (flux - low_flux)
                - (flux_y - down(flux_y, 0))[0:8]
                - (flux_z - down(flux_z, 1))[:, 0:LINE]
                - end_rs[1, s]
            )
        low_flux = flux
    for copy in copies:
        copy.wait_send()

    @pl.when(jnp.logical_not(alone))
    def _():
        part = dummy.at[pl.ds(0, sum(given))]
        pltpu.make_async_copy(part, part, send_sem.at[1]).wait()


def local(sizes, state, conductivity, reaction, source):
    nx, ny, nz = sizes
    plane, line = 4 * (nz // 2), (nx // 4) * ny

    def vmem(*shape):
        return pltpu.VMEM(shape, jnp.float32)

    full, half = (24, 2 * LINE), (16, 2 * LINE)
    tile = (ROWS, LINE)
    scratch = [
        vmem(4, 14, 24, LINE), vmem(2, 2, 4, 2, *tile), vmem(3, 3, 2, 2, *tile), vmem(2, 2, 2, *tile),
        vmem(3, 14, 24, LINE), vmem(2, 2, 3, 2, *tile), vmem(3, 3, 2, 2, *tile), vmem(2, 2, 2, *tile),
        vmem(4, 6, *tile), vmem(4, 4, 5, *tile), vmem(4, 2, 2, 3, *tile), vmem(2, 2, 2, *tile), vmem(2, 2, 4, 2, *tile), vmem(14, *full), vmem(3, 14, *full),
        vmem(13, *half), vmem(12, *full), vmem(12, *half), vmem(12, *half), vmem(12, *half), vmem(6, *half),
        vmem(12, *half), vmem(8, *half), vmem(7, *half), vmem(6, *half), vmem(6, *half), vmem(6, *half), vmem(6, *half),
        vmem(6, *half), vmem(5, *half), vmem(4, *half), vmem(4, *half), vmem(4, *half), vmem(4, *half),
        vmem(8, 6, *half), vmem(2, 3, 1, LINE), vmem(2, 1, 1, LINE), vmem(2, plane - 1, 1, LINE), vmem(2, line - 1, 1, LINE),
        vmem(160, *tile),
        vmem(5, 6, *tile), vmem(5, 2, *tile), vmem(5, 2, *tile), vmem(5, *tile), vmem(4, 16, LINE), vmem(4, ROWS, 2 * LINE), vmem(2, 4, *tile),
        pltpu.SemaphoreType.DMA((4,)), pltpu.SemaphoreType.DMA((16,)), pltpu.SemaphoreType.REGULAR,
    ]
    spec = pl.BlockSpec(memory_space=pltpu.MemorySpace.HBM)
    both = pl.pallas_call(
        functools.partial(kernel, sizes),
        out_shape=jax.ShapeDtypeStruct((2, *state.shape), jnp.float32),
        in_specs=[spec] * 4,
        out_specs=pl.BlockSpec(memory_space=pltpu.VMEM),
        scratch_shapes=scratch,
        compiler_params=pltpu.CompilerParams(
            collective_id=0, has_side_effects=True, vmem_limit_bytes=61 * 1024 * 1024
        ),
    )(state, conductivity, reaction, source)
    return both[0], both[1]


def solution(mesh):
    sizes = tuple(mesh.shape[name] for name in ("gx", "gy", "gz"))
    placed = P("gx", "gy", "gz")
    return jax.shard_map(
        functools.partial(local, sizes),
        mesh=mesh,
        in_specs=(placed,) * 4,
        out_specs=(placed, placed),
        check_vma=False,
    )
```

```python
import functools

import jax
import jax.numpy as jnp
from jax import lax
from jax.experimental import pallas as pl
from jax.experimental.pallas import tpu as pltpu
from jax.sharding import PartitionSpec as P

NEWTON = 2
KRYLOV = 3
EPS_SQUARE = 0.25
SCALE, SHIFT = 0.7, 1.0
MESH = pl.DeviceIdType.MESH

LINE = 128
ROWS = 8


def chebyshev_pair(low):
    centre = (2.0 + low) / 2.0
    half_width = (2.0 - low) / 2.0
    sigma = centre / half_width
    rho = 1.0 / sigma
    rho_new = 1.0 / (2.0 * sigma - rho)
    last = 2.0 * rho_new / half_width
    return (1.0 + rho_new * rho) / centre + last * (1.0 - 1.0 / centre), last / centre


FINE_OWN, FINE_NEAR = chebyshev_pair(0.3)
COARSE_OWN, COARSE_NEAR = chebyshev_pair(0.05)

CROSS = [(0, 0), (1, 0), (-1, 0), (0, 1), (0, -1)]
CORNERS = [(1, 1), (1, -1), (-1, 1), (-1, -1)]


def up(field, axis):
    return pltpu.roll(field, field.shape[axis] - 1, axis)


def down(field, axis):
    return pltpu.roll(field, 1, axis)


def index_of(shape, axis):
    return lax.broadcasted_iota(jnp.int32, shape, axis)


def face_terms(mean_k, difference):
    square = difference * difference
    inverse_root = lax.rsqrt(EPS_SQUARE + square)
    root = (EPS_SQUARE + square) * inverse_root
    return mean_k * root * difference, mean_k * (EPS_SQUARE + 2.0 * square) * inverse_root


def mean_of(one, other):
    return 2.0 * one * other / (one + other)


def fold_rows(field):
    row = index_of((ROWS, field.shape[1]), 0)
    return jnp.concatenate([field[8:16], jnp.where(row < 4, field[16:24], field[0:8])], axis=0)


def pair_sum(field, axis):
    odd = lax.rem(index_of(field.shape, axis), 2) == 1
    return field + jnp.where(odd, down(field, axis), up(field, axis))


def plane_sum(field):
    return pair_sum(pair_sum(field, 0), 1)


def kernel(
    sizes, u_ref, k_ref, r_ref, s_ref, out,
    raw0, corner0, zed0, far0, raw_h, corner_h, zed_h, far_h, v_out_x, v_out_y, v_face_x, v_face_y, v_edge, pack, corner_pack, box_u, box_z, mean_x, mean_y, mean_z, react, src,
    creact, v0, inv, wx, wyu, wyl, wzu, wzl, cinv, cwx, cwyu, cwyl, cwzu, cwzl, zs, sums, got1, got2, got3, dummy,
    end_zs, end_pack, end_halo, end_x, end_y, end_z, end_rs, send_sem, recv_sem, far_sem,
):
    nx, ny, nz = sizes
    mx, my, mz = lax.axis_index("gx"), lax.axis_index("gy"), lax.axis_index("gz")

    group, place_y = mx // 4, lax.rem(mx, 4)
    bx, by = group * 4 + my, place_y
    partner = (group * 4 + my, place_y, mz)
    alone = my == place_y

    def block_at(dx, dy, dz):
        x, y = lax.rem(bx + dx + nx, nx), lax.rem(by + dy + ny, ny)
        return ((x // 4) * 4 + y, lax.rem(x, 4), lax.rem(mz + dz + nz, nz))

    core_line = [(mx, my, (mz // 2) * 2 + 1 - lax.rem(mz, 2))]
    def around(step, size):
        return min(step, size - step)

    chips = nz // 2
    plane_line = []
    steps = [(dy, dx) for dy in range(4) for dx in range(chips)][1:]
    for dy, dx in sorted(steps, key=lambda d: -around(d[0], 4) - around(d[1], chips)):
        x = lax.rem(mz // 2 + dx, chips)
        plane_line.append(((mx // 4) * 4 + lax.rem(mx + dy, 4), my, x * 2 + lax.rem(mz, 2)))
    line = (nx // 4) * ny
    at = (mx // 4) * ny + my
    long_line = []
    for step in sorted(range(1, line), key=lambda d: -around(d, line)):
        there = lax.rem(at + step, line)
        long_line.append(((there // ny) * 4 + lax.rem(mx, 4), lax.rem(there, ny), mz))

    offsets = [(dx, dy, dz) for dx in (-1, 0, 1) for dy in (-1, 0, 1) for dz in (-1, 0, 1)]
    offsets = [d for d in offsets if d != (0, 0, 0)]
    offsets += [(dx, 0, dz) for dx in (2, -2) for dz in (-1, 0, 1)]

    barrier = pltpu.get_barrier_semaphore()
    partners = [block_at(*d) for d in offsets]
    far_ones = [(lax.rem(mx + step, nx), my, mz) for step in (4, nx - 4)]
    far_ones += [(mx, my, lax.rem(mz + step, nz)) for step in (2, nz - 2)]

    @pl.when(jnp.logical_not(alone))
    def _():
        pl.semaphore_signal(barrier, inc=1, device_id=partner, device_id_type=MESH)

    for other in partners:
        pl.semaphore_signal(barrier, inc=1, device_id=other, device_id_type=MESH)

    lane = index_of((ROWS, LINE), 1)
    copies = []

    def send(source, target, slot, device):
        copy = pltpu.make_async_remote_copy(
            source, target, send_sem.at[0], recv_sem.at[slot], device_id=device, device_id_type=MESH
        )
        copy.start()
        copies.append(copy)

    def receive(tiles, slot):
        part = dummy.at[pl.ds(0, tiles)]
        pltpu.make_async_copy(part, part, recv_sem.at[slot]).wait()

    def pack_z(tiles, place, at):
        low = jnp.zeros((ROWS, LINE), jnp.float32)
        high = low
        for g, tile in enumerate(tiles):
            mine = lane // 16 == g
            low = jnp.where(mine, tile if g == 0 else pltpu.roll(tile, 16 * g, 1), low)
            shift = (16 * g + 16) % LINE
            high = jnp.where(mine, pltpu.roll(tile, shift, 1) if shift else tile, high)
        pack[place, 0, at] = low
        pack[place, 1, at] = high

    def unpack_z(low_tiles, high_tiles, g):
        t, g = divmod(g, 8)
        shift = (LINE - 16 * g) % LINE
        above = pltpu.roll(low_tiles[t], shift, 1) if shift else low_tiles[t]
        shift = (LINE - 16 - 16 * g) % LINE
        below = pltpu.roll(high_tiles[t], shift, 1) if shift else high_tiles[t]
        return jnp.where(lane < 64, above, below)

    def pack_corners(raw, place, first, fields):
        low_rows = index_of((ROWS, LINE), 0) < 4
        for f in range(first, first + fields):
            for pair in range(2):
                one, two = raw[f, 5 + 2 * pair, 8:16], raw[f, 6 + 2 * pair, 8:16]
                two = pltpu.roll(two, 4, 0)
                corner_pack[place, 1, f, pair] = jnp.where(low_rows, two, one)
                corner_pack[place, 0, f, pair] = jnp.where(low_rows, one, two)

    def exchange_wide(raw, corner, place, first, fields, all_pairs, slot):
        which = pl.ds(first, fields)
        own = (which, pl.ds(5, 4), pl.ds(8, 8))
        for dx, dy in CROSS[1:3]:
            target = (which, pl.ds(5 - 4 * dx, 4), pl.ds(8 - 8 * dy, 8))
            send(raw.at[own], raw.at[target], slot, block_at(dx, dy, 0))
        for dx, dy in CORNERS:
            pairs = pl.ds(0, 2) if all_pairs else pl.ds((1 + dx) // 2, 1)
            send(
                corner_pack.at[place, (1 + dy) // 2, which, pairs],
                corner.at[(1 - dx) // 2, (1 - dy) // 2, which, pairs],
                slot,
                block_at(dx, dy, 0),
            )
        for dx, dy in CROSS[3:]:
            target = (which, pl.ds(5 - 4 * dx, 4), pl.ds(8 - 8 * dy, 8))
            send(raw.at[own], raw.at[target], slot, block_at(dx, dy, 0))
        return 16 * fields + (8 if all_pairs else 4) * fields

    def exchange_far(raw, zed2, place, fields, slot):
        some, rows, tiles = pl.ds(0, fields), pl.ds(8, 8), (fields + 1) // 2
        send(raw.at[some, pl.ds(8, 1), rows], raw.at[some, pl.ds(0, 1), rows], slot, block_at(2, 0, 0))
        send(raw.at[some, pl.ds(5, 1), rows], raw.at[some, pl.ds(13, 1), rows], slot, block_at(-2, 0, 0))
        for dx in (2, -2):
            for dz in (1, -1):
                send(
                    pack.at[place, (1 + dz) // 2, pl.ds(0, tiles)],
                    zed2.at[(2 - dx) // 4, (1 - dz) // 2, pl.ds(0, tiles)],
                    slot,
                    block_at(dx, 0, dz),
                )
        return 2 * fields + 4 * tiles

    def exchange_z(zed, place, slot):
        for dx, dy in CORNERS + CROSS:
            for dz in (1, -1):
                send(
                    pack.at[place, (1 + dz) // 2],
                    zed.at[1 - dx, 1 - dy, (1 - dz) // 2],
                    slot,
                    block_at(dx, dy, dz),
                )
        return 36

    nothing = jnp.zeros((ROWS, LINE), jnp.float32)

    def wide_slab(raw, corner, zed, zed2, field, i, slim=False):
        outer = i in (0, 13)
        if outer or (slim and i in (1, 2, 11, 12)):
            column, s = ((i - 1) // 4, (i - 1) % 4) if not outer else (0, 3) if i == 0 else (1, 0)
            low, high = (zed2[column, 1], zed2[column, 0]) if outer else (zed[column, 1, 1], zed[column, 1, 0])
            halo = unpack_z(low, high, field * 4 + s)
            mid = jnp.concatenate([raw[field, i, 8:16], halo], axis=1)
            empty = jnp.zeros_like(mid)
            return jnp.concatenate([empty, mid, empty], axis=0)
        column, s = divmod(i - 1, 4)
        if column == 1:
            main = raw[field, i]
        else:
            ends_y = []
            for y in range(2):
                packed = corner[column // 2, y, field, s // 2]
                ends_y.append(pltpu.roll(packed, 4, 0) if s % 2 else packed)
            main = jnp.concatenate([ends_y[0], raw[field, i, 8:16], ends_y[1]], axis=0)
        g = field * 4 + s
        halo = [unpack_z(zed[column, y, 1], zed[column, y, 0], g) for y in range(3)]
        return jnp.concatenate([main, jnp.concatenate(halo, axis=0)], axis=1)

    def exchange_v(tiles, e, between):
        slot = 2 + e
        low_rows = index_of((ROWS, LINE), 0) < 4
        mains = [tile[:, 0:LINE] for tile in tiles]
        packed = nothing
        for s in range(4):
            part = pltpu.roll(tiles[s][:, LINE : 2 * LINE], 16 * s + 8, 1)
            packed = jnp.where(lane // 16 == s, part, packed)
        for pair in range(2):
            one, two = mains[2 * pair], pltpu.roll(mains[2 * pair + 1], 4, 0)
            v_out_y[e, 1, 1 + pair] = jnp.where(low_rows, two, one)
            v_out_y[e, 0, 1 + pair] = jnp.where(low_rows, one, two)
        for way in range(2):
            v_out_y[e, way, 0] = packed
            v_out_y[e, way, 3] = packed
        for n, tile in enumerate(
            (mains[0] + mains[1], mains[2], mains[3], packed, mains[0], mains[1], mains[2] + mains[3])
        ):
            v_out_x[e, n] = tile
        for dx, dy in CORNERS:
            send(
                v_out_y.at[e, (1 + dy) // 2, pl.ds(1 + dx, 2)],
                v_edge.at[e, (1 - dx) // 2, (1 - dy) // 2],
                slot,
                block_at(dx, dy, 0),
            )
        for n, dx in enumerate((1, -1)):
            send(v_out_x.at[e, pl.ds(3 * n, 4)], v_face_x.at[e, n], slot, block_at(dx, 0, 0))
        for n, dy in enumerate((1, -1)):
            send(v_out_y.at[e, 1 - n, pl.ds(1, 3)], v_face_y.at[e, n], slot, block_at(0, dy, 0))
        between()
        receive(8 + 8 + 6, slot)

        def spread(zeds, s):
            return pltpu.roll(zeds, LINE - 8 - 16 * s, 1)

        def both(low, high, s):
            if s % 2 == 0:
                return jnp.where(low_rows, high, low)
            return pltpu.roll(jnp.where(low_rows, low, high), 4, 0)

        slabs = []
        for i in range(12):
            column, s = divmod(i, 4)
            if column == 1:
                mid = tiles[s]
                low, high = v_face_y[e, 0], v_face_y[e, 1]
                side = [
                    both(low[s // 2], high[s // 2], s),
                    spread(jnp.where(low_rows, high[2], low[2]), s),
                ]
                slabs.append(jnp.concatenate([mid, jnp.concatenate(side, axis=1)], axis=0))
                continue
            face = column // 2
            got = v_face_x[e, face]
            z_at, z_edge, one_edge = (3, 1, 0) if face == 0 else (0, 0, 1)
            if 2 <= i < 10:
                mid = jnp.concatenate([got[s - 1 if face == 0 else s + 1], spread(got[z_at], s)], axis=1)
                low, high = v_edge[e, face, 0], v_edge[e, face, 1]
                side = [
                    both(low[one_edge], high[one_edge], s),
                    spread(jnp.where(low_rows, high[z_edge], low[z_edge]), s),
                ]
                slabs.append(jnp.concatenate([mid, jnp.concatenate(side, axis=1)], axis=0))
            elif i in (0, 10):
                two = spread(got[z_at], s) + spread(got[z_at], s + 1)
                slabs.append(jnp.concatenate([got[0 if face == 0 else 3], two], axis=1))
            else:
                slabs.append(None)
        return slabs

    def is_own(i):
        return 5 <= i < 9

    def narrow(slab, i):
        return slab if is_own(i) else fold_rows(slab)

    def put(ref, i, value, whole):
        if whole:
            ref[i] = value
        else:
            ref[i, 0:8] = value[0:8]

    def coefficients():
        u16 = [fold_rows(box_u[i]) if is_own(i) else box_u[i, 0:16] for i in range(14)]
        face_x = [face_terms(mean_x[i], u16[i + 1] - u16[i]) for i in range(13)]
        cface = []
        for j in range(7):
            cface.append(plane_sum(face_x[2 * j][1]))
            if 1 <= j < 6:
                put(cwx, j - 1, cface[j], 1 < j < 5)
        for i in range(7):
            put(wx, i, face_x[i + 3][1], 0 < i < 6)
        odd_row = lax.rem(index_of((16, 2 * LINE), 0), 2) == 1
        odd_lane = lax.rem(index_of((16, 2 * LINE), 1), 2) == 1
        for c in range(6):
            pairs = None
            for half in range(2):
                i = 2 * c + half
                u, re = u16[i + 1], react[i]
                if is_own(i + 1):
                    tall = box_u[i + 1]
                    flux, w = face_terms(mean_y[i], up(tall, 0) - tall)
                    flux_y, w_y = fold_rows(flux), fold_rows(w)
                    low_flux_y, low_y = fold_rows(down(flux, 0)), fold_rows(down(w, 0))
                else:
                    flux_y, w_y = face_terms(mean_y[i, 0:16], up(u, 0) - u)
                    low_flux_y, low_y = down(flux_y, 0), down(w_y, 0)
                flux_z, w_z = face_terms(mean_z[i], up(u, 1) - u)
                low_z = down(w_z, 1)
                force = (
                    src[i]
                    - re * u
                    + (face_x[i + 1][0] - face_x[i][0])
                    + (flux_y - low_flux_y)
                    + (flux_z - down(flux_z, 1))
                )
                put(v0, i, force, 2 <= i < 10)
                if 2 <= i < 10:
                    diagonal = re + face_x[i + 1][1] + face_x[i][1] + w_y + low_y + w_z + low_z
                    put(inv, i - 2, 1.0 / diagonal, 3 <= i < 9)
                if 3 <= i < 9:
                    for ref, weight in ((wyu, w_y), (wyl, low_y), (wzu, w_z), (wzl, low_z)):
                        put(ref, i - 3, weight, 4 <= i < 8)
                now = (w_y, low_y, w_z)
                pairs = now if half == 0 else tuple(one + two for one, two in zip(pairs, now))
            pair_y, pair_low, pair_z = pairs
            sum_y = pair_sum(jnp.where(odd_row, pair_y, up(pair_y, 0)), 1)
            sum_z = pair_sum(jnp.where(odd_lane, pair_z, up(pair_z, 1)), 0)
            if c in (2, 3):
                low_y = pair_sum(jnp.where(odd_row, down(pair_low, 0), pair_low), 1)
            else:
                low_y = pltpu.roll(sum_y, 2, 0)
            low_z = pltpu.roll(sum_z, 2, 1)
            diagonal = creact[c] + cface[c] + cface[c + 1] + sum_y + low_y + sum_z + low_z
            put(cinv, c, 1.0 / diagonal, 1 <= c < 5)
            if 1 <= c < 5:
                for ref, weight in ((cwyu, sum_y), (cwyl, low_y), (cwzu, sum_z), (cwzl, low_z)):
                    put(ref, c - 1, weight, 2 <= c < 4)

    def precondition(v, j):
        def part(whole):
            return slice(0, 16) if whole else slice(0, 8)

        own = [inv[i, part(0 < i < 7)] * v[i + 2][part(0 < i < 7)] for i in range(8)]
        coarse = []
        for c in range(6):
            rows = part(1 <= c < 5)
            pair = v[2 * c][rows] if v[2 * c + 1] is None else v[2 * c][rows] + v[2 * c + 1][rows]
            coarse.append(cinv[c, rows] * plane_sum(pair))
        coarse_z = []
        for c in range(4):
            q, rows = coarse[c + 1], part(1 <= c < 3)
            near = (
                cwx[c, rows] * coarse[c][rows]
                + cwx[c + 1, rows] * coarse[c + 2][rows]
                + cwyu[c, rows] * pltpu.roll(q, 14, 0)[rows]
                + cwyl[c, rows] * pltpu.roll(q, 2, 0)[rows]
                + cwzu[c, rows] * pltpu.roll(q[rows], 2 * LINE - 2, 1)
                + cwzl[c, rows] * pltpu.roll(q[rows], 2, 1)
            )
            coarse_z.append(COARSE_OWN * q[rows] + COARSE_NEAR * (cinv[c + 1, rows] * near))
        for i in range(6):
            q, rows = own[i + 1], part(0 < i < 5)
            near = (
                wx[i, rows] * own[i][rows]
                + wx[i + 1, rows] * own[i + 2][rows]
                + wyu[i, rows] * up(q, 0)[rows]
                + wyl[i, rows] * down(q, 0)[rows]
                + wzu[i, rows] * up(q[rows], 1)
                + wzl[i, rows] * down(q[rows], 1)
            )
            zs[j, i, rows] = (
                FINE_OWN * q[rows] + FINE_NEAR * (inv[i + 1, rows] * near) + coarse_z[(i + 1) // 2][rows]
            )

    def image(j, s):
        i = s + 1
        tall = zs[j, i]
        here = tall[0:8]
        total = react[i + 3, 0:8] * here
        for weight, other in (
            (wx[i, 0:8], zs[j, i - 1, 0:8]),
            (wx[i + 1, 0:8], zs[j, i + 1, 0:8]),
            (wyu[i, 0:8], up(tall, 0)[0:8]),
            (wyl[i, 0:8], down(tall, 0)[0:8]),
            (wzu[i, 0:8], up(here, 1)),
            (wzl[i, 0:8], down(here, 1)),
        ):
            total = total + weight * (here - other)
        return total

    group_of = lane // 16

    def gather(total, moments):
        for n, tile in moments:
            for shift in (64, 32, 16):
                tile = tile + pltpu.roll(tile, shift, 1)
            total = total + jnp.where(group_of == n, tile, 0.0)
        return total

    def global_sum(tile, which, beside):
        group = index_of((1, LINE), 1) // 16
        mixed = jnp.sum(tile, axis=0, keepdims=True)
        phases = ((core_line, got1), (plane_line, got2), (long_line, got3))
        for phase, (partners, got) in enumerate(phases):
            if phase == 1 and which == 0:
                pl.semaphore_wait(far_sem, 4)
            sums[which, phase] = mixed
            slot = 6 + 3 * which + phase
            for n, partner in enumerate(partners):
                send(sums.at[which, phase], got.at[which, n], slot, partner)
            beside(phase)
            part = got.at[which]
            pltpu.make_async_copy(part, part, recv_sem.at[slot]).wait()
            mixed = mixed + jnp.sum(got[which], axis=0)
        return [jnp.sum(jnp.where(group == n, mixed, 0.0), axis=1, keepdims=True) for n in range(6)]

    def solve(m):
        h = [(m[n + 1] + SHIFT * m[n]) * (1.0 / SCALE) for n in range(5)]

        def inverse(pivot, of):
            good = pivot > 1e-6 * of
            return jnp.where(good, 1.0 / jnp.where(good, pivot, 1.0), 0.0)

        i0 = inverse(h[0], jnp.zeros_like(h[0]))
        l1, l2 = h[1] * i0, h[2] * i0
        i1 = inverse(h[2] - l1 * h[1], h[2])
        h21 = h[3] - l2 * h[1]
        l21 = h21 * i1
        i2 = inverse(h[4] - l2 * h[2] - l21 * h21, h[4])
        y0 = m[0]
        y1 = m[1] - l1 * y0
        y2 = m[2] - l2 * y0 - l21 * y1
        c2 = y2 * i2
        c1 = y1 * i1 - l21 * c2
        c0 = y0 * i0 - l1 * c1 - l2 * c2
        return c0, c1, c2

    def total_of(tiles, others):
        total = tiles[0][:, 0:LINE] * others[0]
        for s in range(1, 4):
            total = total + tiles[s][:, 0:LINE] * others[s]
        return total

    given = []

    def give(sources, targets, slot, tiles):
        @pl.when(alone)
        def _():
            for source, target in zip(sources, targets):
                pltpu.make_async_copy(source, target, recv_sem.at[slot]).start()

        @pl.when(jnp.logical_not(alone))
        def _():
            for source, target in zip(sources, targets):
                pltpu.make_async_remote_copy(
                    source, target, send_sem.at[1], recv_sem.at[slot], device_id=partner, device_id_type=MESH
                ).start()

        given.append(tiles)

    pl.semaphore_wait(barrier, len(partners) + 1 - alone.astype(jnp.int32))
    homes = [raw0.at[f, pl.ds(5, 4), pl.ds(8, 8)] for f in range(4)]
    give([u_ref, k_ref], homes[:2], 12, 8)
    give([r_ref, s_ref], homes[2:], 15, 8)
    last_r = pltpu.make_async_copy(r_ref, end_rs.at[0], send_sem.at[2])
    last_s = pltpu.make_async_copy(s_ref, end_rs.at[1], send_sem.at[3])
    last_r.start()
    last_s.start()
    receive(8, 12)
    pack_corners(raw0, 0, 0, 2)
    count = exchange_wide(raw0, corner0, 0, 0, 2, True, 0)
    pack_z([raw0[f, 5 + s, 8:16] for f in range(2) for s in range(4)], 0, 0)
    count += exchange_far(raw0, far0, 0, 2, 0)
    receive(8, 15)
    pack_corners(raw0, 0, 2, 2)
    count += exchange_wide(raw0, corner0, 0, 2, 2, False, 0)
    pack_z([raw0[f, 5 + s, 8:16] for f in range(2, 4) for s in range(4)], 0, 1)
    count += exchange_z(zed0, 0, 0)
    receive(count, 0)
    for other in far_ones:
        pl.semaphore_signal(far_sem, inc=1, device_id=other, device_id_type=MESH)
    def put_box(i, value):
        if is_own(i):
            box_u[i] = value
        else:
            box_u[i, 0:16] = value

    def get_box(i):
        return box_u[i] if is_own(i) else box_u[i, 0:16]

    k_slabs = []
    for i in range(14):
        put_box(i, narrow(wide_slab(raw0, corner0, zed0, far0, 0, i), i))
        k_slabs.append(narrow(wide_slab(raw0, corner0, zed0, far0, 1, i), i))
    k16 = [fold_rows(k_slabs[i]) if is_own(i) else k_slabs[i] for i in range(14)]
    for i in range(13):
        mean_x[i] = mean_of(k16[i], k16[i + 1])
    for i in range(12):
        k = k_slabs[i + 1]
        if is_own(i + 1):
            mean_y[i] = mean_of(k, up(k, 0))
        else:
            mean_y[i, 0:16] = mean_of(k, up(k, 0))
        mean_z[i] = mean_of(k16[i + 1], up(k16[i + 1], 1))
        react[i] = fold_rows(wide_slab(raw0, corner0, zed0, far0, 2, i + 1, True))
        src[i] = fold_rows(wide_slab(raw0, corner0, zed0, far0, 3, i + 1, True))
    for c in range(6):
        creact[c] = plane_sum(react[2 * c] + react[2 * c + 1])

    own = (slice(0, 8), slice(0, LINE))

    def give_field(f, slot):
        row = index_of((ROWS, LINE), 0)
        next_rows = jnp.zeros((ROWS, LINE), jnp.float32)
        next_lanes = next_rows
        for s in range(4):
            tile = pltpu.roll(zs[f, s + 1, 8:16, 0:LINE], 2 * s + 1, 0)
            next_rows = jnp.where(row // 2 == s, tile, next_rows)
            tile = pltpu.roll(zs[f, s + 1, 0:8, LINE : 2 * LINE], 2 * s + 1, 1)
            next_lanes = jnp.where(lane // 2 == s, tile, next_lanes)
        end_pack[f - 3, 0] = next_rows
        end_pack[f - 3, 1] = next_lanes
        region = (f, pl.ds(0, 6), pl.ds(0, 8), pl.ds(0, LINE))
        give([zs.at[region], end_pack.at[f - 3]], [end_zs.at[f - 3], end_halo.at[f - 3]], slot, 8)

    def beside_v(newton, j):
        if newton == 0 and j == 0:
            for i in range(6):
                zs[7, i] = k16[i + 4]
            give_field(7, 14)
        elif newton == 1:
            if j == 0:
                give_field(3, 13)
            give_field(4 + j, 13)

    def end_fields(slabs, halo):
        tall = [jnp.concatenate([slabs[s + 1], pltpu.roll(halo[0], 7 - 2 * s, 0)], axis=0) for s in range(4)]
        wide = [
            jnp.concatenate([slabs[s + 1], pltpu.roll(halo[1], LINE - 1 - 2 * s, 1)], axis=1) for s in range(4)
        ]
        return slabs, tall, wide

    def end_means():
        receive(8, 14)
        slabs, tall, wide = end_fields([end_zs[4, i] for i in range(6)], [end_halo[4, i] for i in range(2)])
        for i in range(5):
            end_x[i] = mean_of(slabs[i], slabs[i + 1])
        for s in range(4):
            end_y[s] = mean_of(tall[s], up(tall[s], 0))
            end_z[s] = mean_of(wide[s], up(wide[s], 1))

    for newton in range(NEWTON):
        coefficients()
        sofar = []
        moments = []
        v = [v0[i] if 2 <= i < 10 else v0[i, 0:8] for i in range(12)]
        tiles = [slab[0:8] for slab in v[4:8]]
        for j in range(KRYLOV):
            at = 4 * newton + j
            precondition(v, at)
            z_tiles = [zs[(at, s + 1) + own] for s in range(4)]
            moments.append((2 * j, total_of(tiles, z_tiles)))
            if newton + 1 < NEWTON:
                for s in range(4):
                    raw_h[j, 5 + s, 8:16] = z_tiles[s]
            tiles = [SCALE * image(at, s) - SHIFT * tiles[s] for s in range(4)]
            moments.append((2 * j + 1, total_of(tiles, z_tiles)))
            if j + 1 < KRYLOV:

                def meanwhile(newton=newton, j=j, moments=moments):
                    sofar.append(gather(sofar[-1] if j else nothing, moments))
                    beside_v(newton, j)

                v = exchange_v(tiles, 2 * newton + j, meanwhile)
                moments = []

        counts = []

        def beside(phase, newton=newton, counts=counts):
            if phase == 1 and newton + 1 < NEWTON:
                pack_corners(raw_h, 1, 0, 3)
                counts.append(exchange_wide(raw_h, corner_h, 1, 0, 3, True, 1))
                pack_z([raw_h[f, 5 + s, 8:16] for f in range(2) for s in range(4)], 1, 0)
                pack_z([raw_h[2, 5 + s, 8:16] for s in range(4)], 1, 1)
                counts.append(exchange_far(raw_h, far_h, 1, 3, 1))
                counts.append(exchange_z(zed_h, 1, 1))
            elif phase == 1:
                give_field(6, 13)
                end_means()
            elif phase == 2 and newton + 1 < NEWTON:
                receive(sum(counts), 1)
                for j in range(3):
                    for i in range(14):
                        slab = narrow(wide_slab(raw_h, corner_h, zed_h, far_h, j, i), i)
                        if is_own(i):
                            box_z[j, i] = slab
                        else:
                            box_z[j, i, 0:16] = slab

        c = solve(global_sum(gather(sofar[-1], moments), newton, beside))
        if newton + 1 < NEWTON:
            for i in range(14):
                rows = slice(0, 24 if is_own(i) else 16)
                total = get_box(i)
                for j in range(3):
                    total = total + c[j] * box_z[j, i, rows]
                put_box(i, total)
                if 4 <= i < 10:
                    zs[3, i - 4] = fold_rows(total) if is_own(i) else total

    last_r.wait()
    last_s.wait()
    receive(8 * 4, 13)
    near = []
    for tiles in ([end_zs.at[:, i] for i in range(6)], [end_halo.at[:, i] for i in range(2)]):
        for tile in tiles:
            total = tile[0]
            for j in range(3):
                total = total + c[j] * tile[1 + j]
            near.append(total)
    last, tall, wide = end_fields(near[:6], near[6:])
    low_flux = None
    for s in range(-1, 4):
        flux, _ = face_terms(end_x[s + 1], last[s + 2] - last[s + 1])
        if s >= 0:
            out[0, s] = last[s + 1]
            flux_y, _ = face_terms(end_y[s], up(tall[s], 0) - tall[s])
            flux_z, _ = face_terms(end_z[s], up(wide[s], 1) - wide[s])
            out[1, s] = (
                end_rs[0, s] * last[s + 1]
                - (flux - low_flux)
                - (flux_y - down(flux_y, 0))[0:8]
                - (flux_z - down(flux_z, 1))[:, 0:LINE]
                - end_rs[1, s]
            )
        low_flux = flux
    for copy in copies:
        copy.wait_send()

    @pl.when(jnp.logical_not(alone))
    def _():
        part = dummy.at[pl.ds(0, sum(given))]
        pltpu.make_async_copy(part, part, send_sem.at[1]).wait()


def local(sizes, state, conductivity, reaction, source):
    nx, ny, nz = sizes
    plane, line = 4 * (nz // 2), (nx // 4) * ny

    def vmem(*shape):
        return pltpu.VMEM(shape, jnp.float32)

    full, half = (24, 2 * LINE), (16, 2 * LINE)
    tile = (ROWS, LINE)
    scratch = [
        vmem(4, 14, 24, LINE), vmem(2, 2, 4, 2, *tile), vmem(3, 3, 2, 2, *tile), vmem(2, 2, 2, *tile),
        vmem(3, 14, 24, LINE), vmem(2, 2, 3, 2, *tile), vmem(3, 3, 2, 2, *tile), vmem(2, 2, 2, *tile),
        vmem(4, 7, *tile), vmem(4, 2, 4, *tile), vmem(4, 2, 4, *tile), vmem(4, 2, 3, *tile), vmem(4, 2, 2, 2, *tile), vmem(2, 2, 2, *tile), vmem(2, 2, 4, 2, *tile), vmem(14, *full), vmem(3, 14, *full),
        vmem(13, *half), vmem(12, *full), vmem(12, *half), vmem(12, *half), vmem(12, *half), vmem(6, *half),
        vmem(12, *half), vmem(8, *half), vmem(7, *half), vmem(6, *half), vmem(6, *half), vmem(6, *half), vmem(6, *half),
        vmem(6, *half), vmem(5, *half), vmem(4, *half), vmem(4, *half), vmem(4, *half), vmem(4, *half),
        vmem(8, 6, *half), vmem(2, 3, 1, LINE), vmem(2, 1, 1, LINE), vmem(2, plane - 1, 1, LINE), vmem(2, line - 1, 1, LINE),
        vmem(160, *tile),
        vmem(5, 6, *tile), vmem(5, 2, *tile), vmem(5, 2, *tile), vmem(5, *tile), vmem(4, 16, LINE), vmem(4, ROWS, 2 * LINE), vmem(2, 4, *tile),
        pltpu.SemaphoreType.DMA((4,)), pltpu.SemaphoreType.DMA((16,)), pltpu.SemaphoreType.REGULAR,
    ]
    spec = pl.BlockSpec(memory_space=pltpu.MemorySpace.HBM)
    both = pl.pallas_call(
        functools.partial(kernel, sizes),
        out_shape=jax.ShapeDtypeStruct((2, *state.shape), jnp.float32),
        in_specs=[spec] * 4,
        out_specs=pl.BlockSpec(memory_space=pltpu.VMEM),
        scratch_shapes=scratch,
        compiler_params=pltpu.CompilerParams(
            collective_id=0, has_side_effects=True, vmem_limit_bytes=61 * 1024 * 1024
        ),
    )(state, conductivity, reaction, source)
    return both[0], both[1]


def solution(mesh):
    sizes = tuple(mesh.shape[name] for name in ("gx", "gy", "gz"))
    placed = P("gx", "gy", "gz")
    return jax.shard_map(
        functools.partial(local, sizes),
        mesh=mesh,
        in_specs=(placed,) * 4,
        out_specs=(placed, placed),
        check_vma=False,
    )
```

```python
import functools

import jax
import jax.numpy as jnp
from jax import lax
from jax.experimental import pallas as pl
from jax.experimental.pallas import tpu as pltpu
from jax.sharding import PartitionSpec as P

NEWTON = 2
KRYLOV = 3
EPS_SQUARE = 0.25
SCALE, SHIFT = 0.7, 1.0
MESH = pl.DeviceIdType.MESH

LINE = 128
ROWS = 8


def chebyshev_pair(low):
    centre = (2.0 + low) / 2.0
    half_width = (2.0 - low) / 2.0
    sigma = centre / half_width
    rho = 1.0 / sigma
    rho_new = 1.0 / (2.0 * sigma - rho)
    last = 2.0 * rho_new / half_width
    return (1.0 + rho_new * rho) / centre + last * (1.0 - 1.0 / centre), last / centre


FINE_OWN, FINE_NEAR = chebyshev_pair(0.3)
COARSE_OWN, COARSE_NEAR = chebyshev_pair(0.05)

CROSS = [(0, 0), (1, 0), (-1, 0), (0, 1), (0, -1)]
CORNERS = [(1, 1), (1, -1), (-1, 1), (-1, -1)]


def up(field, axis):
    return pltpu.roll(field, field.shape[axis] - 1, axis)


def down(field, axis):
    return pltpu.roll(field, 1, axis)


def index_of(shape, axis):
    return lax.broadcasted_iota(jnp.int32, shape, axis)


def face_terms(mean_k, difference):
    square = difference * difference
    inverse_root = lax.rsqrt(EPS_SQUARE + square)
    root = (EPS_SQUARE + square) * inverse_root
    return mean_k * root * difference, mean_k * (EPS_SQUARE + 2.0 * square) * inverse_root


def mean_of(one, other):
    return 2.0 * one * other / (one + other)


def fold_rows(field):
    row = index_of((ROWS, field.shape[1]), 0)
    return jnp.concatenate([field[8:16], jnp.where(row < 4, field[16:24], field[0:8])], axis=0)


def pair_sum(field, axis):
    odd = lax.rem(index_of(field.shape, axis), 2) == 1
    return field + jnp.where(odd, down(field, axis), up(field, axis))


def plane_sum(field):
    return pair_sum(pair_sum(field, 0), 1)


def kernel(
    sizes, u_ref, k_ref, r_ref, s_ref, out,
    raw0, corner0, zed0, far0, raw_h, corner_h, zed_h, far_h, v_out_x, v_out_y, v_face_x, v_face_y, v_edge, pack, corner_pack, box_u, box_z, mean_x, mean_y, mean_z, react, src,
    creact, v0, inv, wx, wyu, wyl, wzu, wzl, cinv, cwx, cwyu, cwyl, cwzu, cwzl, zs, sums, got2, got3, dummy,
    end_zs, end_pack, end_halo, end_x, end_y, end_z, end_rs, send_sem, recv_sem, far_sem,
):
    nx, ny, nz = sizes
    mx, my, mz = lax.axis_index("gx"), lax.axis_index("gy"), lax.axis_index("gz")

    group, place_y = mx // 4, lax.rem(mx, 4)
    bx, by = group * 4 + my, place_y
    partner = (group * 4 + my, place_y, mz)
    alone = my == place_y

    def block_at(dx, dy, dz):
        x, y = lax.rem(bx + dx + nx, nx), lax.rem(by + dy + ny, ny)
        return ((x // 4) * 4 + y, lax.rem(x, 4), lax.rem(mz + dz + nz, nz))

    def around(step, size):
        return min(step, size - step)

    chips = nz // 2
    plane_line = []
    steps = [(dy, dx, dc) for dy in range(4) for dx in range(chips) for dc in range(2)][1:]
    for dy, dx, dc in sorted(steps, key=lambda d: -around(d[0], 4) - around(d[1], chips)):
        x = lax.rem(mz // 2 + dx, chips)
        plane_line.append(((mx // 4) * 4 + lax.rem(mx + dy, 4), my, x * 2 + lax.rem(mz + dc, 2)))
    line = (nx // 4) * ny
    at = (mx // 4) * ny + my
    long_line = []
    for step in sorted(range(1, line), key=lambda d: -around(d, line)):
        there = lax.rem(at + step, line)
        long_line.append(((there // ny) * 4 + lax.rem(mx, 4), lax.rem(there, ny), mz))

    offsets = [(dx, dy, dz) for dx in (-1, 0, 1) for dy in (-1, 0, 1) for dz in (-1, 0, 1)]
    offsets = [d for d in offsets if d != (0, 0, 0)]
    offsets += [(dx, 0, dz) for dx in (2, -2) for dz in (-1, 0, 1)]

    barrier = pltpu.get_barrier_semaphore()
    partners = [block_at(*d) for d in offsets]
    far_ones = [(lax.rem(mx + step, nx), my, mz) for step in (4, nx - 4)]
    far_ones += [(mx, my, lax.rem(mz + step, nz)) for step in (2, nz - 2)]

    @pl.when(jnp.logical_not(alone))
    def _():
        pl.semaphore_signal(barrier, inc=1, device_id=partner, device_id_type=MESH)

    for other in partners:
        pl.semaphore_signal(barrier, inc=1, device_id=other, device_id_type=MESH)

    lane = index_of((ROWS, LINE), 1)
    copies = []

    def send(source, target, slot, device):
        copy = pltpu.make_async_remote_copy(
            source, target, send_sem.at[0], recv_sem.at[slot], device_id=device, device_id_type=MESH
        )
        copy.start()
        copies.append(copy)

    def receive(tiles, slot):
        part = dummy.at[pl.ds(0, tiles)]
        pltpu.make_async_copy(part, part, recv_sem.at[slot]).wait()

    def pack_z(tiles, place, at):
        low = jnp.zeros((ROWS, LINE), jnp.float32)
        high = low
        for g, tile in enumerate(tiles):
            mine = lane // 16 == g
            low = jnp.where(mine, tile if g == 0 else pltpu.roll(tile, 16 * g, 1), low)
            shift = (16 * g + 16) % LINE
            high = jnp.where(mine, pltpu.roll(tile, shift, 1) if shift else tile, high)
        pack[place, 0, at] = low
        pack[place, 1, at] = high

    def unpack_z(low_tiles, high_tiles, g):
        t, g = divmod(g, 8)
        shift = (LINE - 16 * g) % LINE
        above = pltpu.roll(low_tiles[t], shift, 1) if shift else low_tiles[t]
        shift = (LINE - 16 - 16 * g) % LINE
        below = pltpu.roll(high_tiles[t], shift, 1) if shift else high_tiles[t]
        return jnp.where(lane < 64, above, below)

    def pack_corners(raw, place, first, fields):
        low_rows = index_of((ROWS, LINE), 0) < 4
        for f in range(first, first + fields):
            for pair in range(2):
                one, two = raw[f, 5 + 2 * pair, 8:16], raw[f, 6 + 2 * pair, 8:16]
                two = pltpu.roll(two, 4, 0)
                corner_pack[place, 1, f, pair] = jnp.where(low_rows, two, one)
                corner_pack[place, 0, f, pair] = jnp.where(low_rows, one, two)

    def exchange_wide(raw, corner, place, first, fields, all_pairs, slot):
        which = pl.ds(first, fields)
        own = (which, pl.ds(5, 4), pl.ds(8, 8))
        for dx, dy in CROSS[1:3]:
            target = (which, pl.ds(5 - 4 * dx, 4), pl.ds(8 - 8 * dy, 8))
            send(raw.at[own], raw.at[target], slot, block_at(dx, dy, 0))
        for dx, dy in CORNERS:
            pairs = pl.ds(0, 2) if all_pairs else pl.ds((1 + dx) // 2, 1)
            send(
                corner_pack.at[place, (1 + dy) // 2, which, pairs],
                corner.at[(1 - dx) // 2, (1 - dy) // 2, which, pairs],
                slot,
                block_at(dx, dy, 0),
            )
        for dx, dy in CROSS[3:]:
            target = (which, pl.ds(5 - 4 * dx, 4), pl.ds(8 - 8 * dy, 8))
            send(raw.at[own], raw.at[target], slot, block_at(dx, dy, 0))
        return 16 * fields + (8 if all_pairs else 4) * fields

    def exchange_far(raw, zed2, place, fields, slot):
        some, rows, tiles = pl.ds(0, fields), pl.ds(8, 8), (fields + 1) // 2
        send(raw.at[some, pl.ds(8, 1), rows], raw.at[some, pl.ds(0, 1), rows], slot, block_at(2, 0, 0))
        send(raw.at[some, pl.ds(5, 1), rows], raw.at[some, pl.ds(13, 1), rows], slot, block_at(-2, 0, 0))
        for dx in (2, -2):
            for dz in (1, -1):
                send(
                    pack.at[place, (1 + dz) // 2, pl.ds(0, tiles)],
                    zed2.at[(2 - dx) // 4, (1 - dz) // 2, pl.ds(0, tiles)],
                    slot,
                    block_at(dx, 0, dz),
                )
        return 2 * fields + 4 * tiles

    def exchange_z(zed, place, slot):
        for dx, dy in CORNERS + CROSS:
            for dz in (1, -1):
                send(
                    pack.at[place, (1 + dz) // 2],
                    zed.at[1 - dx, 1 - dy, (1 - dz) // 2],
                    slot,
                    block_at(dx, dy, dz),
                )
        return 36

    nothing = jnp.zeros((ROWS, LINE), jnp.float32)

    def wide_slab(raw, corner, zed, zed2, field, i, slim=False):
        outer = i in (0, 13)
        if outer or (slim and i in (1, 2, 11, 12)):
            column, s = ((i - 1) // 4, (i - 1) % 4) if not outer else (0, 3) if i == 0 else (1, 0)
            low, high = (zed2[column, 1], zed2[column, 0]) if outer else (zed[column, 1, 1], zed[column, 1, 0])
            halo = unpack_z(low, high, field * 4 + s)
            mid = jnp.concatenate([raw[field, i, 8:16], halo], axis=1)
            empty = jnp.zeros_like(mid)
            return jnp.concatenate([empty, mid, empty], axis=0)
        column, s = divmod(i - 1, 4)
        if column == 1:
            main = raw[field, i]
        else:
            ends_y = []
            for y in range(2):
                packed = corner[column // 2, y, field, s // 2]
                ends_y.append(pltpu.roll(packed, 4, 0) if s % 2 else packed)
            main = jnp.concatenate([ends_y[0], raw[field, i, 8:16], ends_y[1]], axis=0)
        g = field * 4 + s
        halo = [unpack_z(zed[column, y, 1], zed[column, y, 0], g) for y in range(3)]
        return jnp.concatenate([main, jnp.concatenate(halo, axis=0)], axis=1)

    def exchange_v(tiles, e, between):
        slot = 2 + e
        low_rows = index_of((ROWS, LINE), 0) < 4
        mains = [tile[:, 0:LINE] for tile in tiles]
        packed = nothing
        for s in range(4):
            part = pltpu.roll(tiles[s][:, LINE : 2 * LINE], 16 * s + 8, 1)
            packed = jnp.where(lane // 16 == s, part, packed)
        for pair in range(2):
            one, two = mains[2 * pair], pltpu.roll(mains[2 * pair + 1], 4, 0)
            v_out_y[e, 1, 1 + pair] = jnp.where(low_rows, two, one)
            v_out_y[e, 0, 1 + pair] = jnp.where(low_rows, one, two)
        for way in range(2):
            v_out_y[e, way, 0] = packed
            v_out_y[e, way, 3] = packed
        for n, tile in enumerate(
            (mains[0] + mains[1], mains[2], mains[3], packed, mains[0], mains[1], mains[2] + mains[3])
        ):
            v_out_x[e, n] = tile
        for dx, dy in CORNERS:
            send(
                v_out_y.at[e, (1 + dy) // 2, pl.ds(1 + dx, 2)],
                v_edge.at[e, (1 - dx) // 2, (1 - dy) // 2],
                slot,
                block_at(dx, dy, 0),
            )
        for n, dx in enumerate((1, -1)):
            send(v_out_x.at[e, pl.ds(3 * n, 4)], v_face_x.at[e, n], slot, block_at(dx, 0, 0))
        for n, dy in enumerate((1, -1)):
            send(v_out_y.at[e, 1 - n, pl.ds(1, 3)], v_face_y.at[e, n], slot, block_at(0, dy, 0))
        between()
        receive(8 + 8 + 6, slot)

        def spread(zeds, s):
            return pltpu.roll(zeds, LINE - 8 - 16 * s, 1)

        def both(low, high, s):
            if s % 2 == 0:
                return jnp.where(low_rows, high, low)
            return pltpu.roll(jnp.where(low_rows, low, high), 4, 0)

        slabs = []
        for i in range(12):
            column, s = divmod(i, 4)
            if column == 1:
                mid = tiles[s]
                low, high = v_face_y[e, 0], v_face_y[e, 1]
                side = [
                    both(low[s // 2], high[s // 2], s),
                    spread(jnp.where(low_rows, high[2], low[2]), s),
                ]
                slabs.append(jnp.concatenate([mid, jnp.concatenate(side, axis=1)], axis=0))
                continue
            face = column // 2
            got = v_face_x[e, face]
            z_at, z_edge, one_edge = (3, 1, 0) if face == 0 else (0, 0, 1)
            if 2 <= i < 10:
                mid = jnp.concatenate([got[s - 1 if face == 0 else s + 1], spread(got[z_at], s)], axis=1)
                low, high = v_edge[e, face, 0], v_edge[e, face, 1]
                side = [
                    both(low[one_edge], high[one_edge], s),
                    spread(jnp.where(low_rows, high[z_edge], low[z_edge]), s),
                ]
                slabs.append(jnp.concatenate([mid, jnp.concatenate(side, axis=1)], axis=0))
            elif i in (0, 10):
                two = spread(got[z_at], s) + spread(got[z_at], s + 1)
                slabs.append(jnp.concatenate([got[0 if face == 0 else 3], two], axis=1))
            else:
                slabs.append(None)
        return slabs

    def is_own(i):
        return 5 <= i < 9

    def narrow(slab, i):
        return slab if is_own(i) else fold_rows(slab)

    def put(ref, i, value, whole):
        if whole:
            ref[i] = value
        else:
            ref[i, 0:8] = value[0:8]

    def coefficients():
        u16 = [fold_rows(box_u[i]) if is_own(i) else box_u[i, 0:16] for i in range(14)]
        face_x = [face_terms(mean_x[i], u16[i + 1] - u16[i]) for i in range(13)]
        cface = []
        for j in range(7):
            cface.append(plane_sum(face_x[2 * j][1]))
            if 1 <= j < 6:
                put(cwx, j - 1, cface[j], 1 < j < 5)
        for i in range(7):
            put(wx, i, face_x[i + 3][1], 0 < i < 6)
        odd_row = lax.rem(index_of((16, 2 * LINE), 0), 2) == 1
        odd_lane = lax.rem(index_of((16, 2 * LINE), 1), 2) == 1
        for c in range(6):
            pairs = None
            for half in range(2):
                i = 2 * c + half
                u, re = u16[i + 1], react[i]
                if is_own(i + 1):
                    tall = box_u[i + 1]
                    flux, w = face_terms(mean_y[i], up(tall, 0) - tall)
                    flux_y, w_y = fold_rows(flux), fold_rows(w)
                    low_flux_y, low_y = fold_rows(down(flux, 0)), fold_rows(down(w, 0))
                else:
                    flux_y, w_y = face_terms(mean_y[i, 0:16], up(u, 0) - u)
                    low_flux_y, low_y = down(flux_y, 0), down(w_y, 0)
                flux_z, w_z = face_terms(mean_z[i], up(u, 1) - u)
                low_z = down(w_z, 1)
                force = (
                    src[i]
                    - re * u
                    + (face_x[i + 1][0] - face_x[i][0])
                    + (flux_y - low_flux_y)
                    + (flux_z - down(flux_z, 1))
                )
                put(v0, i, force, 2 <= i < 10)
                if 2 <= i < 10:
                    diagonal = re + face_x[i + 1][1] + face_x[i][1] + w_y + low_y + w_z + low_z
                    put(inv, i - 2, 1.0 / diagonal, 3 <= i < 9)
                if 3 <= i < 9:
                    for ref, weight in ((wyu, w_y), (wyl, low_y), (wzu, w_z), (wzl, low_z)):
                        put(ref, i - 3, weight, 4 <= i < 8)
                now = (w_y, low_y, w_z)
                pairs = now if half == 0 else tuple(one + two for one, two in zip(pairs, now))
            pair_y, pair_low, pair_z = pairs
            sum_y = pair_sum(jnp.where(odd_row, pair_y, up(pair_y, 0)), 1)
            sum_z = pair_sum(jnp.where(odd_lane, pair_z, up(pair_z, 1)), 0)
            if c in (2, 3):
                low_y = pair_sum(jnp.where(odd_row, down(pair_low, 0), pair_low), 1)
            else:
                low_y = pltpu.roll(sum_y, 2, 0)
            low_z = pltpu.roll(sum_z, 2, 1)
            diagonal = creact[c] + cface[c] + cface[c + 1] + sum_y + low_y + sum_z + low_z
            put(cinv, c, 1.0 / diagonal, 1 <= c < 5)
            if 1 <= c < 5:
                for ref, weight in ((cwyu, sum_y), (cwyl, low_y), (cwzu, sum_z), (cwzl, low_z)):
                    put(ref, c - 1, weight, 2 <= c < 4)

    def precondition(v, j):
        def part(whole):
            return slice(0, 16) if whole else slice(0, 8)

        own = [inv[i, part(0 < i < 7)] * v[i + 2][part(0 < i < 7)] for i in range(8)]
        coarse = []
        for c in range(6):
            rows = part(1 <= c < 5)
            pair = v[2 * c][rows] if v[2 * c + 1] is None else v[2 * c][rows] + v[2 * c + 1][rows]
            coarse.append(cinv[c, rows] * plane_sum(pair))
        coarse_z = []
        for c in range(4):
            q, rows = coarse[c + 1], part(1 <= c < 3)
            near = (
                cwx[c, rows] * coarse[c][rows]
                + cwx[c + 1, rows] * coarse[c + 2][rows]
                + cwyu[c, rows] * pltpu.roll(q, 14, 0)[rows]
                + cwyl[c, rows] * pltpu.roll(q, 2, 0)[rows]
                + cwzu[c, rows] * pltpu.roll(q[rows], 2 * LINE - 2, 1)
                + cwzl[c, rows] * pltpu.roll(q[rows], 2, 1)
            )
            coarse_z.append(COARSE_OWN * q[rows] + COARSE_NEAR * (cinv[c + 1, rows] * near))
        for i in range(6):
            q, rows = own[i + 1], part(0 < i < 5)
            near = (
                wx[i, rows] * own[i][rows]
                + wx[i + 1, rows] * own[i + 2][rows]
                + wyu[i, rows] * up(q, 0)[rows]
                + wyl[i, rows] * down(q, 0)[rows]
                + wzu[i, rows] * up(q[rows], 1)
                + wzl[i, rows] * down(q[rows], 1)
            )
            zs[j, i, rows] = (
                FINE_OWN * q[rows] + FINE_NEAR * (inv[i + 1, rows] * near) + coarse_z[(i + 1) // 2][rows]
            )

    def image(j, s):
        i = s + 1
        tall = zs[j, i]
        here = tall[0:8]
        total = react[i + 3, 0:8] * here
        for weight, other in (
            (wx[i, 0:8], zs[j, i - 1, 0:8]),
            (wx[i + 1, 0:8], zs[j, i + 1, 0:8]),
            (wyu[i, 0:8], up(tall, 0)[0:8]),
            (wyl[i, 0:8], down(tall, 0)[0:8]),
            (wzu[i, 0:8], up(here, 1)),
            (wzl[i, 0:8], down(here, 1)),
        ):
            total = total + weight * (here - other)
        return total

    group_of = lane // 16

    def gather(total, moments):
        for n, tile in moments:
            for shift in (64, 32, 16):
                tile = tile + pltpu.roll(tile, shift, 1)
            total = total + jnp.where(group_of == n, tile, 0.0)
        return total

    def global_sum(tile, which, beside):
        group = index_of((1, LINE), 1) // 16
        mixed = jnp.sum(tile, axis=0, keepdims=True)
        for phase, partners, got in ((1, plane_line, got2), (2, long_line, got3)):
            if phase == 1 and which == 0:
                pl.semaphore_wait(far_sem, 4)
            sums[which, phase] = mixed
            slot = 6 + 3 * which + phase
            for n, partner in enumerate(partners):
                send(sums.at[which, phase], got.at[which, n], slot, partner)
            beside(phase)
            part = got.at[which]
            pltpu.make_async_copy(part, part, recv_sem.at[slot]).wait()
            mixed = mixed + jnp.sum(got[which], axis=0)
        return [jnp.sum(jnp.where(group == n, mixed, 0.0), axis=1, keepdims=True) for n in range(6)]

    def solve(m):
        h = [(m[n + 1] + SHIFT * m[n]) * (1.0 / SCALE) for n in range(5)]

        def inverse(pivot, of):
            good = pivot > 1e-6 * of
            return jnp.where(good, 1.0 / jnp.where(good, pivot, 1.0), 0.0)

        i0 = inverse(h[0], jnp.zeros_like(h[0]))
        l1, l2 = h[1] * i0, h[2] * i0
        i1 = inverse(h[2] - l1 * h[1], h[2])
        h21 = h[3] - l2 * h[1]
        l21 = h21 * i1
        i2 = inverse(h[4] - l2 * h[2] - l21 * h21, h[4])
        y0 = m[0]
        y1 = m[1] - l1 * y0
        y2 = m[2] - l2 * y0 - l21 * y1
        c2 = y2 * i2
        c1 = y1 * i1 - l21 * c2
        c0 = y0 * i0 - l1 * c1 - l2 * c2
        return c0, c1, c2

    def total_of(tiles, others):
        total = tiles[0][:, 0:LINE] * others[0]
        for s in range(1, 4):
            total = total + tiles[s][:, 0:LINE] * others[s]
        return total

    given = []

    def give(sources, targets, slot, tiles):
        @pl.when(alone)
        def _():
            for source, target in zip(sources, targets):
                pltpu.make_async_copy(source, target, recv_sem.at[slot]).start()

        @pl.when(jnp.logical_not(alone))
        def _():
            for source, target in zip(sources, targets):
                pltpu.make_async_remote_copy(
                    source, target, send_sem.at[1], recv_sem.at[slot], device_id=partner, device_id_type=MESH
                ).start()

        given.append(tiles)

    pl.semaphore_wait(barrier, len(partners) + 1 - alone.astype(jnp.int32))
    homes = [raw0.at[f, pl.ds(5, 4), pl.ds(8, 8)] for f in range(4)]
    give([u_ref, k_ref], homes[:2], 12, 8)
    give([r_ref, s_ref], homes[2:], 15, 8)
    last_r = pltpu.make_async_copy(r_ref, end_rs.at[0], send_sem.at[2])
    last_s = pltpu.make_async_copy(s_ref, end_rs.at[1], send_sem.at[3])
    last_r.start()
    last_s.start()
    receive(8, 12)
    pack_corners(raw0, 0, 0, 2)
    count = exchange_wide(raw0, corner0, 0, 0, 2, True, 0)
    pack_z([raw0[f, 5 + s, 8:16] for f in range(2) for s in range(4)], 0, 0)
    count += exchange_far(raw0, far0, 0, 2, 0)
    receive(8, 15)
    pack_corners(raw0, 0, 2, 2)
    count += exchange_wide(raw0, corner0, 0, 2, 2, False, 0)
    pack_z([raw0[f, 5 + s, 8:16] for f in range(2, 4) for s in range(4)], 0, 1)
    count += exchange_z(zed0, 0, 0)
    receive(count, 0)
    for other in far_ones:
        pl.semaphore_signal(far_sem, inc=1, device_id=other, device_id_type=MESH)
    def put_box(i, value):
        if is_own(i):
            box_u[i] = value
        else:
            box_u[i, 0:16] = value

    def get_box(i):
        return box_u[i] if is_own(i) else box_u[i, 0:16]

    k_slabs = []
    for i in range(14):
        put_box(i, narrow(wide_slab(raw0, corner0, zed0, far0, 0, i), i))
        k_slabs.append(narrow(wide_slab(raw0, corner0, zed0, far0, 1, i), i))
    k16 = [fold_rows(k_slabs[i]) if is_own(i) else k_slabs[i] for i in range(14)]
    for i in range(13):
        mean_x[i] = mean_of(k16[i], k16[i + 1])
    for i in range(12):
        k = k_slabs[i + 1]
        if is_own(i + 1):
            mean_y[i] = mean_of(k, up(k, 0))
        else:
            mean_y[i, 0:16] = mean_of(k, up(k, 0))
        mean_z[i] = mean_of(k16[i + 1], up(k16[i + 1], 1))
        react[i] = fold_rows(wide_slab(raw0, corner0, zed0, far0, 2, i + 1, True))
        src[i] = fold_rows(wide_slab(raw0, corner0, zed0, far0, 3, i + 1, True))
    for c in range(6):
        creact[c] = plane_sum(react[2 * c] + react[2 * c + 1])

    own = (slice(0, 8), slice(0, LINE))

    def give_field(f, slot):
        row = index_of((ROWS, LINE), 0)
        next_rows = jnp.zeros((ROWS, LINE), jnp.float32)
        next_lanes = next_rows
        for s in range(4):
            tile = pltpu.roll(zs[f, s + 1, 8:16, 0:LINE], 2 * s + 1, 0)
            next_rows = jnp.where(row // 2 == s, tile, next_rows)
            tile = pltpu.roll(zs[f, s + 1, 0:8, LINE : 2 * LINE], 2 * s + 1, 1)
            next_lanes = jnp.where(lane // 2 == s, tile, next_lanes)
        end_pack[f - 3, 0] = next_rows
        end_pack[f - 3, 1] = next_lanes
        region = (f, pl.ds(0, 6), pl.ds(0, 8), pl.ds(0, LINE))
        give([zs.at[region], end_pack.at[f - 3]], [end_zs.at[f - 3], end_halo.at[f - 3]], slot, 8)

    def beside_v(newton, j):
        if newton == 0 and j == 0:
            for i in range(6):
                zs[7, i] = k16[i + 4]
            give_field(7, 14)
        elif newton == 1:
            if j == 0:
                give_field(3, 13)
            give_field(4 + j, 13)

    def end_fields(slabs, halo):
        tall = [jnp.concatenate([slabs[s + 1], pltpu.roll(halo[0], 7 - 2 * s, 0)], axis=0) for s in range(4)]
        wide = [
            jnp.concatenate([slabs[s + 1], pltpu.roll(halo[1], LINE - 1 - 2 * s, 1)], axis=1) for s in range(4)
        ]
        return slabs, tall, wide

    def end_means():
        receive(8, 14)
        slabs, tall, wide = end_fields([end_zs[4, i] for i in range(6)], [end_halo[4, i] for i in range(2)])
        for i in range(5):
            end_x[i] = mean_of(slabs[i], slabs[i + 1])
        for s in range(4):
            end_y[s] = mean_of(tall[s], up(tall[s], 0))
            end_z[s] = mean_of(wide[s], up(wide[s], 1))

    for newton in range(NEWTON):
        coefficients()
        sofar = []
        moments = []
        v = [v0[i] if 2 <= i < 10 else v0[i, 0:8] for i in range(12)]
        tiles = [slab[0:8] for slab in v[4:8]]
        for j in range(KRYLOV):
            at = 4 * newton + j
            precondition(v, at)
            z_tiles = [zs[(at, s + 1) + own] for s in range(4)]
            moments.append((2 * j, total_of(tiles, z_tiles)))
            if newton + 1 < NEWTON:
                for s in range(4):
                    raw_h[j, 5 + s, 8:16] = z_tiles[s]
            tiles = [SCALE * image(at, s) - SHIFT * tiles[s] for s in range(4)]
            moments.append((2 * j + 1, total_of(tiles, z_tiles)))
            if j + 1 < KRYLOV:

                def meanwhile(newton=newton, j=j, moments=moments):
                    sofar.append(gather(sofar[-1] if j else nothing, moments))
                    beside_v(newton, j)

                v = exchange_v(tiles, 2 * newton + j, meanwhile)
                moments = []

        counts = []

        def beside(phase, newton=newton, counts=counts):
            if phase == 1 and newton + 1 < NEWTON:
                pack_corners(raw_h, 1, 0, 3)
                counts.append(exchange_wide(raw_h, corner_h, 1, 0, 3, True, 1))
                pack_z([raw_h[f, 5 + s, 8:16] for f in range(2) for s in range(4)], 1, 0)
                pack_z([raw_h[2, 5 + s, 8:16] for s in range(4)], 1, 1)
                counts.append(exchange_far(raw_h, far_h, 1, 3, 1))
                counts.append(exchange_z(zed_h, 1, 1))
            elif phase == 1:
                give_field(6, 13)
                end_means()
            elif phase == 2 and newton + 1 < NEWTON:
                receive(sum(counts), 1)
                for j in range(3):
                    for i in range(14):
                        slab = narrow(wide_slab(raw_h, corner_h, zed_h, far_h, j, i), i)
                        if is_own(i):
                            box_z[j, i] = slab
                        else:
                            box_z[j, i, 0:16] = slab

        c = solve(global_sum(gather(sofar[-1], moments), newton, beside))
        if newton + 1 < NEWTON:
            for i in range(14):
                rows = slice(0, 24 if is_own(i) else 16)
                total = get_box(i)
                for j in range(3):
                    total = total + c[j] * box_z[j, i, rows]
                put_box(i, total)
                if 4 <= i < 10:
                    zs[3, i - 4] = fold_rows(total) if is_own(i) else total

    last_r.wait()
    last_s.wait()
    receive(8 * 4, 13)
    near = []
    for tiles in ([end_zs.at[:, i] for i in range(6)], [end_halo.at[:, i] for i in range(2)]):
        for tile in tiles:
            total = tile[0]
            for j in range(3):
                total = total + c[j] * tile[1 + j]
            near.append(total)
    last, tall, wide = end_fields(near[:6], near[6:])
    low_flux = None
    for s in range(-1, 4):
        flux, _ = face_terms(end_x[s + 1], last[s + 2] - last[s + 1])
        if s >= 0:
            out[0, s] = last[s + 1]
            flux_y, _ = face_terms(end_y[s], up(tall[s], 0) - tall[s])
            flux_z, _ = face_terms(end_z[s], up(wide[s], 1) - wide[s])
            out[1, s] = (
                end_rs[0, s] * last[s + 1]
                - (flux - low_flux)
                - (flux_y - down(flux_y, 0))[0:8]
                - (flux_z - down(flux_z, 1))[:, 0:LINE]
                - end_rs[1, s]
            )
        low_flux = flux
    for copy in copies:
        copy.wait_send()

    @pl.when(jnp.logical_not(alone))
    def _():
        part = dummy.at[pl.ds(0, sum(given))]
        pltpu.make_async_copy(part, part, send_sem.at[1]).wait()


def local(sizes, state, conductivity, reaction, source):
    nx, ny, nz = sizes
    plane, line = 4 * nz, (nx // 4) * ny

    def vmem(*shape):
        return pltpu.VMEM(shape, jnp.float32)

    full, half = (24, 2 * LINE), (16, 2 * LINE)
    tile = (ROWS, LINE)
    scratch = [
        vmem(4, 14, 24, LINE), vmem(2, 2, 4, 2, *tile), vmem(3, 3, 2, 2, *tile), vmem(2, 2, 2, *tile),
        vmem(3, 14, 24, LINE), vmem(2, 2, 3, 2, *tile), vmem(3, 3, 2, 2, *tile), vmem(2, 2, 2, *tile),
        vmem(4, 7, *tile), vmem(4, 2, 4, *tile), vmem(4, 2, 4, *tile), vmem(4, 2, 3, *tile), vmem(4, 2, 2, 2, *tile), vmem(2, 2, 2, *tile), vmem(2, 2, 4, 2, *tile), vmem(14, *full), vmem(3, 14, *full),
        vmem(13, *half), vmem(12, *full), vmem(12, *half), vmem(12, *half), vmem(12, *half), vmem(6, *half),
        vmem(12, *half), vmem(8, *half), vmem(7, *half), vmem(6, *half), vmem(6, *half), vmem(6, *half), vmem(6, *half),
        vmem(6, *half), vmem(5, *half), vmem(4, *half), vmem(4, *half), vmem(4, *half), vmem(4, *half),
        vmem(8, 6, *half), vmem(2, 3, 1, LINE), vmem(2, plane - 1, 1, LINE), vmem(2, line - 1, 1, LINE),
        vmem(160, *tile),
        vmem(5, 6, *tile), vmem(5, 2, *tile), vmem(5, 2, *tile), vmem(5, *tile), vmem(4, 16, LINE), vmem(4, ROWS, 2 * LINE), vmem(2, 4, *tile),
        pltpu.SemaphoreType.DMA((4,)), pltpu.SemaphoreType.DMA((16,)), pltpu.SemaphoreType.REGULAR,
    ]
    spec = pl.BlockSpec(memory_space=pltpu.MemorySpace.HBM)
    both = pl.pallas_call(
        functools.partial(kernel, sizes),
        out_shape=jax.ShapeDtypeStruct((2, *state.shape), jnp.float32),
        in_specs=[spec] * 4,
        out_specs=pl.BlockSpec(memory_space=pltpu.VMEM),
        scratch_shapes=scratch,
        compiler_params=pltpu.CompilerParams(
            collective_id=0, has_side_effects=True, vmem_limit_bytes=61 * 1024 * 1024
        ),
    )(state, conductivity, reaction, source)
    return both[0], both[1]


def solution(mesh):
    sizes = tuple(mesh.shape[name] for name in ("gx", "gy", "gz"))
    placed = P("gx", "gy", "gz")
    return jax.shard_map(
        functools.partial(local, sizes),
        mesh=mesh,
        in_specs=(placed,) * 4,
        out_specs=(placed, placed),
        check_vma=False,
    )
```
